128 devices in a mesh: row: 8 (over x, core), col: 16 (over z, y).
Axes of the slice: x: 4, y: 4, z: 4, core: 2. Of those that a mesh axis runs over, the one named last changes fastest.
Arguments:
- load_force: float32 [2, 2, 256, 2048], P(None, None, 'row', 'col'), may hold values from -24 to 24
- stiffness: float32 [2, 2, 256, 2048], P(None, None, 'row', 'col'), may hold values from 0.5 to 2
- cracks: int32 [2, 2, 256, 2048], P(None, None, 'row', 'col'), may hold values 0 or 1
- anchor: float32 [2, 256, 2048], P(None, 'row', 'col'), may hold values from 0.1 to 2
- images: bfloat16 [2, 2048, 16384], P(None, 'row', 'col'), may hold values from -6 to 6
- owners: int32 [6144, 1], P(('row', 'col')), may hold values from 0 to 15; in each aligned block of 48 rows (0 to 47, 48 to 95, ...) at most 4 rows name the same one
- source_tile: int32 [6144], P(('row', 'col')), may hold values from 0 to 3
- offsets: int32 [2, 6144], P(None, ('row', 'col')), may hold values from -96 to 96
- blend_weight: float32 [6144], P(('row', 'col')), may hold values from 0.5 to 2
- counts: int32 [1024], P(('row', 'col')), may hold values from 1 to 6
Outputs:
- displacement: float32 [2, 2, 256, 2048], P(None, None, 'row', 'col')
- residual: float32 [2, 2, 256, 2048], P(None, None, 'row', 'col')
- level_zero: bfloat16 [2, 2048, 16384], P(None, 'row', 'col')
- level_one: bfloat16 [2, 1024, 8192], P(None, 'row', 'col')
- level_two: bfloat16 [2, 512, 4096], P(None, 'row', 'col')
The draws below stay inside these ranges and needn't reach their ends.
Inputs may be any that keep to these rules, and one draw needn't show every extreme that they name: `owners`: within the entries of one device no value appears more than 4 times, and some value appears exactly 4 times in some device's entries.
All inputs are finite; a program needn't handle non-finite values. No bound on the sum of `cracks` on one device may be relied on, other than what follows from the above.
Results may differ from the reference program's by a relative error of at most 0.0085.
Values may be sent and summed in bfloat16 or wider, within the bound.
A program may use at most 384 MiB of HBM per device.

```python
import math
import jax
import jax.numpy as jnp
import numpy as np
from jax import lax

S = 2
TILE = 256
SPACING = 8
K = 6
ITERS = 4
TR = 1
TC = 4
VT = 32
MR = 256
MC = 2048
H = 2048
W = 16384
TILES_DEV = 8
ENT_DEV = 48
ENTRIES = 6144
OUT_TILES = 1024
CAP = 4
N_ROW = 8
N_COL = 16


def plant(drawn, key, least, high):
    spot = [jax.random.randint(jax.random.fold_in(key, axis), (), 0, length) for axis, length in enumerate(drawn.shape)]
    widest = drawn.shape.index(max(drawn.shape))
    neighbour = spot[:widest] + [(spot[widest] + 1) % drawn.shape[widest]] + spot[widest + 1:]
    return drawn.at[tuple(spot)].set(least).at[tuple(neighbour)].set(high)


def levels(own_key, dims, split, low, top_value):
    loudness = 1.0
    for dim, blocks in split:
        heights = jax.random.uniform(jax.random.fold_in(jax.random.fold_in(own_key, 6), dim), (blocks,), jnp.float32, low / len(split), top_value / len(split))
        loudness = loudness * jnp.repeat(jnp.exp(heights), dims[dim] // blocks).reshape((-1,) + (1,) * (len(dims) - 1 - dim))
    return loudness


def shared_out(stream_key, own, number, rows, count, top, limit, lean):
    sequence = jax.random.permutation(stream_key, count)
    heavy_load, ordinary = shares(count, rows * top, limit, lean, True), shares(count, rows * top, limit, lean, False)
    places = jnp.arange(count)

    def named(lengths, rotation):
        used = int((lengths > 0).sum())
        fixed = max(1, used // 4)
        passed = fixed + (places - fixed + rotation * (used - fixed)) % max(1, count - fixed)
        return jnp.zeros((count,), jnp.int32).at[sequence[jnp.where(places < fixed, places, passed)]].set(jnp.asarray(lengths, jnp.int32))

    lengths = jnp.where(number % 4 == 0, named(heavy_load, number // 4), named(ordinary, number - number // 4 - 1))
    mixed = jax.random.permutation(jax.random.fold_in(own, 3), count)
    donor, taker = mixed[0:count // 2 * 2:2], mixed[1:count // 2 * 2:2]
    slack = jnp.minimum(lengths[donor] - 1, limit - lengths[taker]) // 2
    slack = jnp.where((donor == sequence[0]) | (taker == sequence[0]) | (lengths[taker] == 0), 0, jnp.maximum(slack, 0))
    passed = jax.random.randint(jax.random.fold_in(own, 4), (count // 2,), 0, 1 << 20) % (slack + 1)
    lengths = lengths.at[donor].add(-passed).at[taker].add(passed)
    labels = jnp.searchsorted(jnp.cumsum(lengths), jnp.arange(rows * top), side="right").astype(jnp.int32)
    listing = labels.reshape(top, rows).T
    listing = listing[jax.random.permutation(jax.random.fold_in(own, 1), rows)]
    rotation = jax.random.randint(jax.random.fold_in(own, 2), (rows, 1), 0, top)
    return jnp.take_along_axis(listing, (jnp.arange(top)[None, :] + rotation) % top, axis=1)


def shares(number_of, total, bound, lean, full):
    loads = [(1 << 20) // math.isqrt(grade ** lean) + 1 for grade in range(1, number_of + 1)]
    largest = bound if full else min(bound, max(-(-total // number_of), total * loads[0] // sum(loads)))
    least = 1 if total - largest >= number_of - 1 else 0
    given, spare = [largest] + [least] * (number_of - 1), total - largest - least * (number_of - 1)
    while spare > 0:
        free = [i for i in range(1, number_of) if given[i] < largest] or [i for i in range(1, number_of) if given[i] < bound]
        mass, left = sum([loads[i] for i in free]), spare
        for i in free:
            more = min(bound - given[i], max(1, left * loads[i] // mass), spare)
            given[i] = given[i] + more
            spare = spare - more
    return np.array(given)


def gaussian(own_key, dims, spread, limit, cuts=(), held_as=jnp.bfloat16):
    values = jax.random.normal(own_key, dims, jnp.float32) * spread
    if len(cuts) > 0:
        values = levels(own_key, dims, cuts, -0.22, 0.18) * values
    return jnp.clip(values, min=-limit, max=limit).astype(held_as)


def setup_inputs(seed: int = 0) -> dict:
    streams_of = jax.random.split(jax.random.key(seed), 11)
    load_force = gaussian(streams_of[0], (S, 2, MR, MC), 4.0, 24.0, ((2, 8), (3, 16)), jnp.float32)
    stiffness = jnp.clip(jnp.exp(math.log(2.0) - 1.3862944 * jax.random.uniform(streams_of[1], (S, 2, MR, MC), jnp.float32) ** levels(streams_of[1], (S, 2, MR, MC), ((2, 8), (3, 16)), -0.2, 0.2)), 0.5, 2.0)
    cracks = plant((jax.random.randint(streams_of[2], (S, 2, MR, MC), 0, 8) < 7).astype(jnp.int32), jax.random.fold_in(streams_of[2], 1), 0, 1)
    anchor = jnp.clip(jnp.exp(math.log(2.0) - 2.9957323 * jax.random.uniform(streams_of[3], (S, MR, MC), jnp.float32) ** levels(streams_of[3], (S, MR, MC), ((1, 8), (2, 16)), -0.2, 0.2)), 0.1, 2.0)
    images = gaussian(streams_of[4], (S, H, W), 1.0, 6.0, ((1, 8), (2, 16)))
    owners_keys = jax.random.split(jax.random.fold_in(streams_of[5], 1), ENTRIES // ENT_DEV)
    owners_turns = jax.random.permutation(jax.random.fold_in(streams_of[5], 3), ENTRIES // ENT_DEV)
    owners = jax.vmap(lambda own, number: shared_out(jax.random.fold_in(streams_of[5], 2), own, number, ENT_DEV, N_COL, 1, CAP, 2))(owners_keys, owners_turns).reshape((ENTRIES, 1))
    source_tile = plant(jax.random.randint(streams_of[6], (ENTRIES,), 0, TR * TC), jax.random.fold_in(streams_of[6], 1), 0, (TR * TC) - 1).astype(jnp.int32)
    offsets = plant(jax.random.randint(streams_of[7], (2, ENTRIES), 0 - 3 * TILE // 8, 3 * TILE // 8 + 1), jax.random.fold_in(streams_of[7], 1), 0 - 3 * TILE // 8, (3 * TILE // 8 + 1) - 1).astype(jnp.int32)
    blend_weight = jnp.clip(jnp.exp(math.log(2.0) - 1.3862944 * jax.random.uniform(streams_of[8], (ENTRIES,), jnp.float32) ** levels(streams_of[8], (ENTRIES,), ((0, 128),), -0.2, 0.2)), 0.5, 2.0)
    counts = plant(jax.random.randint(streams_of[9], (OUT_TILES,), 1, K + 1), jax.random.fold_in(streams_of[9], 1), 1, K).astype(jnp.int32)
    return dict(load_force=load_force, stiffness=stiffness, cracks=cracks, anchor=anchor, images=images, owners=owners, source_tile=source_tile, offsets=offsets, blend_weight=blend_weight, counts=counts)


def tent_weight(offset):
    return jnp.maximum(0.0, 1.0 - jnp.abs(offset))


def sample_matrix(shift_value):
    position = jnp.arange(TILE, dtype=jnp.float32)
    matrix = tent_weight(position[None, None, :] - position[None, :, None] - shift_value[:, None, None])
    return matrix.astype(jnp.bfloat16)


def warp_tiles(picked, local_anchor, offset_pair, weights):
    shift_y = offset_pair[0].astype(jnp.float32) + SPACING * jnp.repeat(local_anchor[:, 0].reshape(-1), K)
    shift_x = offset_pair[1].astype(jnp.float32) + SPACING * jnp.repeat(local_anchor[:, 1].reshape(-1), K)

    def warp_group(inputs):
        tiles_group, along_y, along_x, weight_group = inputs
        across_matrix = lax.optimization_barrier(sample_matrix(along_x)).astype(jnp.float32)
        down_matrix = lax.optimization_barrier(sample_matrix(along_y)).astype(jnp.float32)
        across = jnp.einsum("ecw,ebw->ecb", tiles_group.astype(jnp.float32), across_matrix)
        across = lax.optimization_barrier(across.astype(jnp.bfloat16)).astype(jnp.float32)
        result = jnp.einsum("eac,ecb->eab", down_matrix, across)
        result = result * weight_group[:, None, None]
        return jnp.sum(result.reshape(TC, K, TILE, TILE), axis=1)

    groups = S * TR
    warped = lax.map(warp_group, (picked.reshape(groups, TC * K, TILE, TILE), shift_y.reshape(groups, TC * K),
                                  shift_x.reshape(groups, TC * K), weights.reshape(groups, TC * K)))
    return warped.reshape(S, TR, TC, TILE, TILE)


def operate(field_now, right_spring, left_spring, down_spring, up_spring, anchor_spring):
    zero_col = jnp.zeros_like(field_now[..., :1])
    zero_row = jnp.zeros_like(field_now[..., :1, :])
    right_value = jnp.concatenate([field_now[..., 1:], zero_col], axis=3)
    left_value = jnp.concatenate([zero_col, field_now[..., :-1]], axis=3)
    down_value = jnp.concatenate([field_now[..., 1:, :], zero_row], axis=2)
    up_value = jnp.concatenate([zero_row, field_now[..., :-1, :]], axis=2)
    return (anchor_spring * field_now + right_spring * (field_now - right_value) + left_spring * (field_now - left_value)
            + down_spring * (field_now - down_value) + up_spring * (field_now - up_value))


def section_dot(first, second):
    return jnp.sum(first * second, axis=(1, 2, 3), keepdims=True)


def reference(load_force, stiffness, cracks, anchor, images, owners, source_tile, offsets, blend_weight, counts):
    springs = stiffness * cracks.astype(jnp.float32)
    right_spring = springs[:, 0:1]
    down_spring = springs[:, 1:2]
    left_spring = jnp.concatenate([jnp.zeros_like(right_spring[..., :1]), right_spring[..., :-1]], axis=3)
    up_spring = jnp.concatenate([jnp.zeros_like(down_spring[:, :, :1]), down_spring[:, :, :-1]], axis=2)
    anchor_spring = anchor[:, None]
    displacement = jnp.zeros_like(load_force)
    residual = load_force
    direction = load_force
    norm_now = section_dot(residual, residual)
    for iteration in range(ITERS):
        applied = operate(direction, right_spring, left_spring, down_spring, up_spring, anchor_spring)
        step_size = norm_now / section_dot(direction, applied)
        displacement = displacement + step_size * direction
        residual = residual - step_size * applied
        norm_next = section_dot(residual, residual)
        direction = residual + (norm_next / norm_now) * direction
        norm_now = norm_next

    half_cell = VT // 2
    grid_anchor = displacement[:, :, half_cell::VT, half_cell::VT]
    grid_anchor = grid_anchor.reshape(S, 2, N_ROW, TR, N_COL, TC).transpose(2, 4, 0, 1, 3, 5)
    grid_anchor = grid_anchor.reshape(N_ROW * N_COL, S, 2, TR, TC)
    tiles_all = images.reshape(S, N_ROW, TR, TILE, N_COL, TC, TILE).transpose(1, 4, 0, 2, 5, 3, 6)
    tiles_all = tiles_all.reshape(N_ROW, N_COL * TILES_DEV, TILE, TILE)
    section_of = (jnp.arange(ENT_DEV, dtype=jnp.int32) // (TR * TC * K)).astype(jnp.int32)
    list_slot = (jnp.arange(ENT_DEV, dtype=jnp.int32) % K).astype(jnp.int32)

    def one_device(device):
        row_index = (device // N_COL).astype(jnp.int32)
        entry_start = (device * ENT_DEV).astype(jnp.int32)
        owner_col = lax.dynamic_slice_in_dim(owners[:, 0], entry_start, ENT_DEV)
        local_tile = lax.dynamic_slice_in_dim(source_tile, entry_start, ENT_DEV)
        offset_pair = lax.dynamic_slice_in_dim(offsets, entry_start, ENT_DEV, axis=1)
        blends = lax.dynamic_slice_in_dim(blend_weight, entry_start, ENT_DEV)
        tile_counts = lax.dynamic_slice_in_dim(counts, (device * TILES_DEV).astype(jnp.int32), TILES_DEV)
        weights = blends * (list_slot < jnp.repeat(tile_counts, K)).astype(jnp.float32)
        row_tiles = lax.dynamic_index_in_dim(tiles_all, row_index, 0, keepdims=False)
        tile_index = (owner_col * TILES_DEV + section_of * (TR * TC) + local_tile).astype(jnp.int32)
        picked = jnp.take(row_tiles, tile_index, axis=0)
        local_anchor = lax.dynamic_index_in_dim(grid_anchor, device, 0, keepdims=False)
        return warp_tiles(picked, local_anchor, offset_pair, weights)

    warped = lax.map(one_device, jnp.arange(N_ROW * N_COL, dtype=jnp.int32))
    warped = warped.reshape(N_ROW, N_COL, S, TR, TC, TILE, TILE).transpose(2, 0, 3, 5, 1, 4, 6).reshape(S, H, W)
    level_zero = warped.astype(jnp.bfloat16)
    level_one = jnp.mean(warped.reshape(S, H // 2, 2, W // 2, 2), axis=(2, 4)).astype(jnp.bfloat16)
    level_two = jnp.mean(warped.reshape(S, H // 4, 4, W // 4, 4), axis=(2, 4)).astype(jnp.bfloat16)
    return (displacement, residual, level_zero, level_one, level_two)
```

```python
import jax
import jax.numpy as jnp
from jax import lax
from jax.experimental import pallas as pl
from jax.experimental.pallas import tpu as pltpu
from jax.sharding import PartitionSpec as P

S = 2
TILE = 256
SPACING = 8
K = 6
ITERS = 4
TC = 4
ENT_DEV = 48
VR = 32
VC = 128
N_ROW = 8
N_COL = 16
WIDE = TC * TILE
ROWS = VR + 16
COLS = 2 * VC
MESH = pl.DeviceIdType.MESH
F32 = jnp.float32
BF16 = jnp.bfloat16


def flipped(v, mask):
    if mask == 1:
        return v + 1 - 2 * lax.rem(v, 2)
    return 3 - v


def peer_col(y, z, mask, i):
    py = flipped(y, mask) if i % 2 == 1 else y
    pz = flipped(z, mask) if i // 2 == 1 else z
    return pz * 4 + py


GATHER_MASK = (1, 3)
SCATTER_MASK = (3, 1)


def relax_kernel(
    load_ref, stiff_ref, crack_ref, anchor_ref, meta_ref, images_ref,
    disp_ref, resid_ref, metas_ref, gathered_ref,
    fields, strips, halo_v, halo_h, halo_c,
    coef, xs, rs, ps, qs, ws,
    part_a, part_b, got_a, got_b, note, notes,
    halo_send, halo_recv, send_a, recv_a, send_b, recv_b,
    note_send, note_recv, tile_send, tile_recv,
):
    r = lax.axis_index("row")
    c = lax.axis_index("col")
    y = lax.rem(c, 4)
    z = c // 4
    up, down = lax.rem(r + N_ROW - 1, N_ROW), lax.rem(r + 1, N_ROW)
    left, right = lax.rem(c + N_COL - 1, N_COL), lax.rem(c + 1, N_COL)
    corners = ((up, left), (up, right), (down, left), (down, right))

    barrier = pltpu.get_barrier_semaphore()

    @pl.loop(1, N_ROW)
    def _(d):
        pl.semaphore_signal(barrier, inc=1, device_id=(lax.rem(r + d, N_ROW), c), device_id_type=MESH)

    @pl.loop(1, N_COL)
    def _(d):
        pl.semaphore_signal(barrier, inc=1, device_id=(r, lax.rem(c + d, N_COL)), device_id_type=MESH)

    for corner in corners:
        pl.semaphore_signal(barrier, inc=1, device_id=corner, device_id_type=MESH)

    for s in range(S):
        for k in range(2):
            fields[2 * s + k] = load_ref[s, k]
            fields[4 + 2 * s + k] = stiff_ref[s, k] * crack_ref[s, k].astype(F32)
        fields[8 + s] = anchor_ref[s]
    lane = lax.broadcasted_iota(jnp.int32, (VR, VC), 1)
    first = jnp.zeros((VR, VC), F32)
    last = jnp.zeros((VR, VC), F32)
    for f in range(10):
        block = fields[f]
        here = (lane >= 4 * f) & (lane < 4 * f + 4)
        first = jnp.where(here, block if f == 0 else pltpu.roll(block, 4 * f, 1), first)
        last = jnp.where(here, pltpu.roll(block, 4 * f + 4, 1), last)
    strips[0] = first
    strips[1] = last

    pl.semaphore_wait(barrier, N_ROW - 1 + N_COL - 1 + 4)

    halo = []
    for n, (source, target, device) in enumerate((
        (fields.at[:, pl.ds(VR - 8, 8), :], halo_v.at[0], (down, c)),
        (fields.at[:, pl.ds(0, 8), :], halo_v.at[1], (up, c)),
        (strips.at[1], halo_h.at[0], (r, right)),
        (strips.at[0], halo_h.at[1], (r, left)),
        (strips.at[1, pl.ds(VR - 8, 8)], halo_c.at[0], (down, right)),
        (strips.at[0, pl.ds(VR - 8, 8)], halo_c.at[1], (down, left)),
        (strips.at[1, pl.ds(0, 8)], halo_c.at[2], (up, right)),
        (strips.at[0, pl.ds(0, 8)], halo_c.at[3], (up, left)),
    )):
        halo.append(pltpu.make_async_remote_copy(
            src_ref=source, dst_ref=target, send_sem=halo_send.at[n], recv_sem=halo_recv.at[n],
            device_id=device, device_id_type=MESH))
    for copy in halo:
        copy.start()

    tiles = []
    for i in (3, 1, 2):
        for s in range(S):
            tiles.append(pltpu.make_async_remote_copy(
                src_ref=images_ref.at[s], dst_ref=gathered_ref.at[s, i - 1],
                send_sem=tile_send.at[s, i - 1], recv_sem=tile_recv.at[s, i - 1],
                device_id=(r, peer_col(y, z, GATHER_MASK[s], i)), device_id_type=MESH))
    for copy in tiles:
        copy.start()

    for copy in halo:
        copy.wait_recv()

    wide_row = lax.broadcasted_iota(jnp.int32, (ROWS, VC), 0) + r * VR - 8
    wide_lane = lax.broadcasted_iota(jnp.int32, (ROWS, VC), 1)
    side_col = jnp.where(wide_lane < VC // 2, wide_lane + VC, wide_lane - VC) + c * VC
    row_in = (wide_row >= 0) & (wide_row < VR * N_ROW)
    side_in = row_in & (side_col >= 0) & (side_col < VC * N_COL)
    from_left = jnp.concatenate([halo_c[0], halo_h[0], halo_c[2]], axis=0)
    from_right = jnp.concatenate([halo_c[1], halo_h[1], halo_c[3]], axis=0)

    def widened(f):
        own = jnp.concatenate([halo_v[0, f], fields[f], halo_v[1, f]], axis=0)
        to_left = pltpu.roll(from_left, 124 - 4 * f, 1)
        to_right = from_right if f == 0 else pltpu.roll(from_right, VC - 4 * f, 1)
        side = jnp.where(wide_lane < 4, to_right, jnp.where(wide_lane >= 124, to_left, 0.0))
        return jnp.concatenate(
            [jnp.where(row_in, own, 0.0), jnp.where(side_in, side, 0.0)], axis=1)

    inside = jnp.concatenate([row_in.astype(F32), side_in.astype(F32)], axis=1)
    for s in range(S):
        to_right = widened(4 + 2 * s)
        to_low = widened(5 + 2 * s)
        to_left = pltpu.roll(to_right, 1, 1) * inside
        to_high = pltpu.roll(to_low, 1, 0) * inside
        coef[s, 0] = widened(8 + s) + to_right + to_left + to_low + to_high
        coef[s, 1] = to_right
        coef[s, 2] = to_left
        coef[s, 3] = to_low
        coef[s, 4] = to_high
        for k in range(2):
            rs[2 * s + k] = widened(2 * s + k)
    zero = jnp.zeros((ROWS, COLS), F32)
    for f in range(4):
        xs[f] = zero
        ps[f] = zero
        qs[f] = zero

    def step(it, carry):
        sums = []
        for s in range(S):
            rr = jnp.zeros((8, VC), F32)
            rw = jnp.zeros((8, VC), F32)
            for k in range(2):
                v = rs[2 * s + k]
                w = coef[s, 0] * v
                w = w - coef[s, 1] * pltpu.roll(v, COLS - 1, 1)
                w = w - coef[s, 2] * pltpu.roll(v, 1, 1)
                w = w - coef[s, 3] * pltpu.roll(v, ROWS - 1, 0)
                w = w - coef[s, 4] * pltpu.roll(v, 1, 0)
                ws[2 * s + k] = w
                own_v = v[8:8 + VR, 0:VC]
                own_w = w[8:8 + VR, 0:VC]
                rr = rr + jnp.sum((own_v * own_v).reshape(VR // 8, 8, VC), axis=0)
                rw = rw + jnp.sum((own_v * own_w).reshape(VR // 8, 8, VC), axis=0)
            sums.append((jnp.sum(rr, axis=0, keepdims=True), jnp.sum(rw, axis=0, keepdims=True)))
        part_a[it] = jnp.concatenate(
            [sums[0][0], sums[1][0], sums[0][1], sums[1][1], jnp.zeros((4, VC), F32)], axis=0)

        @pl.loop(1, N_ROW)
        def _(d):
            pltpu.make_async_remote_copy(
                src_ref=part_a.at[it], dst_ref=got_a.at[it, d - 1], send_sem=send_a.at[it],
                recv_sem=recv_a.at[it], device_id=(lax.rem(r + d, N_ROW), c), device_id_type=MESH).start()

        pltpu.make_async_remote_copy(
            src_ref=got_a.at[it], dst_ref=got_a.at[it], send_sem=send_a.at[it],
            recv_sem=recv_a.at[it], device_id=(down, c), device_id_type=MESH).wait_recv()
        part_b[it] = part_a[it] + jnp.sum(got_a[it], axis=0)

        @pl.loop(1, N_COL)
        def _(d):
            pltpu.make_async_remote_copy(
                src_ref=part_b.at[it], dst_ref=got_b.at[it, d - 1], send_sem=send_b.at[it],
                recv_sem=recv_b.at[it], device_id=(r, lax.rem(c + d, N_COL)), device_id_type=MESH).start()

        pltpu.make_async_remote_copy(
            src_ref=got_b.at[it], dst_ref=got_b.at[it], send_sem=send_b.at[it],
            recv_sem=recv_b.at[it], device_id=(r, right), device_id_type=MESH).wait_recv()
        total = jnp.sum(part_b[it] + jnp.sum(got_b[it], axis=0), axis=1, keepdims=True)
        rr = total[0:2]
        rw = total[2:4]
        rr_old, alpha_old = carry
        beta = jnp.where(it == 0, 0.0, rr / rr_old)
        alpha = rr / (rw - beta * rr / alpha_old)
        for s in range(S):
            a = alpha[s:s + 1]
            b = beta[s:s + 1]
            for k in range(2):
                f = 2 * s + k
                p = rs[f] + b * ps[f]
                q = ws[f] + b * qs[f]
                ps[f] = p
                qs[f] = q
                xs[f] = xs[f] + a * p
                rs[f] = rs[f] - a * q
        return rr, alpha

    lax.fori_loop(0, ITERS, step, (jnp.ones((2, 1), F32), jnp.ones((2, 1), F32)))

    rows = [xs[f, pl.ds(8 + VR // 2, 1), pl.ds(0, VC)] for f in range(4)]
    note[...] = jnp.concatenate([meta_ref[pl.ds(0, 4), :]] + rows, axis=0)
    told = []
    for s in range(S):
        for i in (1, 2, 3):
            told.append(pltpu.make_async_remote_copy(
                src_ref=note, dst_ref=notes.at[s, i - 1],
                send_sem=note_send.at[s, i - 1], recv_sem=note_recv.at[s, i - 1],
                device_id=(r, peer_col(y, z, SCATTER_MASK[s], i)), device_id_type=MESH))
    for copy in told:
        copy.start()
    for s in range(S):
        metas_ref[s, 0] = note[...]
        for k in range(2):
            f = 2 * s + k
            disp_ref[s, k] = xs[f, pl.ds(8, VR), pl.ds(0, VC)]
            resid_ref[s, k] = rs[f, pl.ds(8, VR), pl.ds(0, VC)]
    for copy in told:
        copy.wait_recv()
    for s in range(S):
        for i in (1, 2, 3):
            metas_ref[s, i] = notes[s, i - 1]

    for copy in told:
        copy.wait_send()
    for copy in halo:
        copy.wait_send()

    @pl.loop(0, ITERS)
    def _(it):
        pltpu.make_async_remote_copy(
            src_ref=got_a.at[it], dst_ref=got_a.at[it], send_sem=send_a.at[it],
            recv_sem=recv_a.at[it], device_id=(down, c), device_id_type=MESH).wait_send()
        pltpu.make_async_remote_copy(
            src_ref=got_b.at[it], dst_ref=got_b.at[it], send_sem=send_b.at[it],
            recv_sem=recv_b.at[it], device_id=(r, right), device_id_type=MESH).wait_send()

    for copy in tiles:
        copy.wait()


def relax(load_force, stiffness, cracks, anchor, meta, images):
    vmem = pl.BlockSpec(memory_space=pltpu.VMEM)
    anywhere = pl.BlockSpec(memory_space=pl.ANY)
    dma = pltpu.SemaphoreType.DMA
    wide = (ROWS, COLS)
    return pl.pallas_call(
        relax_kernel,
        out_shape=(
            jax.ShapeDtypeStruct((S, 2, VR, VC), F32),
            jax.ShapeDtypeStruct((S, 2, VR, VC), F32),
            jax.ShapeDtypeStruct((S, 4, 8, VC), F32),
            jax.ShapeDtypeStruct((S, 3, TILE, WIDE), BF16),
        ),
        in_specs=[vmem] * 5 + [anywhere],
        out_specs=(vmem, vmem, vmem, anywhere),
        scratch_shapes=[
            pltpu.VMEM((10, VR, VC), F32),
            pltpu.VMEM((2, VR, VC), F32),
            pltpu.VMEM((2, 10, 8, VC), F32),
            pltpu.VMEM((2, VR, VC), F32),
            pltpu.VMEM((4, 8, VC), F32),
            pltpu.VMEM((S, 5) + wide, F32),
            pltpu.VMEM((4,) + wide, F32),
            pltpu.VMEM((4,) + wide, F32),
            pltpu.VMEM((4,) + wide, F32),
            pltpu.VMEM((4,) + wide, F32),
            pltpu.VMEM((4,) + wide, F32),
            pltpu.VMEM((ITERS, 8, VC), F32),
            pltpu.VMEM((ITERS, 8, VC), F32),
            pltpu.VMEM((ITERS, N_ROW - 1, 8, VC), F32),
            pltpu.VMEM((ITERS, N_COL - 1, 8, VC), F32),
            pltpu.VMEM((8, VC), F32),
            pltpu.VMEM((S, 3, 8, VC), F32),
            dma((8,)), dma((8,)),
            dma((ITERS,)), dma((ITERS,)), dma((ITERS,)), dma((ITERS,)),
            dma((S, 3)), dma((S, 3)), dma((S, 3)), dma((S, 3)),
        ],
        compiler_params=pltpu.CompilerParams(
            collective_id=0, has_side_effects=True, vmem_limit_bytes=32 * 1024 * 1024),
        name="relax_and_gather",
    )(load_force, stiffness, cracks, anchor, meta, images)


def warp_kernel(meta_ref, images_ref, gathered_ref, part_ref, tiles, acc, out, sems, out_sems):
    c = lax.axis_index("col")
    y = lax.rem(c, 4)
    z = c // 4
    loads = []
    for s in range(S):
        loads.append(pltpu.make_async_copy(images_ref.at[s], tiles.at[s, 0], sems.at[s, 0]))
        loads.append(pltpu.make_async_copy(
            gathered_ref.at[s], tiles.at[s, pl.ds(1, 3)], sems.at[s, 1]))
    for copy in loads:
        copy.start()
    for copy in loads:
        copy.wait()
    row = lax.broadcasted_iota(jnp.int32, (TILE, TILE), 0)
    lane = lax.broadcasted_iota(jnp.int32, (TILE, TILE), 1)
    apart = (lane - row).astype(F32)

    def tent(offset):
        return jnp.maximum(0.0, 1.0 - jnp.abs(offset)).astype(BF16)

    for s in range(S):
        mask = GATHER_MASK[s]

        def target(n, carry):
            i = n // TC
            j = lax.rem(n, TC)
            acc[...] = jnp.zeros((TILE, TILE), F32)

            def entry(k, carry):
                e = s * 24 + j * K + k
                code = meta_ref[s, i, 0, e].astype(jnp.int32)
                weight = meta_ref[s, i, 3, e]
                owner = code // 4
                tile = lax.rem(code, 4)
                oy = lax.rem(owner, 4)
                oz = owner // 4
                mine = ((oy == y) | (oy == flipped(y, mask))) & ((oz == z) | (oz == flipped(z, mask)))

                @pl.when(mine & (weight > 0.0))
                def _():
                    slot = jnp.where(oy == y, 0, 1) + jnp.where(oz == z, 0, 2)
                    at = 32 * j + 16
                    sy = meta_ref[s, i, 1, e] + SPACING * meta_ref[s, i, 4 + 2 * s, at]
                    sx = meta_ref[s, i, 2, e] + SPACING * meta_ref[s, i, 5 + 2 * s, at]
                    source = tiles[s, slot, :, pl.ds(pl.multiple_of(tile * TILE, TILE), TILE)]
                    across = jnp.dot(source, tent(-apart - sx), preferred_element_type=F32)
                    down = jnp.dot(tent(apart - sy), across.astype(BF16), preferred_element_type=F32)
                    acc[...] += weight * down

                return carry

            lax.fori_loop(0, K, entry, 0)
            out[s, i, :, pl.ds(pl.multiple_of(j * TILE, TILE), TILE)] = acc[...].astype(BF16)

            @pl.when(j == TC - 1)
            def _():
                pltpu.make_async_copy(out.at[s, i], part_ref.at[s, i], out_sems.at[s, i]).start()

            return carry

        lax.fori_loop(0, 4 * TC, target, 0)

    for s in range(S):
        for i in range(4):
            pltpu.make_async_copy(out.at[s, i], part_ref.at[s, i], out_sems.at[s, i]).wait()


def warp(metas, images, gathered):
    anywhere = pl.BlockSpec(memory_space=pl.ANY)
    dma = pltpu.SemaphoreType.DMA
    return pl.pallas_call(
        warp_kernel,
        out_shape=jax.ShapeDtypeStruct((S, 4, TILE, WIDE), BF16),
        in_specs=[pl.BlockSpec(memory_space=pltpu.SMEM), anywhere, anywhere],
        out_specs=anywhere,
        scratch_shapes=[
            pltpu.VMEM((S, 4, TILE, WIDE), BF16),
            pltpu.VMEM((TILE, TILE), F32),
            pltpu.VMEM((S, 4, TILE, WIDE), BF16),
            dma((S, 2)), dma((S, 4)),
        ],
        compiler_params=pltpu.CompilerParams(vmem_limit_bytes=32 * 1024 * 1024),
        name="warp_partials",
    )(metas, images, gathered)


CHUNK = 64
CHUNKS = TILE // CHUNK


def scatter_kernel(part_ref, zero_ref, one_ref, two_ref, own, got, pool, half, quarter, own_sem, send_sem, recv_sem):
    r = lax.axis_index("row")
    c = lax.axis_index("col")
    y = lax.rem(c, 4)
    z = c // 4
    barrier = pltpu.get_barrier_semaphore()
    for s in range(S):
        for i in (1, 2, 3):
            pl.semaphore_signal(
                barrier, inc=1, device_id=(r, peer_col(y, z, SCATTER_MASK[s], i)), device_id_type=MESH)
    mine = pltpu.make_async_copy(part_ref.at[:, 0], own, own_sem)
    mine.start()
    row = lax.broadcasted_iota(jnp.int32, (TILE, VC), 0)
    lane = lax.broadcasted_iota(jnp.int32, (TILE, VC), 1)
    pool[...] = jnp.where(row // 2 == lane, 0.25, 0.0).astype(BF16)
    pl.semaphore_wait(barrier, 6)

    def sent(q, s, i):
        rows = pl.ds(pl.multiple_of(q * CHUNK, CHUNK), CHUNK)
        return pltpu.make_async_remote_copy(
            src_ref=part_ref.at[s, i, rows], dst_ref=got.at[s, i - 1, rows],
            send_sem=send_sem.at[s, i - 1, q], recv_sem=recv_sem.at[s, i - 1, q],
            device_id=(r, peer_col(y, z, SCATTER_MASK[s], i)), device_id_type=MESH)

    @pl.loop(0, CHUNKS)
    def _(q):
        for i in (3, 1, 2):
            for s in range(S):
                sent(q, s, i).start()

    mine.wait()

    def pooled(block):
        high = block.astype(BF16)
        low = (block - high.astype(F32)).astype(BF16)
        matrix = pool[...]
        return (jnp.dot(high, matrix, preferred_element_type=F32)
                + jnp.dot(low, matrix, preferred_element_type=F32))

    @pl.loop(0, CHUNKS)
    def _(q):
        rows = pl.ds(pl.multiple_of(q * CHUNK, CHUNK), CHUNK)
        for s in range(S):
            for i in (1, 2, 3):
                sent(q, s, i).wait_recv()
            for j in range(TC):
                cols = pl.ds(j * TILE, TILE)
                block = own[s, rows, cols].astype(F32)
                for i in range(3):
                    block = block + got[s, i, rows, cols].astype(F32)
                zero_ref[s, rows, cols] = block.astype(BF16)
                half[j] = pooled(block)
            ones = []
            for j in range(TC):
                piece = half[j, pl.ds(0, CHUNK // 2, stride=2), :] + half[j, pl.ds(1, CHUNK // 2, stride=2), :]
                one_ref[s, pl.ds(pl.multiple_of(q * (CHUNK // 2), CHUNK // 2), CHUNK // 2), pl.ds(j * VC, VC)] = (
                    piece.astype(BF16))
                ones.append(piece)
            for j in range(2):
                quarter[j] = pooled(jnp.concatenate(ones[2 * j:2 * j + 2], axis=1))
                piece = quarter[j, pl.ds(0, CHUNK // 4, stride=2), :] + quarter[j, pl.ds(1, CHUNK // 4, stride=2), :]
                two_ref[s, pl.ds(pl.multiple_of(q * (CHUNK // 4), CHUNK // 4), CHUNK // 4), pl.ds(j * VC, VC)] = (
                    piece.astype(BF16))

    @pl.loop(0, CHUNKS)
    def _(q):
        for i in (3, 1, 2):
            for s in range(S):
                sent(q, s, i).wait_send()


def scatter(part):
    vmem = pl.BlockSpec(memory_space=pltpu.VMEM)
    dma = pltpu.SemaphoreType.DMA
    return pl.pallas_call(
        scatter_kernel,
        out_shape=(
            jax.ShapeDtypeStruct((S, TILE, WIDE), BF16),
            jax.ShapeDtypeStruct((S, TILE // 2, WIDE // 2), BF16),
            jax.ShapeDtypeStruct((S, TILE // 4, WIDE // 4), BF16),
        ),
        in_specs=[pl.BlockSpec(memory_space=pl.ANY)],
        out_specs=(vmem, vmem, vmem),
        scratch_shapes=[
            pltpu.VMEM((S, TILE, WIDE), BF16),
            pltpu.VMEM((S, 3, TILE, WIDE), BF16),
            pltpu.VMEM((TILE, VC), BF16),
            pltpu.VMEM((TC, CHUNK, VC), F32),
            pltpu.VMEM((2, CHUNK // 2, VC), F32),
            dma, dma((S, 3, CHUNKS)), dma((S, 3, CHUNKS)),
        ],
        compiler_params=pltpu.CompilerParams(
            collective_id=1, has_side_effects=True, vmem_limit_bytes=32 * 1024 * 1024),
        name="scatter_and_pool",
    )(part)


def shards(load_force, stiffness, cracks, anchor, images, owners, source_tile, offsets, blend_weight, counts):
    slot = jnp.arange(ENT_DEV, dtype=jnp.int32) % K
    weights = jnp.where(slot < jnp.repeat(counts, K), blend_weight, 0.0)
    codes = (owners[:, 0] * TC + source_tile).astype(F32)
    meta = jnp.concatenate([codes[None], offsets.astype(F32), weights[None]], axis=0)
    meta = jnp.pad(meta, ((0, 4), (0, VC - ENT_DEV)))
    displacement, residual, metas, gathered = relax(load_force, stiffness, cracks, anchor, meta, images)
    part = warp(metas, images, gathered)
    level_zero, level_one, level_two = scatter(part)
    return displacement, residual, level_zero, level_one, level_two


def solution(mesh):
    flat = P(("row", "col"))
    in_specs = (
        P(None, None, "row", "col"),
        P(None, None, "row", "col"),
        P(None, None, "row", "col"),
        P(None, "row", "col"),
        P(None, "row", "col"),
        P(("row", "col"), None),
        flat,
        P(None, ("row", "col")),
        flat,
        flat,
    )
    out_specs = (
        P(None, None, "row", "col"),
        P(None, None, "row", "col"),
        P(None, "row", "col"),
        P(None, "row", "col"),
        P(None, "row", "col"),
    )
    return jax.shard_map(shards, mesh=mesh, in_specs=in_specs, out_specs=out_specs, check_vma=False)
```

```python
import jax
import jax.numpy as jnp
from jax import lax
from jax.experimental import pallas as pl
from jax.experimental.pallas import tpu as pltpu
from jax.sharding import PartitionSpec as P

S = 2
TILE = 256
SPACING = 8
K = 6
ITERS = 4
TC = 4
ENT_DEV = 48
VR = 32
VC = 128
N_ROW = 8
N_COL = 16
WIDE = TC * TILE
ROWS = VR + 16
COLS = 2 * VC
MESH = pl.DeviceIdType.MESH
F32 = jnp.float32
BF16 = jnp.bfloat16


def flipped(v, mask):
    if mask == 1:
        return v + 1 - 2 * lax.rem(v, 2)
    return 3 - v


def peer_col(y, z, mask, i):
    py = flipped(y, mask) if i % 2 == 1 else y
    pz = flipped(z, mask) if i // 2 == 1 else z
    return pz * 4 + py


GATHER_MASK = (1, 3)
SCATTER_MASK = (3, 1)


NOTE = 32


def relax_kernel(
    load_hbm, stiff_hbm, crack_hbm, anchor_hbm, owner_hbm, source_hbm, offset_hbm, blend_hbm, count_hbm, images_hbm,
    disp_ref, resid_ref, metas_ref, tiles_ref,
    fields, stiff, crack, owner, source, offset, blend, count,
    strips, halo_v, halo_h, halo_c, coef, rs, ws, us, qs, ts, ps, xs,
    part_a, part_b, got_a, got_b, note, notes,
    load_sem, own_sem, halo_send, halo_recv, send_a, recv_a, send_b, recv_b,
    note_send, note_recv, tile_send, tile_recv,
):
    r = lax.axis_index("row")
    c = lax.axis_index("col")
    y = lax.rem(c, 4)
    z = c // 4
    up, down = lax.rem(r + N_ROW - 1, N_ROW), lax.rem(r + 1, N_ROW)
    left, right = lax.rem(c + N_COL - 1, N_COL), lax.rem(c + 1, N_COL)
    corners = ((up, left), (up, right), (down, left), (down, right))

    barrier = pltpu.get_barrier_semaphore()

    @pl.loop(1, N_ROW)
    def _(d):
        pl.semaphore_signal(barrier, inc=1, device_id=(lax.rem(r + d, N_ROW), c), device_id_type=MESH)

    @pl.loop(1, N_COL)
    def _(d):
        pl.semaphore_signal(barrier, inc=1, device_id=(r, lax.rem(c + d, N_COL)), device_id_type=MESH)

    for corner in corners:
        pl.semaphore_signal(barrier, inc=1, device_id=corner, device_id_type=MESH)

    loads = []
    for n, (near, far) in enumerate((
        (stiff_hbm, stiff), (crack_hbm, crack),
        (load_hbm.at[0], fields.at[pl.ds(0, 2)]), (load_hbm.at[1], fields.at[pl.ds(2, 2)]),
        (anchor_hbm, fields.at[pl.ds(8, 2)]),
        (owner_hbm, owner), (source_hbm, source), (offset_hbm, offset), (blend_hbm, blend), (count_hbm, count),
    )):
        loads.append(pltpu.make_async_copy(near, far, load_sem.at[n]))
    for copy in loads:
        copy.start()
    for copy in loads:
        copy.wait()
    for s in range(S):
        for k in range(2):
            fields[4 + 2 * s + k] = stiff[s, k] * crack[s, k].astype(F32)
    lane = lax.broadcasted_iota(jnp.int32, (VR, VC), 1)
    first = jnp.zeros((VR, VC), F32)
    last = jnp.zeros((VR, VC), F32)
    for f in range(10):
        block = fields[f]
        here = (lane >= 4 * f) & (lane < 4 * f + 4)
        first = jnp.where(here, block if f == 0 else pltpu.roll(block, 4 * f, 1), first)
        last = jnp.where(here, pltpu.roll(block, 4 * f + 4, 1), last)
    strips[0] = first
    strips[1] = last

    pl.semaphore_wait(barrier, N_ROW - 1 + N_COL - 1 + 4)

    halo = []
    for n, (near, far, device) in enumerate((
        (fields.at[:, pl.ds(VR - 8, 8), :], halo_v.at[0], (down, c)),
        (fields.at[:, pl.ds(0, 8), :], halo_v.at[1], (up, c)),
        (strips.at[1], halo_h.at[0], (r, right)),
        (strips.at[0], halo_h.at[1], (r, left)),
        (strips.at[1, pl.ds(VR - 8, 8)], halo_c.at[0], (down, right)),
        (strips.at[0, pl.ds(VR - 8, 8)], halo_c.at[1], (down, left)),
        (strips.at[1, pl.ds(0, 8)], halo_c.at[2], (up, right)),
        (strips.at[0, pl.ds(0, 8)], halo_c.at[3], (up, left)),
    )):
        halo.append(pltpu.make_async_remote_copy(
            src_ref=near, dst_ref=far, send_sem=halo_send.at[n], recv_sem=halo_recv.at[n],
            device_id=device, device_id_type=MESH))
    for copy in halo:
        copy.start()

    half = TILE // 2

    def tile_copy(s, n, slot_from, slot_to, part, peer):
        rows = pl.ds(part * half, half)
        near = images_hbm.at[s, rows] if slot_from == 0 else tiles_ref.at[s, slot_from, rows]
        return pltpu.make_async_remote_copy(
            src_ref=near, dst_ref=tiles_ref.at[s, slot_to, rows],
            send_sem=tile_send.at[s, n], recv_sem=tile_recv.at[s, n],
            device_id=(r, peer_col(y, z, GATHER_MASK[s], peer)), device_id_type=MESH)

    direct = [
        [tile_copy(s, 0, 0, 2, 0, 2), tile_copy(s, 1, 0, 1, 1, 1), tile_copy(s, 2, 0, 1, 0, 1), tile_copy(s, 3, 0, 2, 1, 2)]
        for s in range(S)
    ]
    relayed = [[tile_copy(s, 4, 2, 3, 0, 1), tile_copy(s, 5, 1, 3, 1, 2)] for s in range(S)]
    for n in range(4):
        for s in range(S):
            direct[s][n].start()
    own = pltpu.make_async_copy(images_hbm, tiles_ref.at[:, 0], own_sem)
    own.start()

    entry_lane = lax.broadcasted_iota(jnp.int32, (1, ENT_DEV), 1)
    listed = jnp.zeros((1, ENT_DEV), jnp.int32)
    for t in range(ENT_DEV // K):
        listed = jnp.where(entry_lane // K == t, count[:, t:t + 1], listed)
    note[...] = jnp.zeros((NOTE, VC), F32)
    note[0:1, 0:ENT_DEV] = owner[...].astype(F32)
    note[1:2, 0:ENT_DEV] = source[...].astype(F32)
    note[2:4, 0:ENT_DEV] = offset[...].astype(F32)
    note[4:5, 0:ENT_DEV] = jnp.where(lax.rem(entry_lane, K) < listed, blend[...], 0.0)

    for copy in halo:
        copy.wait_recv()

    wide_row = lax.broadcasted_iota(jnp.int32, (ROWS, VC), 0) + r * VR - 8
    wide_lane = lax.broadcasted_iota(jnp.int32, (ROWS, VC), 1)
    side_col = jnp.where(wide_lane < VC // 2, wide_lane + VC, wide_lane - VC) + c * VC
    row_in = (wide_row >= 0) & (wide_row < VR * N_ROW)
    side_in = row_in & (side_col >= 0) & (side_col < VC * N_COL)
    from_left = jnp.concatenate([halo_c[0], halo_h[0], halo_c[2]], axis=0)
    from_right = jnp.concatenate([halo_c[1], halo_h[1], halo_c[3]], axis=0)

    def widened(f):
        center = jnp.concatenate([halo_v[0, f], fields[f], halo_v[1, f]], axis=0)
        to_left = pltpu.roll(from_left, 124 - 4 * f, 1)
        to_right = from_right if f == 0 else pltpu.roll(from_right, VC - 4 * f, 1)
        side = jnp.where(wide_lane < 4, to_right, jnp.where(wide_lane >= 124, to_left, 0.0))
        return jnp.concatenate(
            [jnp.where(row_in, center, 0.0), jnp.where(side_in, side, 0.0)], axis=1)

    inside = jnp.concatenate([row_in.astype(F32), side_in.astype(F32)], axis=1)
    for s in range(S):
        to_right = widened(4 + 2 * s)
        to_low = widened(5 + 2 * s)
        to_left = pltpu.roll(to_right, 1, 1) * inside
        to_high = pltpu.roll(to_low, 1, 0) * inside
        coef[s, 0] = widened(8 + s) + to_right + to_left + to_low + to_high
        coef[s, 1] = to_right
        coef[s, 2] = to_left
        coef[s, 3] = to_low
        coef[s, 4] = to_high
        for k in range(2):
            rs[2 * s + k] = widened(2 * s + k)

    def operate(near, far):
        for f in range(4):
            s = f // 2
            v = near[f]
            w = coef[s, 0] * v
            w = w - coef[s, 1] * pltpu.roll(v, COLS - 1, 1)
            w = w - coef[s, 2] * pltpu.roll(v, 1, 1)
            w = w - coef[s, 3] * pltpu.roll(v, ROWS - 1, 0)
            w = w - coef[s, 4] * pltpu.roll(v, 1, 0)
            far[f] = w

    def core(ref, f):
        return ref[f, pl.ds(8, VR), pl.ds(0, VC)]

    def reduced(n, pairs):
        rows = []
        for one, other in pairs:
            for s in range(S):
                total = jnp.zeros((8, VC), F32)
                for k in range(2):
                    f = 2 * s + k
                    total = total + jnp.sum((core(one, f) * core(other, f)).reshape(VR // 8, 8, VC), axis=0)
                rows.append(jnp.sum(total, axis=0, keepdims=True))
        height = -(-len(rows) // 8) * 8
        if height > len(rows):
            rows.append(jnp.zeros((height - len(rows), VC), F32))
        span = pl.ds(0, height)
        part_a[n, span] = jnp.concatenate(rows, axis=0)

        @pl.loop(1, N_ROW)
        def _(d):
            pltpu.make_async_remote_copy(
                src_ref=part_a.at[n, span], dst_ref=got_a.at[n, d - 1, span], send_sem=send_a.at[n],
                recv_sem=recv_a.at[n], device_id=(lax.rem(r + d, N_ROW), c), device_id_type=MESH).start()

        sum_copy(n, height, 0).wait_recv()
        part_b[n, span] = part_a[n, span] + jnp.sum(got_a[n, :, span], axis=0)

        @pl.loop(1, N_COL)
        def _(d):
            pltpu.make_async_remote_copy(
                src_ref=part_b.at[n, span], dst_ref=got_b.at[n, d - 1, span], send_sem=send_b.at[n],
                recv_sem=recv_b.at[n], device_id=(r, lax.rem(c + d, N_COL)), device_id_type=MESH).start()

        sum_copy(n, height, 1).wait_recv()
        total = part_b[n, span] + jnp.sum(got_b[n, :, span], axis=0)
        total = jnp.sum(total, axis=1, keepdims=True)
        return [total[2 * m:2 * m + 2] for m in range(len(pairs))]

    def sum_copy(n, height, phase):
        got, send, recv = ((got_a, send_a, recv_a), (got_b, send_b, recv_b))[phase]
        return pltpu.make_async_remote_copy(
            src_ref=got.at[n, :, pl.ds(0, height)], dst_ref=got.at[n, :, pl.ds(0, height)],
            send_sem=send.at[n], recv_sem=recv.at[n],
            device_id=((down, c), (r, right))[phase], device_id_type=MESH)

    operate(rs, ws)
    operate(ws, us)
    m0, m1, m2, m3 = reduced(0, ((rs, rs), (rs, ws), (ws, ws), (ws, us)))
    a0 = m0 / m1
    n1 = a0 * a0 * m2 - m0
    b0 = n1 / m0
    g0 = 1.0 + b0
    a1 = n1 / (g0 * g0 * m1 - 2.0 * g0 * a0 * m2 + a0 * a0 * m3)
    for f in range(4):
        s = f // 2
        step0, step1, grow = a0[s:s + 1], a1[s:s + 1], g0[s:s + 1]
        v, w = rs[f], ws[f]
        p = grow * v - step0 * w
        q = grow * w - step0 * us[f]
        ps[f] = p
        qs[f] = q
        xs[f] = step0 * v + step1 * p
        rs[f] = v - step0 * w - step1 * q

    for s in range(S):
        direct[s][0].wait_recv()
        relayed[s][0].start()
        direct[s][1].wait_recv()
        relayed[s][1].start()

    operate(rs, ws)
    middle = 8 + VR // 2
    basis = (xs, ps, rs, ws, qs)
    for b, ref in enumerate(basis):
        for f in range(4):
            note[8 + 4 * b + f:9 + 4 * b + f, :] = ref[f, pl.ds(middle, 1), pl.ds(0, VC)]
    told = []
    for s in range(S):
        for i in (1, 2, 3):
            told.append(pltpu.make_async_remote_copy(
                src_ref=note, dst_ref=notes.at[s, i - 1],
                send_sem=note_send.at[s, i - 1], recv_sem=note_recv.at[s, i - 1],
                device_id=(r, peer_col(y, z, SCATTER_MASK[s], i)), device_id_type=MESH))
    for copy in told:
        copy.start()
    operate(ws, us)
    operate(qs, ts)
    rr, rw, rq, ww, wq, qq, wu, uq, qt = reduced(1, (
        (rs, rs), (rs, ws), (rs, qs), (ws, ws), (ws, qs), (qs, qs), (ws, us), (us, qs), (qs, ts)))
    b1 = rr / n1
    a2 = rr / (rw - b1 * rr / a1)
    q2q2 = ww + 2.0 * b1 * wq + b1 * b1 * qq
    n3 = rr - 2.0 * a2 * (rw + b1 * rq) + a2 * a2 * q2q2
    b2 = n3 / rr
    r3ar3 = rw - 2.0 * a2 * (ww + b1 * wq) + a2 * a2 * (wu + 2.0 * b1 * uq + b1 * b1 * qt)
    a3 = n3 / (r3ar3 - b2 * n3 / a2)

    weights = (None, (a2 + a3 * b2) * b1, a2 + a3 * b2 + a3, -a3 * a2, -a3 * a2 * b1)
    for f in range(4):
        s, k = f // 2, f % 2
        step2, step3 = a2[s:s + 1], a3[s:s + 1]
        grow1, grow2 = b1[s:s + 1], b2[s:s + 1]
        v, w, q = core(rs, f), core(ws, f), core(qs, f)
        p2 = v + grow1 * core(ps, f)
        q2 = w + grow1 * q
        r3 = v - step2 * q2
        p3 = r3 + grow2 * p2
        q3 = w - step2 * (core(us, f) + grow1 * core(ts, f)) + grow2 * q2
        disp_ref[s, k] = core(xs, f) + step2 * p2 + step3 * p3
        resid_ref[s, k] = r3 - step3 * q3

    for copy in told:
        copy.wait_recv()
    note_lane = lax.broadcasted_iota(jnp.int32, (1, VC), 1)
    for s in range(S):
        for i in range(4):
            text = note if i == 0 else notes.at[s, i - 1]
            at = text[0:1, :].astype(jnp.int32)
            at_y, at_z = lax.rem(at, 4), at // 4
            weight = text[4:5, :]
            mine = (at_y == y) | (at_y == flipped(y, GATHER_MASK[s]))
            mine = mine & ((at_z == z) | (at_z == flipped(z, GATHER_MASK[s])))
            mine = mine & (weight > 0.0) & (note_lane < ENT_DEV)
            slot = jnp.where(at_y == y, 0, 1) + jnp.where(at_z == z, 0, 2)
            key = jnp.where(mine, slot * TC + text[1:2, :].astype(jnp.int32), -1)
            shift = text[8 + 2 * s:10 + 2 * s, :]
            for b in range(1, 5):
                shift = shift + weights[b][s:s + 1] * text[8 + 4 * b + 2 * s:10 + 4 * b + 2 * s, :]
            metas_ref[s, i] = jnp.concatenate(
                [key.astype(F32), text[2:4, :], weight, shift, jnp.zeros((2, VC), F32)], axis=0)

    for copy in told:
        copy.wait_send()
    for copy in halo:
        copy.wait_send()
    for n, height in enumerate((8, 24)):
        for phase in range(2):
            sum_copy(n, height, phase).wait_send()
    own.wait()
    for s in range(S):
        direct[s][2].wait_recv()
        direct[s][3].wait_recv()
        for copy in relayed[s]:
            copy.wait()
        for copy in direct[s]:
            copy.wait_send()


def relax(*operands):
    vmem = pl.BlockSpec(memory_space=pltpu.VMEM)
    hbm = pl.BlockSpec(memory_space=pltpu.HBM)
    dma = pltpu.SemaphoreType.DMA
    wide = pltpu.VMEM((4, ROWS, COLS), F32)
    block = (S, 2, VR, VC)
    return pl.pallas_call(
        relax_kernel,
        out_shape=(
            jax.ShapeDtypeStruct(block, F32),
            jax.ShapeDtypeStruct(block, F32),
            jax.ShapeDtypeStruct((S, 4, 8, VC), F32),
            jax.ShapeDtypeStruct((S, 4, TILE, WIDE), BF16),
        ),
        in_specs=[hbm] * 10,
        out_specs=(vmem, vmem, vmem, vmem),
        scratch_shapes=[
            pltpu.VMEM((10, VR, VC), F32),
            pltpu.VMEM(block, F32),
            pltpu.VMEM(block, jnp.int32),
            pltpu.VMEM((1, ENT_DEV), jnp.int32),
            pltpu.VMEM((1, ENT_DEV), jnp.int32),
            pltpu.VMEM((2, ENT_DEV), jnp.int32),
            pltpu.VMEM((1, ENT_DEV), F32),
            pltpu.VMEM((1, ENT_DEV // K), jnp.int32),
            pltpu.VMEM((2, VR, VC), F32),
            pltpu.VMEM((2, 10, 8, VC), F32),
            pltpu.VMEM((2, VR, VC), F32),
            pltpu.VMEM((4, 8, VC), F32),
            pltpu.VMEM((S, 5, ROWS, COLS), F32),
            wide, wide, wide, wide, wide, wide, wide,
            pltpu.VMEM((2, 24, VC), F32),
            pltpu.VMEM((2, 24, VC), F32),
            pltpu.VMEM((2, N_ROW - 1, 24, VC), F32),
            pltpu.VMEM((2, N_COL - 1, 24, VC), F32),
            pltpu.VMEM((NOTE, VC), F32),
            pltpu.VMEM((S, 3, NOTE, VC), F32),
            dma((10,)), dma, dma((8,)), dma((8,)),
            dma((2,)), dma((2,)), dma((2,)), dma((2,)),
            dma((S, 3)), dma((S, 3)), dma((S, 6)), dma((S, 6)),
        ],
        compiler_params=pltpu.CompilerParams(
            collective_id=0, has_side_effects=True, vmem_limit_bytes=32 * 1024 * 1024),
        name="relax_and_gather",
    )(*operands)


BATCH = 2


def warp_kernel(meta_ref, tiles_ref, part_ref, apart, where_list, weight_list):
    def listing(s, n, count):
        i = n // (TC * K)
        e = lax.rem(n, TC * K)
        key = meta_ref[s, i, 0, s * TC * K + e].astype(jnp.int32)
        where_list[count] = ((s * 4 + i) * 32 + e) * 16 + jnp.maximum(key, 0)
        weight_list[count] = meta_ref[s, i, 3, s * TC * K + e]
        return count + jnp.where(key >= 0, 1, 0)

    count = 0
    for s in range(S):
        count = lax.fori_loop(0, 4 * TC * K, lambda n, total, s=s: listing(s, n, total), count)
    for n in range(BATCH - 1):
        where_list[count + n] = 0
        weight_list[count + n] = 0.0

    row = lax.broadcasted_iota(jnp.int32, (TILE, TILE), 0)
    lane = lax.broadcasted_iota(jnp.int32, (TILE, TILE), 1)
    apart[...] = (lane - row).astype(F32).astype(BF16)
    part_ref[...] = jnp.zeros(part_ref.shape, BF16)

    def sampled(shift, side):
        shift = jnp.full((1, TILE), shift, F32)
        low = jnp.floor(shift)
        at_low = jnp.maximum(0.0, 1.0 - jnp.abs(low - shift)).astype(BF16)
        at_high = jnp.maximum(0.0, 1.0 - jnp.abs(low + 1.0 - shift)).astype(BF16)
        low_place = (side * low).astype(BF16)
        high_place = (side * (low + 1.0)).astype(BF16)
        matrix = apart[...]
        return jnp.where(matrix == low_place, at_low, jnp.where(matrix == high_place, at_high, jnp.zeros((), BF16)))

    def entry(n):
        code = where_list[n]
        key = code & 15
        e = (code >> 4) & 31
        place = code >> 9
        s = place >> 2
        i = place & 3
        j = (e * 43) >> 8
        at = s * TC * K + e
        sy = meta_ref[s, i, 1, at] + SPACING * meta_ref[s, i, 4, 32 * j + 16]
        sx = meta_ref[s, i, 2, at] + SPACING * meta_ref[s, i, 5, 32 * j + 16]
        source = tiles_ref[s, key >> 2, :, pl.ds(pl.multiple_of((key & 3) * TILE, TILE), TILE)]
        across = jnp.dot(source, sampled(sx, -1.0), preferred_element_type=F32)
        down = jnp.dot(sampled(sy, 1.0), across.astype(BF16), preferred_element_type=F32)
        return weight_list[n] * down, (s, i, slice(None), pl.ds(pl.multiple_of(j * TILE, TILE), TILE))

    def batch(b, carry):
        found = [entry(b * BATCH + n) for n in range(BATCH)]
        for value, place in found:
            part_ref[place] = (part_ref[place].astype(F32) + value).astype(BF16)
        return carry

    lax.fori_loop(0, (count + BATCH - 1) // BATCH, batch, 0)


def warp(metas, tiles):
    vmem = pl.BlockSpec(memory_space=pltpu.VMEM)
    return pl.pallas_call(
        warp_kernel,
        out_shape=jax.ShapeDtypeStruct((S, 4, TILE, WIDE), BF16),
        in_specs=[pl.BlockSpec(memory_space=pltpu.SMEM), vmem],
        out_specs=vmem,
        scratch_shapes=[
            pltpu.VMEM((TILE, TILE), BF16),
            pltpu.SMEM((256,), jnp.int32),
            pltpu.SMEM((256,), F32),
        ],
        compiler_params=pltpu.CompilerParams(vmem_limit_bytes=32 * 1024 * 1024),
        name="warp_partials",
    )(metas, tiles)


CHUNK = 64
HALVES = 2
SUBS = TILE // CHUNK // HALVES


def scatter_kernel(
    part_ref, zero_ref, one_ref, two_ref,
    relay, onward, got, pool, half, quarter,
    relay_send, relay_recv, direct_send, direct_recv, onward_send, onward_recv,
):
    r = lax.axis_index("row")
    c = lax.axis_index("col")
    y = lax.rem(c, 4)
    z = c // 4
    barrier = pltpu.get_barrier_semaphore()
    for s in range(S):
        for i in (1, 2):
            pl.semaphore_signal(
                barrier, inc=1, device_id=(r, peer_col(y, z, SCATTER_MASK[s], i)), device_id_type=MESH)
    row = lax.broadcasted_iota(jnp.int32, (TILE, VC), 0)
    lane = lax.broadcasted_iota(jnp.int32, (TILE, VC), 1)
    pool[...] = jnp.where(row // 2 == lane, 0.25, 0.0).astype(BF16)
    pl.semaphore_wait(barrier, 2 * S)

    def rows_of(h, u):
        return pl.ds((h * SUBS + u) * CHUNK, CHUNK)

    def copy_to(s, peer, near, far, send, recv):
        return pltpu.make_async_remote_copy(
            src_ref=near, dst_ref=far, send_sem=send, recv_sem=recv,
            device_id=(r, peer_col(y, z, SCATTER_MASK[s], peer)), device_id_type=MESH)

    def to_relay(s, h, u):
        return copy_to(s, h + 1, part_ref.at[s, 3, rows_of(h, u)], relay.at[s, h, u],
                       relay_send.at[s, h, u], relay_recv.at[s, h, u])

    def to_end(s, h, u):
        return copy_to(s, h + 1, part_ref.at[s, h + 1, rows_of(h, u)], got.at[s, h, rows_of(h, u)],
                       direct_send.at[s, h, u], direct_recv.at[s, h, u])

    def to_end_summed(s, h, u):
        other = 1 - h
        return copy_to(s, other + 1, onward.at[s, h, u], got.at[s, other, rows_of(h, u)],
                       onward_send.at[s, h, u], onward_recv.at[s, h, u])

    steps = [(u, h, s) for u in range(SUBS) for h in range(HALVES) for s in range(S)]
    for u, h, s in steps:
        to_relay(s, h, u).start()
    for u, h, s in steps:
        to_end(s, h, u).start()
    for u, h, s in steps:
        to_relay(s, h, u).wait_recv()
        added = relay[s, h, u].astype(F32) + part_ref[s, 2 - h, rows_of(h, u)].astype(F32)
        onward[s, h, u] = added.astype(BF16)
        to_end_summed(s, h, u).start()

    def pooled(block):
        high = block.astype(BF16)
        low = (block - high.astype(F32)).astype(BF16)
        matrix = pool[...]
        return (jnp.dot(high, matrix, preferred_element_type=F32)
                + jnp.dot(low, matrix, preferred_element_type=F32))

    for u, h, s in steps:
        to_end(s, h, u).wait_recv()
        to_end_summed(s, h, u).wait_recv()
        q = h * SUBS + u
        rows = rows_of(h, u)
        for j in range(TC):
            cols = pl.ds(j * TILE, TILE)
            block = part_ref[s, 0, rows, cols].astype(F32)
            for i in range(2):
                block = block + got[s, i, rows, cols].astype(F32)
            zero_ref[s, rows, cols] = block.astype(BF16)
            half[j] = pooled(block)
        ones = []
        for j in range(TC):
            piece = half[j, pl.ds(0, CHUNK // 2, stride=2), :] + half[j, pl.ds(1, CHUNK // 2, stride=2), :]
            one_ref[s, pl.ds(q * (CHUNK // 2), CHUNK // 2), pl.ds(j * VC, VC)] = piece.astype(BF16)
            ones.append(piece)
        for j in range(2):
            quarter[j] = pooled(jnp.concatenate(ones[2 * j:2 * j + 2], axis=1))
            piece = quarter[j, pl.ds(0, CHUNK // 4, stride=2), :] + quarter[j, pl.ds(1, CHUNK // 4, stride=2), :]
            two_ref[s, pl.ds(q * (CHUNK // 4), CHUNK // 4), pl.ds(j * VC, VC)] = piece.astype(BF16)

    for u, h, s in steps:
        to_relay(s, h, u).wait_send()
        to_end(s, h, u).wait_send()
        to_end_summed(s, h, u).wait_send()


def scatter(part):
    vmem = pl.BlockSpec(memory_space=pltpu.VMEM)
    dma = pltpu.SemaphoreType.DMA
    parts = (S, HALVES, SUBS)
    return pl.pallas_call(
        scatter_kernel,
        out_shape=(
            jax.ShapeDtypeStruct((S, TILE, WIDE), BF16),
            jax.ShapeDtypeStruct((S, TILE // 2, WIDE // 2), BF16),
            jax.ShapeDtypeStruct((S, TILE // 4, WIDE // 4), BF16),
        ),
        in_specs=[vmem],
        out_specs=(vmem, vmem, vmem),
        scratch_shapes=[
            pltpu.VMEM(parts + (CHUNK, WIDE), BF16),
            pltpu.VMEM(parts + (CHUNK, WIDE), BF16),
            pltpu.VMEM((S, 2, TILE, WIDE), BF16),
            pltpu.VMEM((TILE, VC), BF16),
            pltpu.VMEM((TC, CHUNK, VC), F32),
            pltpu.VMEM((2, CHUNK // 2, VC), F32),
            dma(parts), dma(parts), dma(parts), dma(parts), dma(parts), dma(parts),
        ],
        compiler_params=pltpu.CompilerParams(
            collective_id=1, has_side_effects=True, vmem_limit_bytes=32 * 1024 * 1024),
        name="scatter_and_pool",
    )(part)


def store_kernel(*refs):
    count = (len(refs) - 1) // 2
    sems = refs[-1]
    copies = [pltpu.make_async_copy(refs[n], refs[count + n], sems.at[n]) for n in range(count)]
    for copy in copies:
        copy.start()
    for copy in copies:
        copy.wait()


def store(*arrays):
    count = len(arrays)
    return pl.pallas_call(
        store_kernel,
        out_shape=tuple(jax.ShapeDtypeStruct(a.shape, a.dtype) for a in arrays),
        in_specs=[pl.BlockSpec(memory_space=pltpu.VMEM)] * count,
        out_specs=(pl.BlockSpec(memory_space=pltpu.HBM),) * count,
        scratch_shapes=[pltpu.SemaphoreType.DMA((count,))],
        compiler_params=pltpu.CompilerParams(vmem_limit_bytes=32 * 1024 * 1024),
        name="store_results",
    )(*arrays)


def shards(load_force, stiffness, cracks, anchor, images, owners, source_tile, offsets, blend_weight, counts):
    flat = [a.reshape(1, -1) for a in (owners, source_tile)]
    displacement, residual, metas, tiles = relax(
        load_force, stiffness, cracks, anchor, *flat, offsets, blend_weight.reshape(1, -1), counts.reshape(1, -1), images)
    part = warp(metas, tiles)
    level_zero, level_one, level_two = scatter(part)
    return store(displacement, residual, level_zero, level_one, level_two)


def solution(mesh):
    flat = P(("row", "col"))
    in_specs = (
        P(None, None, "row", "col"),
        P(None, None, "row", "col"),
        P(None, None, "row", "col"),
        P(None, "row", "col"),
        P(None, "row", "col"),
        P(("row", "col"), None),
        flat,
        P(None, ("row", "col")),
        flat,
        flat,
    )
    out_specs = (
        P(None, None, "row", "col"),
        P(None, None, "row", "col"),
        P(None, "row", "col"),
        P(None, "row", "col"),
        P(None, "row", "col"),
    )
    return jax.shard_map(shards, mesh=mesh, in_specs=in_specs, out_specs=out_specs, check_vma=False)
```

```python
import jax
import jax.numpy as jnp
from jax import lax
from jax.experimental import pallas as pl
from jax.experimental.pallas import tpu as pltpu
from jax.sharding import PartitionSpec as P

S = 2
TILE = 256
SPACING = 8
K = 6
ITERS = 4
TC = 4
ENT_DEV = 48
VR = 32
VC = 128
N_ROW = 8
N_COL = 16
WIDE = TC * TILE
ROWS = VR + 16
COLS = 2 * VC
MESH = pl.DeviceIdType.MESH
F32 = jnp.float32
BF16 = jnp.bfloat16


def flipped(v, mask):
    if mask == 1:
        return v + 1 - 2 * lax.rem(v, 2)
    return 3 - v


def peer_col(y, z, mask, i):
    py = flipped(y, mask) if i % 2 == 1 else y
    pz = flipped(z, mask) if i // 2 == 1 else z
    return pz * 4 + py


GATHER_MASK = (1, 3)
SCATTER_MASK = (3, 1)


NOTE = 24
MOMENTS = 2 * ITERS
SCALE = 8.0


def two_sum(a, b):
    total = a + b
    part = total - a
    return total, (a - (total - part)) + (b - part)


def renormed(high, low):
    total = high + low
    return total, low - (total - high)


def split(a):
    wide = a * 4097.0
    high = wide - (wide - a)
    return high, a - high


def two_product(a, b, a_parts, b_parts):
    (ah, al), (bh, bl) = a_parts, b_parts
    product = a * b
    return product, ((ah * bh - product) + ah * bl + al * bh) + al * bl


def added(x, y):
    total, rest = two_sum(x[0], y[0])
    return renormed(total, rest + (x[1] + y[1]))


def times(x, y):
    product, rest = two_product(x[0], y[0], split(x[0]), split(y[0]))
    return renormed(product, rest + (x[0] * y[1] + x[1] * y[0]))


def minus(x):
    return -x[0], -x[1]


def over(x, y):
    first = x[0] / y[0]
    nothing = jnp.zeros_like(first)
    rest = added(x, minus(times((first, nothing), y)))
    return renormed(first, rest[0] / y[0])


def residual_polynomial(moment):
    one = (jnp.ones_like(moment[0][0]), jnp.zeros_like(moment[0][0]))
    rho, pi = [one], [one]
    upper = moment[0]
    for k in range(ITERS):
        lower = None
        for j, weight in enumerate(pi):
            term = moment[j + k + 1] if k == 0 else times(weight, moment[j + k + 1])
            lower = term if lower is None else added(lower, term)
        step = over(upper, lower)
        moved = [minus(times(step, weight)) if k else minus(step) for weight in pi]
        rho = [rho[0]] + [added(rho[j], moved[j - 1]) for j in range(1, k + 1)] + [moved[k]]
        if k == ITERS - 1:
            return rho
        upper = moment[k + 1]
        for j in range(1, k + 2):
            upper = added(upper, times(rho[j], moment[j + k + 1]))
        grow = minus(over(upper, lower))
        pi = [added(rho[j], times(grow, pi[j]) if k else grow) for j in range(k + 1)] + [rho[k + 1]]


def relax_kernel(
    load_hbm, stiff_hbm, crack_hbm, anchor_hbm, owner_hbm, source_hbm, offset_hbm, blend_hbm, count_hbm, images_hbm,
    disp_ref, resid_ref, metas_ref, codes_ref, tiles_ref, blank_ref,
    fields, stiff, crack, owner, source, offset, blend, count,
    strips, halo_v, halo_h, halo_c, coef, krylov,
    part_a, part_b, got_a, got_b, note, notes, sums,
    load_sem, own_sem, halo_send, halo_recv, send_a, recv_a, send_b, recv_b,
    note_send, note_recv, tile_send, tile_recv,
):
    r = lax.axis_index("row")
    c = lax.axis_index("col")
    y = lax.rem(c, 4)
    z = c // 4
    up, down = lax.rem(r + N_ROW - 1, N_ROW), lax.rem(r + 1, N_ROW)
    left, right = lax.rem(c + N_COL - 1, N_COL), lax.rem(c + 1, N_COL)
    corners = ((up, left), (up, right), (down, left), (down, right))

    barrier = pltpu.get_barrier_semaphore()

    @pl.loop(1, N_ROW)
    def _(d):
        pl.semaphore_signal(barrier, inc=1, device_id=(lax.rem(r + d, N_ROW), c), device_id_type=MESH)

    @pl.loop(1, N_COL)
    def _(d):
        pl.semaphore_signal(barrier, inc=1, device_id=(r, lax.rem(c + d, N_COL)), device_id_type=MESH)

    for corner in corners:
        pl.semaphore_signal(barrier, inc=1, device_id=corner, device_id_type=MESH)

    loads = []
    for n, (near, far) in enumerate((
        (stiff_hbm, stiff), (crack_hbm, crack),
        (load_hbm.at[0], fields.at[pl.ds(0, 2)]), (load_hbm.at[1], fields.at[pl.ds(2, 2)]),
        (anchor_hbm, fields.at[pl.ds(8, 2)]),
        (owner_hbm, owner), (source_hbm, source), (offset_hbm, offset), (blend_hbm, blend), (count_hbm, count),
    )):
        loads.append(pltpu.make_async_copy(near, far, load_sem.at[n]))
    for copy in loads:
        copy.start()
    for copy in loads:
        copy.wait()
    for s in range(S):
        for k in range(2):
            fields[4 + 2 * s + k] = stiff[s, k] * crack[s, k].astype(F32)
    lane = lax.broadcasted_iota(jnp.int32, (VR, VC), 1)
    first = jnp.zeros((VR, VC), F32)
    last = jnp.zeros((VR, VC), F32)
    for f in range(10):
        block = fields[f]
        here = (lane >= 4 * f) & (lane < 4 * f + 4)
        first = jnp.where(here, block if f == 0 else pltpu.roll(block, 4 * f, 1), first)
        last = jnp.where(here, pltpu.roll(block, 4 * f + 4, 1), last)
    strips[0] = first
    strips[1] = last

    pl.semaphore_wait(barrier, N_ROW - 1 + N_COL - 1 + 4)

    halo = []
    for n, (near, far, device) in enumerate((
        (fields.at[:, pl.ds(VR - 8, 8), :], halo_v.at[0], (down, c)),
        (fields.at[:, pl.ds(0, 8), :], halo_v.at[1], (up, c)),
        (strips.at[1], halo_h.at[0], (r, right)),
        (strips.at[0], halo_h.at[1], (r, left)),
        (strips.at[1, pl.ds(VR - 8, 8)], halo_c.at[0], (down, right)),
        (strips.at[0, pl.ds(VR - 8, 8)], halo_c.at[1], (down, left)),
        (strips.at[1, pl.ds(0, 8)], halo_c.at[2], (up, right)),
        (strips.at[0, pl.ds(0, 8)], halo_c.at[3], (up, left)),
    )):
        halo.append(pltpu.make_async_remote_copy(
            src_ref=near, dst_ref=far, send_sem=halo_send.at[n], recv_sem=halo_recv.at[n],
            device_id=device, device_id_type=MESH))
    for copy in halo:
        copy.start()

    half = TILE // 2

    def tile_copy(s, n, slot_from, slot_to, part, peer):
        rows = pl.ds(part * half, half)
        near = images_hbm.at[s, rows] if slot_from == 0 else tiles_ref.at[s, slot_from, rows]
        return pltpu.make_async_remote_copy(
            src_ref=near, dst_ref=tiles_ref.at[s, slot_to, rows],
            send_sem=tile_send.at[s, n], recv_sem=tile_recv.at[s, n],
            device_id=(r, peer_col(y, z, GATHER_MASK[s], peer)), device_id_type=MESH)

    direct = [
        [tile_copy(s, 0, 0, 2, 0, 2), tile_copy(s, 1, 0, 1, 1, 1), tile_copy(s, 2, 0, 1, 0, 1), tile_copy(s, 3, 0, 2, 1, 2)]
        for s in range(S)
    ]
    relayed = [[tile_copy(s, 4, 2, 3, 0, 1), tile_copy(s, 5, 1, 3, 1, 2)] for s in range(S)]
    for n in range(4):
        for s in range(S):
            direct[s][n].start()
    own = pltpu.make_async_copy(images_hbm, tiles_ref.at[:, 0], own_sem)
    own.start()

    entry_lane = lax.broadcasted_iota(jnp.int32, (1, ENT_DEV), 1)
    listed = jnp.zeros((1, ENT_DEV), jnp.int32)
    for t in range(ENT_DEV // K):
        listed = jnp.where(entry_lane // K == t, count[:, t:t + 1], listed)
    note[...] = jnp.zeros((NOTE, VC), F32)
    note[0:1, 0:ENT_DEV] = owner[...].astype(F32)
    note[1:2, 0:ENT_DEV] = source[...].astype(F32)
    note[2:4, 0:ENT_DEV] = offset[...].astype(F32)
    note[4:5, 0:ENT_DEV] = jnp.where(lax.rem(entry_lane, K) < listed, blend[...], 0.0)

    blank_ref[...] = jnp.zeros(blank_ref.shape, BF16)

    for copy in halo:
        copy.wait_recv()

    wide_row = lax.broadcasted_iota(jnp.int32, (ROWS, VC), 0) + r * VR - 8
    wide_lane = lax.broadcasted_iota(jnp.int32, (ROWS, VC), 1)
    side_col = jnp.where(wide_lane < VC // 2, wide_lane + VC, wide_lane - VC) + c * VC
    row_in = (wide_row >= 0) & (wide_row < VR * N_ROW)
    side_in = row_in & (side_col >= 0) & (side_col < VC * N_COL)
    from_left = jnp.concatenate([halo_c[0], halo_h[0], halo_c[2]], axis=0)
    from_right = jnp.concatenate([halo_c[1], halo_h[1], halo_c[3]], axis=0)

    def widened(f):
        center = jnp.concatenate([halo_v[0, f], fields[f], halo_v[1, f]], axis=0)
        to_left = pltpu.roll(from_left, 124 - 4 * f, 1)
        to_right = from_right if f == 0 else pltpu.roll(from_right, VC - 4 * f, 1)
        side = jnp.where(wide_lane < 4, to_right, jnp.where(wide_lane >= 124, to_left, 0.0))
        return jnp.concatenate(
            [jnp.where(row_in, center, 0.0), jnp.where(side_in, side, 0.0)], axis=1)

    inside = jnp.concatenate([row_in.astype(F32), side_in.astype(F32)], axis=1)
    for s in range(S):
        to_right = widened(4 + 2 * s)
        to_low = widened(5 + 2 * s)
        to_left = pltpu.roll(to_right, 1, 1) * inside
        to_high = pltpu.roll(to_low, 1, 0) * inside
        coef[s, 0] = widened(8 + s) + to_right + to_left + to_low + to_high
        coef[s, 1] = to_right
        coef[s, 2] = to_left
        coef[s, 3] = to_low
        coef[s, 4] = to_high
        for k in range(2):
            krylov[0, 2 * s + k] = widened(2 * s + k)

    for n in range(ITERS):
        for f in range(4):
            s = f // 2
            v = krylov[n, f]
            w = coef[s, 0] * v
            w = w - coef[s, 1] * pltpu.roll(v, COLS - 1, 1)
            w = w - coef[s, 2] * pltpu.roll(v, 1, 1)
            w = w - coef[s, 3] * pltpu.roll(v, ROWS - 1, 0)
            w = w - coef[s, 4] * pltpu.roll(v, 1, 0)
            krylov[n + 1, f] = w * (1.0 / SCALE)

    middle = 8 + VR // 2
    for n in range(ITERS):
        for f in range(4):
            note[8 + 4 * n + f:9 + 4 * n + f, :] = krylov[n, f, pl.ds(middle, 1), pl.ds(0, VC)]
    told = []
    for s in range(S):
        for i in (1, 2, 3):
            told.append(pltpu.make_async_remote_copy(
                src_ref=note, dst_ref=notes.at[s, i - 1],
                send_sem=note_send.at[s, i - 1], recv_sem=note_recv.at[s, i - 1],
                device_id=(r, peer_col(y, z, SCATTER_MASK[s], i)), device_id_type=MESH))

    moments = [[None] * S for _ in range(MOMENTS)]
    for s in range(S):
        totals = [None] * MOMENTS
        for f in (2 * s, 2 * s + 1):
            for g in range(VR // 8):
                vectors = [krylov[n, f, pl.ds(8 + 8 * g, 8), pl.ds(0, VC)] for n in range(ITERS + 1)]
                parts = [split(v) for v in vectors]
                for m in range(MOMENTS):
                    a, b = m // 2, m - m // 2
                    product, rest = two_product(vectors[a], vectors[b], parts[a], parts[b])
                    if totals[m] is None:
                        totals[m] = (product, rest)
                    else:
                        total, slip = two_sum(totals[m][0], product)
                        totals[m] = (total, totals[m][1] + (rest + slip))
        for m in range(MOMENTS):
            moments[m][s] = totals[m]

    level = [moments[m][s] for m in range(MOMENTS) for s in range(S)]
    sublane = lax.broadcasted_iota(jnp.int32, (8, VC), 0)
    packed = []
    for base in range(0, len(level), 8):
        group = level[base:base + 8]
        shift = 4
        while shift:
            low = lax.rem(sublane // shift, 2) == 0
            merged = []
            for n in range(shift):
                a, b = group[n], group[n + shift]
                first = tuple(jnp.where(low, u, pltpu.roll(v, shift, 0)) for u, v in zip(a, b))
                second = tuple(jnp.where(low, pltpu.roll(u, 8 - shift, 0), v) for u, v in zip(a, b))
                merged.append(added(first, second))
            group = merged
            shift //= 2
        packed.append(group[0])
    height = 4 * 8
    part_a[...] = jnp.concatenate([packed[0][0], packed[1][0], packed[0][1], packed[1][1]], axis=0)

    @pl.loop(1, N_ROW)
    def _(d):
        pltpu.make_async_remote_copy(
            src_ref=part_a, dst_ref=got_a.at[d - 1], send_sem=send_a,
            recv_sem=recv_a, device_id=(lax.rem(r + d, N_ROW), c), device_id_type=MESH).start()

    for copy in told:
        copy.start()

    def sum_copy(phase):
        got, send, recv = ((got_a, send_a, recv_a), (got_b, send_b, recv_b))[phase]
        return pltpu.make_async_remote_copy(
            src_ref=got, dst_ref=got, send_sem=send, recv_sem=recv,
            device_id=((down, c), (r, right))[phase], device_id_type=MESH)

    def gathered(own_part, got):
        terms = [(own_part[0:16], own_part[16:32])]
        terms += [(got[n, 0:16], got[n, 16:32]) for n in range(got.shape[0])]
        while len(terms) > 1:
            terms = [added(terms[n], terms[n + 1]) if n + 1 < len(terms) else terms[n]
                     for n in range(0, len(terms), 2)]
        return terms[0]

    sum_copy(0).wait_recv()
    part_b[...] = jnp.concatenate(gathered(part_a, got_a), axis=0)

    @pl.loop(1, N_COL)
    def _(d):
        pltpu.make_async_remote_copy(
            src_ref=part_b, dst_ref=got_b.at[d - 1], send_sem=send_b,
            recv_sem=recv_b, device_id=(r, lax.rem(c + d, N_COL)), device_id_type=MESH).start()

    for s in range(S):
        direct[s][0].wait_recv()
        relayed[s][0].start()
        direct[s][1].wait_recv()
        relayed[s][1].start()

    sum_copy(1).wait_recv()
    total = gathered(part_b, got_b)
    shift = VC // 2
    while shift:
        total = added(total, tuple(pltpu.roll(part, shift, 1) for part in total))
        shift //= 2
    sums[0:16] = total[0]
    sums[16:32] = total[1]
    rho = residual_polynomial([
        (sums[2 * m:2 * m + 2, :], sums[16 + 2 * m:18 + 2 * m, :]) for m in range(MOMENTS)])
    rho = [weight[0] for weight in rho]

    for f in range(4):
        s, k = f // 2, f % 2
        vectors = [krylov[n, f, pl.ds(8, VR), pl.ds(0, VC)] for n in range(ITERS + 1)]
        moved = rho[1][s:s + 1] * vectors[0]
        rest = vectors[0]
        for n in range(1, ITERS + 1):
            rest = rest + rho[n][s:s + 1] * vectors[n]
            if n < ITERS:
                moved = moved + rho[n + 1][s:s + 1] * vectors[n]
        disp_ref[s, k] = moved * (-1.0 / SCALE)
        resid_ref[s, k] = rest

    for copy in told:
        copy.wait_recv()
    note_lane = lax.broadcasted_iota(jnp.int32, (1, VC), 1)
    for s in range(S):
        for i in range(4):
            text = note if i == 0 else notes.at[s, i - 1]
            at = text[0:1, :].astype(jnp.int32)
            at_y, at_z = lax.rem(at, 4), at // 4
            weight = text[4:5, :]
            mine = (at_y == y) | (at_y == flipped(y, GATHER_MASK[s]))
            mine = mine & ((at_z == z) | (at_z == flipped(z, GATHER_MASK[s])))
            mine = mine & (weight > 0.0)
            slot = jnp.where(at_y == y, 0, 1) + jnp.where(at_z == z, 0, 2)
            key = slot * TC + text[1:2, :].astype(jnp.int32)
            code = ((s * 4 + i) * 32 + note_lane - s * TC * K) * 16 + key
            codes_ref[s * 4 + i:s * 4 + i + 1, :] = jnp.where(mine, code, -1)
            shift = rho[1][s:s + 1] * text[8 + 2 * s:10 + 2 * s, :]
            for n in range(1, ITERS):
                shift = shift + rho[n + 1][s:s + 1] * text[8 + 4 * n + 2 * s:10 + 4 * n + 2 * s, :]
            metas_ref[s, i] = jnp.concatenate(
                [text[2:4, :], weight, shift * (-SPACING / SCALE), jnp.zeros((3, VC), F32)], axis=0)

    for copy in told:
        copy.wait_send()
    for copy in halo:
        copy.wait_send()
    for phase in range(2):
        sum_copy(phase).wait_send()
    own.wait()
    for s in range(S):
        direct[s][2].wait_recv()
        direct[s][3].wait_recv()
        for copy in relayed[s]:
            copy.wait()
        for copy in direct[s]:
            copy.wait_send()


def relax(*operands):
    vmem = pl.BlockSpec(memory_space=pltpu.VMEM)
    hbm = pl.BlockSpec(memory_space=pltpu.HBM)
    dma = pltpu.SemaphoreType.DMA
    block = (S, 2, VR, VC)
    operands = [pltpu.with_memory_space_constraint(a, pltpu.HBM) for a in operands]
    return pl.pallas_call(
        relax_kernel,
        out_shape=(
            jax.ShapeDtypeStruct(block, F32),
            jax.ShapeDtypeStruct(block, F32),
            jax.ShapeDtypeStruct((S, 4, 8, VC), F32),
            jax.ShapeDtypeStruct((S * 4, VC), jnp.int32),
            jax.ShapeDtypeStruct((S, 4, TILE, WIDE), BF16),
            jax.ShapeDtypeStruct((S, 4, TILE, WIDE), BF16),
        ),
        in_specs=[hbm] * 10,
        out_specs=(vmem,) * 6,
        scratch_shapes=[
            pltpu.VMEM((10, VR, VC), F32),
            pltpu.VMEM(block, F32),
            pltpu.VMEM(block, jnp.int32),
            pltpu.VMEM((1, ENT_DEV), jnp.int32),
            pltpu.VMEM((1, ENT_DEV), jnp.int32),
            pltpu.VMEM((2, ENT_DEV), jnp.int32),
            pltpu.VMEM((1, ENT_DEV), F32),
            pltpu.VMEM((1, ENT_DEV // K), jnp.int32),
            pltpu.VMEM((2, VR, VC), F32),
            pltpu.VMEM((2, 10, 8, VC), F32),
            pltpu.VMEM((2, VR, VC), F32),
            pltpu.VMEM((4, 8, VC), F32),
            pltpu.VMEM((S, 5, ROWS, COLS), F32),
            pltpu.VMEM((ITERS + 1, 4, ROWS, COLS), F32),
            pltpu.VMEM((32, VC), F32),
            pltpu.VMEM((32, VC), F32),
            pltpu.VMEM((N_ROW - 1, 32, VC), F32),
            pltpu.VMEM((N_COL - 1, 32, VC), F32),
            pltpu.VMEM((NOTE, VC), F32),
            pltpu.VMEM((S, 3, NOTE, VC), F32),
            pltpu.VMEM((32, VC), F32),
            dma((10,)), dma, dma((8,)), dma((8,)),
            dma, dma, dma, dma,
            dma((S, 3)), dma((S, 3)), dma((S, 6)), dma((S, 6)),
        ],
        compiler_params=pltpu.CompilerParams(
            collective_id=0, has_side_effects=True, vmem_limit_bytes=32 * 1024 * 1024),
        name="relax_and_gather",
    )(*operands)


BATCH = 4


def warp_kernel(code_ref, meta_ref, tiles_ref, blank_ref, part_ref, apart, listed):
    count = 0
    for n in range(S * 4):
        def listing(e, total, n=n):
            code = code_ref[n, n // 4 * TC * K + e]
            listed[total] = code
            return total + jnp.where(code >= 0, 1, 0)

        count = lax.fori_loop(0, TC * K, listing, count, unroll=8)
    for n in range(BATCH - 1):
        listed[count + n] = -1

    row = lax.broadcasted_iota(jnp.int32, (TILE, TILE), 0)
    lane = lax.broadcasted_iota(jnp.int32, (TILE, TILE), 1)
    apart[...] = (lane - row).astype(F32).astype(BF16)

    def sampled(shift, side):
        shift = jnp.full((1, TILE), shift, F32)
        low = jnp.floor(shift)
        at_low = jnp.maximum(0.0, 1.0 - jnp.abs(low - shift)).astype(BF16)
        at_high = jnp.maximum(0.0, 1.0 - jnp.abs(low + 1.0 - shift)).astype(BF16)
        low_place = (side * low).astype(BF16)
        high_place = (side * (low + 1.0)).astype(BF16)
        matrix = apart[...]
        return jnp.where(matrix == low_place, at_low, jnp.where(matrix == high_place, at_high, jnp.zeros((), BF16)))

    def entry(n):
        code = listed[n]
        weight_on = jnp.where(code >= 0, 1.0, 0.0)
        code = jnp.maximum(code, 0)
        key = code & 15
        e = (code >> 4) & 31
        place = code >> 9
        s = place >> 2
        i = place & 3
        j = (e * 43) >> 8
        at = s * TC * K + e
        sy = meta_ref[s, i, 0, at] + meta_ref[s, i, 3, 32 * j + 16]
        sx = meta_ref[s, i, 1, at] + meta_ref[s, i, 4, 32 * j + 16]
        source = tiles_ref[s, key >> 2, :, pl.ds(pl.multiple_of((key & 3) * TILE, TILE), TILE)]
        across = jnp.dot(source, sampled(sx, -1.0), preferred_element_type=F32)
        down = jnp.dot(sampled(sy, 1.0), across.astype(BF16), preferred_element_type=F32)
        weight = weight_on * meta_ref[s, i, 2, at]
        return weight * down, (s, i, slice(None), pl.ds(pl.multiple_of(j * TILE, TILE), TILE))

    def batch(b, carry):
        found = [entry(b * BATCH + n) for n in range(BATCH)]
        for value, place in found:
            part_ref[place] = (part_ref[place].astype(F32) + value).astype(BF16)
        return carry

    lax.fori_loop(0, (count + BATCH - 1) // BATCH, batch, 0)


def warp(codes, metas, tiles, blank):
    vmem = pl.BlockSpec(memory_space=pltpu.VMEM)
    smem = pl.BlockSpec(memory_space=pltpu.SMEM)
    return pl.pallas_call(
        warp_kernel,
        out_shape=jax.ShapeDtypeStruct((S, 4, TILE, WIDE), BF16),
        in_specs=[smem, smem, vmem, vmem],
        out_specs=vmem,
        scratch_shapes=[pltpu.VMEM((TILE, TILE), BF16), pltpu.SMEM((256,), jnp.int32)],
        input_output_aliases={3: 0},
        compiler_params=pltpu.CompilerParams(vmem_limit_bytes=32 * 1024 * 1024),
        name="warp_partials",
    )(codes, metas, tiles, blank)


CHUNK = 64
HALVES = 2
SUBS = TILE // CHUNK // HALVES


def scatter_kernel(
    part_ref, zero_ref, one_ref, two_ref,
    relay, onward, got, pool, half, quarter,
    relay_send, relay_recv, direct_send, direct_recv, onward_send, onward_recv,
):
    r = lax.axis_index("row")
    c = lax.axis_index("col")
    y = lax.rem(c, 4)
    z = c // 4
    barrier = pltpu.get_barrier_semaphore()
    for s in range(S):
        for i in (1, 2):
            pl.semaphore_signal(
                barrier, inc=1, device_id=(r, peer_col(y, z, SCATTER_MASK[s], i)), device_id_type=MESH)
    row = lax.broadcasted_iota(jnp.int32, (TILE, VC), 0)
    lane = lax.broadcasted_iota(jnp.int32, (TILE, VC), 1)
    pool[...] = jnp.where(row // 2 == lane, 0.25, 0.0).astype(BF16)
    pl.semaphore_wait(barrier, 2 * S)

    def rows_of(h, u):
        return pl.ds((h * SUBS + u) * CHUNK, CHUNK)

    def copy_to(s, peer, near, far, send, recv):
        return pltpu.make_async_remote_copy(
            src_ref=near, dst_ref=far, send_sem=send, recv_sem=recv,
            device_id=(r, peer_col(y, z, SCATTER_MASK[s], peer)), device_id_type=MESH)

    def to_relay(s, h, u):
        return copy_to(s, h + 1, part_ref.at[s, 3, rows_of(h, u)], relay.at[s, h, u],
                       relay_send.at[s, h, u], relay_recv.at[s, h, u])

    def to_end(s, h, u):
        return copy_to(s, h + 1, part_ref.at[s, h + 1, rows_of(h, u)], got.at[s, h, rows_of(h, u)],
                       direct_send.at[s, h, u], direct_recv.at[s, h, u])

    def to_end_summed(s, h, u):
        other = 1 - h
        return copy_to(s, other + 1, onward.at[s, h, u], got.at[s, other, rows_of(h, u)],
                       onward_send.at[s, h, u], onward_recv.at[s, h, u])

    steps = [(u, h, s) for u in range(SUBS) for h in range(HALVES) for s in range(S)]
    for u, h, s in steps:
        to_relay(s, h, u).start()
    for u, h, s in steps:
        to_end(s, h, u).start()
    for u, h, s in steps:
        to_relay(s, h, u).wait_recv()
        added = relay[s, h, u].astype(F32) + part_ref[s, 2 - h, rows_of(h, u)].astype(F32)
        onward[s, h, u] = added.astype(BF16)
        to_end_summed(s, h, u).start()

    def pooled(block):
        high = block.astype(BF16)
        low = (block - high.astype(F32)).astype(BF16)
        matrix = pool[...]
        return (jnp.dot(high, matrix, preferred_element_type=F32)
                + jnp.dot(low, matrix, preferred_element_type=F32))

    for u, h, s in steps:
        to_end(s, h, u).wait_recv()
        to_end_summed(s, h, u).wait_recv()
        q = h * SUBS + u
        rows = rows_of(h, u)
        for j in range(TC):
            cols = pl.ds(j * TILE, TILE)
            block = part_ref[s, 0, rows, cols].astype(F32)
            for i in range(2):
                block = block + got[s, i, rows, cols].astype(F32)
            zero_ref[s, rows, cols] = block.astype(BF16)
            half[j] = pooled(block)
        ones = []
        for j in range(TC):
            piece = half[j, pl.ds(0, CHUNK // 2, stride=2), :] + half[j, pl.ds(1, CHUNK // 2, stride=2), :]
            one_ref[s, pl.ds(q * (CHUNK // 2), CHUNK // 2), pl.ds(j * VC, VC)] = piece.astype(BF16)
            ones.append(piece)
        for j in range(2):
            quarter[j] = pooled(jnp.concatenate(ones[2 * j:2 * j + 2], axis=1))
            piece = quarter[j, pl.ds(0, CHUNK // 4, stride=2), :] + quarter[j, pl.ds(1, CHUNK // 4, stride=2), :]
            two_ref[s, pl.ds(q * (CHUNK // 4), CHUNK // 4), pl.ds(j * VC, VC)] = piece.astype(BF16)

    for u, h, s in steps:
        to_relay(s, h, u).wait_send()
        to_end(s, h, u).wait_send()
        to_end_summed(s, h, u).wait_send()


def scatter(part):
    vmem = pl.BlockSpec(memory_space=pltpu.VMEM)
    dma = pltpu.SemaphoreType.DMA
    parts = (S, HALVES, SUBS)
    return pl.pallas_call(
        scatter_kernel,
        out_shape=(
            jax.ShapeDtypeStruct((S, TILE, WIDE), BF16),
            jax.ShapeDtypeStruct((S, TILE // 2, WIDE // 2), BF16),
            jax.ShapeDtypeStruct((S, TILE // 4, WIDE // 4), BF16),
        ),
        in_specs=[vmem],
        out_specs=(vmem, vmem, vmem),
        scratch_shapes=[
            pltpu.VMEM(parts + (CHUNK, WIDE), BF16),
            pltpu.VMEM(parts + (CHUNK, WIDE), BF16),
            pltpu.VMEM((S, 2, TILE, WIDE), BF16),
            pltpu.VMEM((TILE, VC), BF16),
            pltpu.VMEM((TC, CHUNK, VC), F32),
            pltpu.VMEM((2, CHUNK // 2, VC), F32),
            dma(parts), dma(parts), dma(parts), dma(parts), dma(parts), dma(parts),
        ],
        compiler_params=pltpu.CompilerParams(
            collective_id=1, has_side_effects=True, vmem_limit_bytes=32 * 1024 * 1024),
        name="scatter_and_pool",
    )(part)


def store_kernel(*refs):
    count = (len(refs) - 1) // 2
    sems = refs[-1]
    copies = [pltpu.make_async_copy(refs[n], refs[count + n], sems.at[n]) for n in range(count)]
    for copy in copies:
        copy.start()
    for copy in copies:
        copy.wait()


def store(*arrays):
    count = len(arrays)
    return pl.pallas_call(
        store_kernel,
        out_shape=tuple(jax.ShapeDtypeStruct(a.shape, a.dtype) for a in arrays),
        in_specs=[pl.BlockSpec(memory_space=pltpu.VMEM)] * count,
        out_specs=(pl.BlockSpec(memory_space=pltpu.HBM),) * count,
        scratch_shapes=[pltpu.SemaphoreType.DMA((count,))],
        compiler_params=pltpu.CompilerParams(vmem_limit_bytes=32 * 1024 * 1024),
        name="store_results",
    )(*arrays)


def shards(load_force, stiffness, cracks, anchor, images, owners, source_tile, offsets, blend_weight, counts):
    flat = [a.reshape(1, -1) for a in (owners, source_tile)]
    displacement, residual, metas, codes, tiles, blank = relax(
        load_force, stiffness, cracks, anchor, *flat, offsets, blend_weight.reshape(1, -1), counts.reshape(1, -1), images)
    part = warp(codes, metas, tiles, blank)
    level_zero, level_one, level_two = scatter(part)
    return store(displacement, residual, level_zero, level_one, level_two)


def solution(mesh):
    flat = P(("row", "col"))
    in_specs = (
        P(None, None, "row", "col"),
        P(None, None, "row", "col"),
        P(None, None, "row", "col"),
        P(None, "row", "col"),
        P(None, "row", "col"),
        P(("row", "col"), None),
        flat,
        P(None, ("row", "col")),
        flat,
        flat,
    )
    out_specs = (
        P(None, None, "row", "col"),
        P(None, None, "row", "col"),
        P(None, "row", "col"),
        P(None, "row", "col"),
        P(None, "row", "col"),
    )
    return jax.shard_map(shards, mesh=mesh, in_specs=in_specs, out_specs=out_specs, check_vma=False)
```

```python
import jax
import jax.numpy as jnp
from jax import lax
from jax.experimental import pallas as pl
from jax.experimental.pallas import tpu as pltpu
from jax.sharding import PartitionSpec as P

S = 2
TILE = 256
SPACING = 8
K = 6
ITERS = 4
TC = 4
ENT_DEV = 48
VR = 32
VC = 128
N_ROW = 8
N_COL = 16
WIDE = TC * TILE
ROWS = VR + 16
COLS = 2 * VC
MESH = pl.DeviceIdType.MESH
F32 = jnp.float32
BF16 = jnp.bfloat16


def flipped(v, mask):
    if mask == 1:
        return v + 1 - 2 * lax.rem(v, 2)
    return 3 - v


def peer_col(y, z, mask, i):
    py = flipped(y, mask) if i % 2 == 1 else y
    pz = flipped(z, mask) if i // 2 == 1 else z
    return pz * 4 + py


GATHER_MASK = (1, 3)
SCATTER_MASK = (3, 1)


NOTE = 24
LIST = 256
MOMENTS = 2 * ITERS
SCALE = 8.0


def two_sum(a, b):
    total = a + b
    part = total - a
    return total, (a - (total - part)) + (b - part)


def renormed(high, low):
    total = high + low
    return total, low - (total - high)


def split(a):
    wide = a * 4097.0
    high = wide - (wide - a)
    return high, a - high


def two_product(a, b, a_parts, b_parts):
    (ah, al), (bh, bl) = a_parts, b_parts
    product = a * b
    return product, ((ah * bh - product) + ah * bl + al * bh) + al * bl


def added(x, y):
    total, rest = two_sum(x[0], y[0])
    return renormed(total, rest + (x[1] + y[1]))


def times(x, y):
    product, rest = two_product(x[0], y[0], split(x[0]), split(y[0]))
    return renormed(product, rest + (x[0] * y[1] + x[1] * y[0]))


def minus(x):
    return -x[0], -x[1]


def over(x, y):
    first = x[0] / y[0]
    nothing = jnp.zeros_like(first)
    rest = added(x, minus(times((first, nothing), y)))
    return renormed(first, rest[0] / y[0])


def residual_polynomial(moment):
    one = (jnp.ones_like(moment[0][0]), jnp.zeros_like(moment[0][0]))
    rho, pi = [one], [one]
    upper = moment[0]
    for k in range(ITERS):
        lower = None
        for j, weight in enumerate(pi):
            term = moment[j + k + 1] if k == 0 else times(weight, moment[j + k + 1])
            lower = term if lower is None else added(lower, term)
        step = over(upper, lower)
        moved = [minus(times(step, weight)) if k else minus(step) for weight in pi]
        rho = [rho[0]] + [added(rho[j], moved[j - 1]) for j in range(1, k + 1)] + [moved[k]]
        if k == ITERS - 1:
            return rho
        upper = moment[k + 1]
        for j in range(1, k + 2):
            upper = added(upper, times(rho[j], moment[j + k + 1]))
        grow = minus(over(upper, lower))
        pi = [added(rho[j], times(grow, pi[j]) if k else grow) for j in range(k + 1)] + [rho[k + 1]]


def relax_kernel(
    load_hbm, stiff_hbm, crack_hbm, anchor_hbm, owner_hbm, source_hbm, offset_hbm, blend_hbm, count_hbm, images_hbm,
    disp_ref, resid_ref, list_ref, tiles_ref, blank_ref,
    fields, stiff, crack, owner, source, offset, blend, count,
    strips, halo_v, halo_h, halo_c, coef, krylov,
    part_a, part_b, got_a, got_b, note, notes, sums,
    load_sem, own_sem, halo_send, halo_recv, send_a, recv_a, send_b, recv_b,
    note_send, note_recv, tile_send, tile_recv,
):
    r = lax.axis_index("row")
    c = lax.axis_index("col")
    y = lax.rem(c, 4)
    z = c // 4
    up, down = lax.rem(r + N_ROW - 1, N_ROW), lax.rem(r + 1, N_ROW)
    left, right = lax.rem(c + N_COL - 1, N_COL), lax.rem(c + 1, N_COL)
    corners = ((up, left), (up, right), (down, left), (down, right))

    barrier = pltpu.get_barrier_semaphore()

    @pl.loop(1, N_ROW)
    def _(d):
        pl.semaphore_signal(barrier, inc=1, device_id=(lax.rem(r + d, N_ROW), c), device_id_type=MESH)

    @pl.loop(1, N_COL)
    def _(d):
        pl.semaphore_signal(barrier, inc=1, device_id=(r, lax.rem(c + d, N_COL)), device_id_type=MESH)

    for corner in corners:
        pl.semaphore_signal(barrier, inc=1, device_id=corner, device_id_type=MESH)

    loads = []
    for n, (near, far) in enumerate((
        (stiff_hbm, stiff), (crack_hbm, crack),
        (load_hbm.at[0], fields.at[pl.ds(0, 2)]), (load_hbm.at[1], fields.at[pl.ds(2, 2)]),
        (anchor_hbm, fields.at[pl.ds(8, 2)]),
        (owner_hbm, owner), (source_hbm, source), (offset_hbm, offset), (blend_hbm, blend), (count_hbm, count),
    )):
        loads.append(pltpu.make_async_copy(near, far, load_sem.at[n]))
    for copy in loads:
        copy.start()
    for copy in loads:
        copy.wait()
    for s in range(S):
        for k in range(2):
            fields[4 + 2 * s + k] = stiff[s, k] * crack[s, k].astype(F32)
    lane = lax.broadcasted_iota(jnp.int32, (VR, VC), 1)
    first = jnp.zeros((VR, VC), F32)
    last = jnp.zeros((VR, VC), F32)
    for f in range(10):
        block = fields[f]
        here = (lane >= 4 * f) & (lane < 4 * f + 4)
        first = jnp.where(here, block if f == 0 else pltpu.roll(block, 4 * f, 1), first)
        last = jnp.where(here, pltpu.roll(block, 4 * f + 4, 1), last)
    strips[0] = first
    strips[1] = last

    pl.semaphore_wait(barrier, N_ROW - 1 + N_COL - 1 + 4)

    halo = []
    for n, (near, far, device) in enumerate((
        (fields.at[:, pl.ds(VR - 8, 8), :], halo_v.at[0], (down, c)),
        (fields.at[:, pl.ds(0, 8), :], halo_v.at[1], (up, c)),
        (strips.at[1], halo_h.at[0], (r, right)),
        (strips.at[0], halo_h.at[1], (r, left)),
        (strips.at[1, pl.ds(VR - 8, 8)], halo_c.at[0], (down, right)),
        (strips.at[0, pl.ds(VR - 8, 8)], halo_c.at[1], (down, left)),
        (strips.at[1, pl.ds(0, 8)], halo_c.at[2], (up, right)),
        (strips.at[0, pl.ds(0, 8)], halo_c.at[3], (up, left)),
    )):
        halo.append(pltpu.make_async_remote_copy(
            src_ref=near, dst_ref=far, send_sem=halo_send.at[n], recv_sem=halo_recv.at[n],
            device_id=device, device_id_type=MESH))
    for copy in halo:
        copy.start()

    half = TILE // 2

    def tile_copy(s, n, slot_from, slot_to, part, peer):
        rows = pl.ds(part * half, half)
        near = images_hbm.at[s, rows] if slot_from == 0 else tiles_ref.at[s, slot_from, rows]
        return pltpu.make_async_remote_copy(
            src_ref=near, dst_ref=tiles_ref.at[s, slot_to, rows],
            send_sem=tile_send.at[s, n], recv_sem=tile_recv.at[s, n],
            device_id=(r, peer_col(y, z, GATHER_MASK[s], peer)), device_id_type=MESH)

    direct = [
        [tile_copy(s, 0, 0, 2, 0, 2), tile_copy(s, 1, 0, 1, 1, 1), tile_copy(s, 2, 0, 1, 0, 1), tile_copy(s, 3, 0, 2, 1, 2)]
        for s in range(S)
    ]
    relayed = [[tile_copy(s, 4, 2, 3, 0, 1), tile_copy(s, 5, 1, 3, 1, 2)] for s in range(S)]
    for n in range(4):
        for s in range(S):
            direct[s][n].start()
    own = pltpu.make_async_copy(images_hbm, tiles_ref.at[:, 0], own_sem)
    own.start()

    entry_lane = lax.broadcasted_iota(jnp.int32, (1, ENT_DEV), 1)
    listed = jnp.zeros((1, ENT_DEV), jnp.int32)
    for t in range(ENT_DEV // K):
        listed = jnp.where(entry_lane // K == t, count[:, t:t + 1], listed)
    note[...] = jnp.zeros((NOTE, VC), F32)
    note[0:1, 0:ENT_DEV] = owner[...].astype(F32)
    note[1:2, 0:ENT_DEV] = source[...].astype(F32)
    note[2:4, 0:ENT_DEV] = offset[...].astype(F32)
    note[4:5, 0:ENT_DEV] = jnp.where(lax.rem(entry_lane, K) < listed, blend[...], 0.0)

    blank_ref[...] = jnp.zeros(blank_ref.shape, BF16)

    for copy in halo:
        copy.wait_recv()

    wide_row = lax.broadcasted_iota(jnp.int32, (ROWS, VC), 0) + r * VR - 8
    wide_lane = lax.broadcasted_iota(jnp.int32, (ROWS, VC), 1)
    side_col = jnp.where(wide_lane < VC // 2, wide_lane + VC, wide_lane - VC) + c * VC
    row_in = (wide_row >= 0) & (wide_row < VR * N_ROW)
    side_in = row_in & (side_col >= 0) & (side_col < VC * N_COL)
    from_left = jnp.concatenate([halo_c[0], halo_h[0], halo_c[2]], axis=0)
    from_right = jnp.concatenate([halo_c[1], halo_h[1], halo_c[3]], axis=0)

    def widened(f):
        center = jnp.concatenate([halo_v[0, f], fields[f], halo_v[1, f]], axis=0)
        to_left = pltpu.roll(from_left, 124 - 4 * f, 1)
        to_right = from_right if f == 0 else pltpu.roll(from_right, VC - 4 * f, 1)
        side = jnp.where(wide_lane < 4, to_right, jnp.where(wide_lane >= 124, to_left, 0.0))
        return jnp.concatenate(
            [jnp.where(row_in, center, 0.0), jnp.where(side_in, side, 0.0)], axis=1)

    inside = jnp.concatenate([row_in.astype(F32), side_in.astype(F32)], axis=1)
    for s in range(S):
        to_right = widened(4 + 2 * s)
        to_low = widened(5 + 2 * s)
        to_left = pltpu.roll(to_right, 1, 1) * inside
        to_high = pltpu.roll(to_low, 1, 0) * inside
        coef[s, 0] = widened(8 + s) + to_right + to_left + to_low + to_high
        coef[s, 1] = to_right
        coef[s, 2] = to_left
        coef[s, 3] = to_low
        coef[s, 4] = to_high
        for k in range(2):
            krylov[0, 2 * s + k] = widened(2 * s + k)

    for n in range(ITERS):
        for f in range(4):
            s = f // 2
            v = krylov[n, f]
            w = coef[s, 0] * v
            w = w - coef[s, 1] * pltpu.roll(v, COLS - 1, 1)
            w = w - coef[s, 2] * pltpu.roll(v, 1, 1)
            w = w - coef[s, 3] * pltpu.roll(v, ROWS - 1, 0)
            w = w - coef[s, 4] * pltpu.roll(v, 1, 0)
            krylov[n + 1, f] = w * (1.0 / SCALE)

    middle = 8 + VR // 2
    for n in range(ITERS):
        for f in range(4):
            note[8 + 4 * n + f:9 + 4 * n + f, :] = krylov[n, f, pl.ds(middle, 1), pl.ds(0, VC)]
    told = []
    for s in range(S):
        for i in (1, 2, 3):
            told.append(pltpu.make_async_remote_copy(
                src_ref=note, dst_ref=notes.at[s, i - 1],
                send_sem=note_send.at[s, i - 1], recv_sem=note_recv.at[s, i - 1],
                device_id=(r, peer_col(y, z, SCATTER_MASK[s], i)), device_id_type=MESH))

    moments = [[None] * S for _ in range(MOMENTS)]
    for s in range(S):
        totals = [None] * MOMENTS
        for f in (2 * s, 2 * s + 1):
            for g in range(VR // 8):
                vectors = [krylov[n, f, pl.ds(8 + 8 * g, 8), pl.ds(0, VC)] for n in range(ITERS + 1)]
                parts = [split(v) for v in vectors]
                for m in range(MOMENTS):
                    a, b = m // 2, m - m // 2
                    product, rest = two_product(vectors[a], vectors[b], parts[a], parts[b])
                    if totals[m] is None:
                        totals[m] = (product, rest)
                    else:
                        total, slip = two_sum(totals[m][0], product)
                        totals[m] = (total, totals[m][1] + (rest + slip))
        for m in range(MOMENTS):
            moments[m][s] = totals[m]

    level = [moments[m][s] for m in range(MOMENTS) for s in range(S)]
    sublane = lax.broadcasted_iota(jnp.int32, (8, VC), 0)
    packed = []
    for base in range(0, len(level), 8):
        group = level[base:base + 8]
        shift = 4
        while shift:
            low = lax.rem(sublane // shift, 2) == 0
            merged = []
            for n in range(shift):
                a, b = group[n], group[n + shift]
                first = tuple(jnp.where(low, u, pltpu.roll(v, shift, 0)) for u, v in zip(a, b))
                second = tuple(jnp.where(low, pltpu.roll(u, 8 - shift, 0), v) for u, v in zip(a, b))
                merged.append(added(first, second))
            group = merged
            shift //= 2
        packed.append(group[0])
    packed = [added(pair, tuple(pltpu.roll(part, VC // 2, 1) for part in pair)) for pair in packed]
    sum_lane = lax.broadcasted_iota(jnp.int32, (8, VC), 1)
    part_a[...] = jnp.concatenate(
        [jnp.where(sum_lane < VC // 2, one, two) for one, two in zip(*packed)], axis=0)

    @pl.loop(1, N_ROW)
    def _(d):
        pltpu.make_async_remote_copy(
            src_ref=part_a, dst_ref=got_a.at[d - 1], send_sem=send_a,
            recv_sem=recv_a, device_id=(lax.rem(r + d, N_ROW), c), device_id_type=MESH).start()

    def sum_copy(phase):
        got, send, recv = ((got_a, send_a, recv_a), (got_b, send_b, recv_b))[phase]
        return pltpu.make_async_remote_copy(
            src_ref=got, dst_ref=got, send_sem=send, recv_sem=recv,
            device_id=((down, c), (r, right))[phase], device_id_type=MESH)

    def gathered(own_part, got):
        terms = [(own_part[0:8], own_part[8:16])]
        terms += [(got[n, 0:8], got[n, 8:16]) for n in range(got.shape[0])]
        while len(terms) > 1:
            terms = [added(terms[n], terms[n + 1]) if n + 1 < len(terms) else terms[n]
                     for n in range(0, len(terms), 2)]
        return terms[0]

    sum_copy(0).wait_recv()
    part_b[...] = jnp.concatenate(gathered(part_a, got_a), axis=0)

    @pl.loop(1, N_COL)
    def _(d):
        pltpu.make_async_remote_copy(
            src_ref=part_b, dst_ref=got_b.at[d - 1], send_sem=send_b,
            recv_sem=recv_b, device_id=(r, lax.rem(c + d, N_COL)), device_id_type=MESH).start()

    for copy in told:
        copy.start()

    for s in range(S):
        direct[s][0].wait_recv()
        relayed[s][0].start()
        direct[s][1].wait_recv()
        relayed[s][1].start()

    sum_copy(1).wait_recv()
    total = gathered(part_b, got_b)
    shift = VC // 4
    while shift:
        inner = lax.rem(sum_lane, VC // 2) < VC // 2 - shift
        total = added(total, tuple(
            jnp.where(inner, pltpu.roll(part, VC - shift, 1), pltpu.roll(part, VC // 2 - shift, 1)) for part in total))
        shift //= 2
    upper_lanes = sum_lane < VC // 2
    spread = [(jnp.where(upper_lanes, part, pltpu.roll(part, VC // 2, 1)),
               jnp.where(upper_lanes, pltpu.roll(part, VC // 2, 1), part)) for part in total]
    total = [jnp.concatenate(pair, axis=0) for pair in spread]
    sums[0:16] = total[0]
    sums[16:32] = total[1]
    rho = residual_polynomial([
        (sums[2 * m:2 * m + 2, :], sums[16 + 2 * m:18 + 2 * m, :]) for m in range(MOMENTS)])
    rho = [weight[0] for weight in rho]

    for f in range(4):
        s, k = f // 2, f % 2
        vectors = [krylov[n, f, pl.ds(8, VR), pl.ds(0, VC)] for n in range(ITERS + 1)]
        moved = rho[1][s:s + 1] * vectors[0]
        rest = vectors[0]
        for n in range(1, ITERS + 1):
            rest = rest + rho[n][s:s + 1] * vectors[n]
            if n < ITERS:
                moved = moved + rho[n + 1][s:s + 1] * vectors[n]
        disp_ref[s, k] = moved * (-1.0 / SCALE)
        resid_ref[s, k] = rest

    for copy in told:
        copy.wait_recv()
    texts = [(s, note if i == 0 else notes.at[s, i - 1]) for s in range(S) for i in range(4)]
    note_lane = lax.broadcasted_iota(jnp.int32, (8, VC), 1)
    note_row = lax.broadcasted_iota(jnp.int32, (8, VC), 0)

    def stacked(n):
        rows = jnp.concatenate([text[n:n + 1, :] for _, text in texts], axis=0)
        return jnp.where(note_row < 4, rows, pltpu.roll(rows, VC - TC * K, 1))

    def shifted(k):
        rows = []
        for s, text in texts:
            row = rho[1][s:s + 1] * text[8 + 2 * s + k:9 + 2 * s + k, :]
            for n in range(1, ITERS):
                row = row + rho[n + 1][s:s + 1] * text[8 + 4 * n + 2 * s + k:9 + 4 * n + 2 * s + k, :]
            rows.append(row)
        rows = jnp.concatenate(rows, axis=0) * (-SPACING / SCALE)
        shift = stacked(2 + k)
        for j in range(TC):
            shift = shift + jnp.where(note_lane // K == j, rows[:, 32 * j + 16:32 * j + 17], 0.0)
        return shift

    owner_col = stacked(0).astype(jnp.int32)
    weight = stacked(4)
    at_y, at_z = lax.rem(owner_col, 4), owner_col // 4
    near = [((at_y == y) | (at_y == flipped(y, m))) & ((at_z == z) | (at_z == flipped(z, m))) for m in GATHER_MASK]
    mine = jnp.where(note_row < 4, near[0].astype(F32), near[1].astype(F32))
    mine = jnp.where((weight > 0.0) & (note_lane < TC * K), mine, 0.0)
    slot = jnp.where(at_y == y, 0, 1) + jnp.where(at_z == z, 0, 2)
    key = slot * TC + stacked(1).astype(jnp.int32)
    code = ((note_row * TC + note_lane // K) * 16 + key).astype(F32)
    rank = mine
    for step in (1, 2, 4, 8, 16):
        rank = rank + jnp.where(note_lane >= step, pltpu.roll(rank, step, 1), 0.0)
    above = jnp.sum(mine, axis=1, keepdims=True) + jnp.zeros((8, VC), F32)
    base = above
    for step in (1, 2, 4):
        base = base + jnp.where(note_row >= step, pltpu.roll(base, step, 0), 0.0)
    total = base[7:8, :]
    rank = jnp.where(mine > 0.0, rank + (base - above) - 1.0, -1.0)
    columns = [jnp.transpose(part)[0:TC * K] for part in (rank, code, shifted(0), shifted(1), weight)]
    place = lax.broadcasted_iota(jnp.int32, (TC * K, LIST), 1).astype(F32)
    listed = [jnp.zeros((1, LIST), F32)] * 4
    for n in range(8):
        chosen = columns[0][:, n:n + 1] == place
        listed = [old + jnp.sum(jnp.where(chosen, column[:, n:n + 1], 0.0), axis=0, keepdims=True)
                  for old, column in zip(listed, columns[1:])]
    list_ref[...] = jnp.concatenate(
        listed + [jnp.concatenate([total] * (LIST // VC), axis=1), jnp.zeros((3, LIST), F32)], axis=0)

    for copy in told:
        copy.wait_send()
    for copy in halo:
        copy.wait_send()
    for phase in range(2):
        sum_copy(phase).wait_send()
    own.wait()
    for s in range(S):
        direct[s][2].wait_recv()
        direct[s][3].wait_recv()
        for copy in relayed[s]:
            copy.wait()
        for copy in direct[s]:
            copy.wait_send()


def relax(*operands):
    vmem = pl.BlockSpec(memory_space=pltpu.VMEM)
    hbm = pl.BlockSpec(memory_space=pltpu.HBM)
    dma = pltpu.SemaphoreType.DMA
    block = (S, 2, VR, VC)
    operands = [pltpu.with_memory_space_constraint(a, pltpu.HBM) for a in operands]
    return pl.pallas_call(
        relax_kernel,
        out_shape=(
            jax.ShapeDtypeStruct(block, F32),
            jax.ShapeDtypeStruct(block, F32),
            jax.ShapeDtypeStruct((8, LIST), F32),
            jax.ShapeDtypeStruct((S, 4, TILE, WIDE), BF16),
            jax.ShapeDtypeStruct((S, 4, TILE, WIDE), BF16),
        ),
        in_specs=[hbm] * 10,
        out_specs=(vmem,) * 5,
        scratch_shapes=[
            pltpu.VMEM((10, VR, VC), F32),
            pltpu.VMEM(block, F32),
            pltpu.VMEM(block, jnp.int32),
            pltpu.VMEM((1, ENT_DEV), jnp.int32),
            pltpu.VMEM((1, ENT_DEV), jnp.int32),
            pltpu.VMEM((2, ENT_DEV), jnp.int32),
            pltpu.VMEM((1, ENT_DEV), F32),
            pltpu.VMEM((1, ENT_DEV // K), jnp.int32),
            pltpu.VMEM((2, VR, VC), F32),
            pltpu.VMEM((2, 10, 8, VC), F32),
            pltpu.VMEM((2, VR, VC), F32),
            pltpu.VMEM((4, 8, VC), F32),
            pltpu.VMEM((S, 5, ROWS, COLS), F32),
            pltpu.VMEM((ITERS + 1, 4, ROWS, COLS), F32),
            pltpu.VMEM((16, VC), F32),
            pltpu.VMEM((16, VC), F32),
            pltpu.VMEM((N_ROW - 1, 16, VC), F32),
            pltpu.VMEM((N_COL - 1, 16, VC), F32),
            pltpu.VMEM((NOTE, VC), F32),
            pltpu.VMEM((S, 3, NOTE, VC), F32),
            pltpu.VMEM((32, VC), F32),
            dma((10,)), dma, dma((8,)), dma((8,)),
            dma, dma, dma, dma,
            dma((S, 3)), dma((S, 3)), dma((S, 6)), dma((S, 6)),
        ],
        compiler_params=pltpu.CompilerParams(
            collective_id=0, has_side_effects=True, vmem_limit_bytes=32 * 1024 * 1024),
        name="relax_and_gather",
    )(*operands)


BATCH = 6


def warp_kernel(list_ref, tiles_ref, blank_ref, part_ref, apart):
    count = list_ref[4, 0].astype(jnp.int32)
    row = lax.broadcasted_iota(jnp.int32, (TILE, TILE), 0)
    lane = lax.broadcasted_iota(jnp.int32, (TILE, TILE), 1)
    apart[...] = (lane - row).astype(F32).astype(BF16)

    def sampled(shift, side):
        shift = jnp.full((1, TILE), shift, F32)
        low = jnp.floor(shift)
        at_low = jnp.maximum(0.0, 1.0 - jnp.abs(low - shift)).astype(BF16)
        at_high = jnp.maximum(0.0, 1.0 - jnp.abs(low + 1.0 - shift)).astype(BF16)
        low_place = (side * low).astype(BF16)
        high_place = (side * (low + 1.0)).astype(BF16)
        matrix = apart[...]
        return jnp.where(matrix == low_place, at_low, jnp.where(matrix == high_place, at_high, jnp.zeros((), BF16)))

    def entry(n):
        code = list_ref[0, n].astype(jnp.int32)
        key = code & 15
        j = (code >> 4) & 3
        place = code >> 6
        s = place >> 2
        source = tiles_ref[s, key >> 2, :, pl.ds(pl.multiple_of((key & 3) * TILE, TILE), TILE)]
        across = jnp.dot(source, sampled(list_ref[2, n], -1.0), preferred_element_type=F32)
        down = jnp.dot(sampled(list_ref[1, n], 1.0), across.astype(BF16), preferred_element_type=F32)
        return list_ref[3, n] * down, (s, place & 3, slice(None), pl.ds(pl.multiple_of(j * TILE, TILE), TILE))

    def batch(b, carry):
        found = [entry(b * BATCH + n) for n in range(BATCH)]
        for value, place in found:
            part_ref[place] = (part_ref[place].astype(F32) + value).astype(BF16)
        return carry

    lax.fori_loop(0, (count + BATCH - 1) // BATCH, batch, 0)


def warp(entries, tiles, blank):
    vmem = pl.BlockSpec(memory_space=pltpu.VMEM)
    smem = pl.BlockSpec(memory_space=pltpu.SMEM)
    return pl.pallas_call(
        warp_kernel,
        out_shape=jax.ShapeDtypeStruct((S, 4, TILE, WIDE), BF16),
        in_specs=[smem, vmem, vmem],
        out_specs=vmem,
        scratch_shapes=[pltpu.VMEM((TILE, TILE), BF16)],
        input_output_aliases={2: 0},
        compiler_params=pltpu.CompilerParams(vmem_limit_bytes=32 * 1024 * 1024),
        name="warp_partials",
    )(entries, tiles, blank)


CHUNK = 64
HALVES = 2
SUBS = TILE // CHUNK // HALVES


def scatter_kernel(
    part_ref, zero_ref, one_ref, two_ref,
    relay, onward, got, pool, half, quarter,
    relay_send, relay_recv, direct_send, direct_recv, onward_send, onward_recv,
):
    r = lax.axis_index("row")
    c = lax.axis_index("col")
    y = lax.rem(c, 4)
    z = c // 4
    barrier = pltpu.get_barrier_semaphore()
    for s in range(S):
        for i in (1, 2):
            pl.semaphore_signal(
                barrier, inc=1, device_id=(r, peer_col(y, z, SCATTER_MASK[s], i)), device_id_type=MESH)
    row = lax.broadcasted_iota(jnp.int32, (TILE, VC), 0)
    lane = lax.broadcasted_iota(jnp.int32, (TILE, VC), 1)
    pool[...] = jnp.where(row // 2 == lane, 0.25, 0.0).astype(BF16)
    pl.semaphore_wait(barrier, 2 * S)

    def rows_of(h, u):
        return pl.ds((h * SUBS + u) * CHUNK, CHUNK)

    def copy_to(s, peer, near, far, send, recv):
        return pltpu.make_async_remote_copy(
            src_ref=near, dst_ref=far, send_sem=send, recv_sem=recv,
            device_id=(r, peer_col(y, z, SCATTER_MASK[s], peer)), device_id_type=MESH)

    def to_relay(s, h, u):
        return copy_to(s, h + 1, part_ref.at[s, 3, rows_of(h, u)], relay.at[s, h, u],
                       relay_send.at[s, h, u], relay_recv.at[s, h, u])

    def to_end(s, h, u):
        return copy_to(s, h + 1, part_ref.at[s, h + 1, rows_of(h, u)], got.at[s, h, rows_of(h, u)],
                       direct_send.at[s, h, u], direct_recv.at[s, h, u])

    def to_end_summed(s, h, u):
        other = 1 - h
        return copy_to(s, other + 1, onward.at[s, h, u], got.at[s, other, rows_of(h, u)],
                       onward_send.at[s, h, u], onward_recv.at[s, h, u])

    steps = [(u, h, s) for u in range(SUBS) for h in range(HALVES) for s in range(S)]
    for u, h, s in steps:
        to_relay(s, h, u).start()
    for u, h, s in steps:
        to_end(s, h, u).start()
    for u, h, s in steps:
        to_relay(s, h, u).wait_recv()
        added = relay[s, h, u].astype(F32) + part_ref[s, 2 - h, rows_of(h, u)].astype(F32)
        onward[s, h, u] = added.astype(BF16)
        to_end_summed(s, h, u).start()

    def pooled(block):
        high = block.astype(BF16)
        low = (block - high.astype(F32)).astype(BF16)
        matrix = pool[...]
        return (jnp.dot(high, matrix, preferred_element_type=F32)
                + jnp.dot(low, matrix, preferred_element_type=F32))

    for u, h, s in steps:
        to_end(s, h, u).wait_recv()
        to_end_summed(s, h, u).wait_recv()
        q = h * SUBS + u
        rows = rows_of(h, u)
        for j in range(TC):
            cols = pl.ds(j * TILE, TILE)
            block = part_ref[s, 0, rows, cols].astype(F32)
            for i in range(2):
                block = block + got[s, i, rows, cols].astype(F32)
            zero_ref[s, rows, cols] = block.astype(BF16)
            half[j] = pooled(block)
        ones = []
        for j in range(TC):
            piece = half[j, pl.ds(0, CHUNK // 2, stride=2), :] + half[j, pl.ds(1, CHUNK // 2, stride=2), :]
            one_ref[s, pl.ds(q * (CHUNK // 2), CHUNK // 2), pl.ds(j * VC, VC)] = piece.astype(BF16)
            ones.append(piece)
        for j in range(2):
            quarter[j] = pooled(jnp.concatenate(ones[2 * j:2 * j + 2], axis=1))
            piece = quarter[j, pl.ds(0, CHUNK // 4, stride=2), :] + quarter[j, pl.ds(1, CHUNK // 4, stride=2), :]
            two_ref[s, pl.ds(q * (CHUNK // 4), CHUNK // 4), pl.ds(j * VC, VC)] = piece.astype(BF16)

    for u, h, s in steps:
        to_relay(s, h, u).wait_send()
        to_end(s, h, u).wait_send()
        to_end_summed(s, h, u).wait_send()


def scatter(part):
    vmem = pl.BlockSpec(memory_space=pltpu.VMEM)
    dma = pltpu.SemaphoreType.DMA
    parts = (S, HALVES, SUBS)
    return pl.pallas_call(
        scatter_kernel,
        out_shape=(
            jax.ShapeDtypeStruct((S, TILE, WIDE), BF16),
            jax.ShapeDtypeStruct((S, TILE // 2, WIDE // 2), BF16),
            jax.ShapeDtypeStruct((S, TILE // 4, WIDE // 4), BF16),
        ),
        in_specs=[vmem],
        out_specs=(vmem, vmem, vmem),
        scratch_shapes=[
            pltpu.VMEM(parts + (CHUNK, WIDE), BF16),
            pltpu.VMEM(parts + (CHUNK, WIDE), BF16),
            pltpu.VMEM((S, 2, TILE, WIDE), BF16),
            pltpu.VMEM((TILE, VC), BF16),
            pltpu.VMEM((TC, CHUNK, VC), F32),
            pltpu.VMEM((2, CHUNK // 2, VC), F32),
            dma(parts), dma(parts), dma(parts), dma(parts), dma(parts), dma(parts),
        ],
        compiler_params=pltpu.CompilerParams(
            collective_id=1, has_side_effects=True, vmem_limit_bytes=32 * 1024 * 1024),
        name="scatter_and_pool",
    )(part)


def store_kernel(*refs):
    count = (len(refs) - 1) // 2
    sems = refs[-1]
    copies = [pltpu.make_async_copy(refs[n], refs[count + n], sems.at[n]) for n in range(count)]
    for copy in copies:
        copy.start()
    for copy in copies:
        copy.wait()


def store(*arrays):
    count = len(arrays)
    return pl.pallas_call(
        store_kernel,
        out_shape=tuple(jax.ShapeDtypeStruct(a.shape, a.dtype) for a in arrays),
        in_specs=[pl.BlockSpec(memory_space=pltpu.VMEM)] * count,
        out_specs=(pl.BlockSpec(memory_space=pltpu.HBM),) * count,
        scratch_shapes=[pltpu.SemaphoreType.DMA((count,))],
        compiler_params=pltpu.CompilerParams(vmem_limit_bytes=32 * 1024 * 1024),
        name="store_results",
    )(*arrays)


def shards(load_force, stiffness, cracks, anchor, images, owners, source_tile, offsets, blend_weight, counts):
    flat = [a.reshape(1, -1) for a in (owners, source_tile)]
    displacement, residual, entries, tiles, blank = relax(
        load_force, stiffness, cracks, anchor, *flat, offsets, blend_weight.reshape(1, -1), counts.reshape(1, -1), images)
    part = warp(entries, tiles, blank)
    level_zero, level_one, level_two = scatter(part)
    return store(displacement, residual, level_zero, level_one, level_two)


def solution(mesh):
    flat = P(("row", "col"))
    in_specs = (
        P(None, None, "row", "col"),
        P(None, None, "row", "col"),
        P(None, None, "row", "col"),
        P(None, "row", "col"),
        P(None, "row", "col"),
        P(("row", "col"), None),
        flat,
        P(None, ("row", "col")),
        flat,
        flat,
    )
    out_specs = (
        P(None, None, "row", "col"),
        P(None, None, "row", "col"),
        P(None, "row", "col"),
        P(None, "row", "col"),
        P(None, "row", "col"),
    )
    return jax.shard_map(shards, mesh=mesh, in_specs=in_specs, out_specs=out_specs, check_vma=False)
```

```python
import jax
import jax.numpy as jnp
from jax import lax
from jax.experimental import pallas as pl
from jax.experimental.pallas import tpu as pltpu
from jax.sharding import PartitionSpec as P

S = 2
TILE = 256
SPACING = 8
K = 6
ITERS = 4
TC = 4
ENT_DEV = 48
VR = 32
VC = 128
VT = 32
N_ROW = 8
N_COL = 16
WIDE = TC * TILE
ROWS = VR + 16
COLS = 2 * VC
MESH = pl.DeviceIdType.MESH
F32 = jnp.float32
BF16 = jnp.bfloat16


def flipped(v, mask):
    if mask == 1:
        return v + 1 - 2 * lax.rem(v, 2)
    return 3 - v


def peer_col(y, z, mask, i):
    py = flipped(y, mask) if i % 2 == 1 else y
    pz = flipped(z, mask) if i // 2 == 1 else z
    return pz * 4 + py


GATHER_MASK = (1, 3)
SCATTER_MASK = (3, 1)


NOTE = 8
LIST = 256
MOMENTS = 2 * ITERS
SCALE = 8.0


def two_sum(a, b):
    total = a + b
    part = total - a
    return total, (a - (total - part)) + (b - part)


def renormed(high, low):
    total = high + low
    return total, low - (total - high)


def split(a):
    wide = a * 4097.0
    high = wide - (wide - a)
    return high, a - high


def two_product(a, b, a_parts, b_parts):
    (ah, al), (bh, bl) = a_parts, b_parts
    product = a * b
    return product, ((ah * bh - product) + ah * bl + al * bh) + al * bl


def added(x, y):
    total, rest = two_sum(x[0], y[0])
    return renormed(total, rest + (x[1] + y[1]))


def times(x, y):
    product, rest = two_product(x[0], y[0], split(x[0]), split(y[0]))
    return renormed(product, rest + (x[0] * y[1] + x[1] * y[0]))


def minus(x):
    return -x[0], -x[1]


def over(x, y):
    first = x[0] / y[0]
    nothing = jnp.zeros_like(first)
    rest = added(x, minus(times((first, nothing), y)))
    return renormed(first, rest[0] / y[0])


def residual_polynomial(moment):
    one = (jnp.ones_like(moment[0][0]), jnp.zeros_like(moment[0][0]))
    rho, pi = [one], [one]
    upper = moment[0]
    for k in range(ITERS):
        lower = None
        for j, weight in enumerate(pi):
            term = moment[j + k + 1] if k == 0 else times(weight, moment[j + k + 1])
            lower = term if lower is None else added(lower, term)
        step = over(upper, lower)
        moved = [minus(times(step, weight)) if k else minus(step) for weight in pi]
        rho = [rho[0]] + [added(rho[j], moved[j - 1]) for j in range(1, k + 1)] + [moved[k]]
        if k == ITERS - 1:
            return rho
        upper = moment[k + 1]
        for j in range(1, k + 2):
            upper = added(upper, times(rho[j], moment[j + k + 1]))
        grow = minus(over(upper, lower))
        pi = [added(rho[j], times(grow, pi[j]) if k else grow) for j in range(k + 1)] + [rho[k + 1]]


def relax_kernel(
    load_hbm, stiff_hbm, crack_hbm, anchor_hbm, owner_hbm, source_hbm, offset_hbm, blend_hbm, count_hbm, images_hbm,
    disp_ref, resid_ref, list_ref, own_ref, place_ref, tiles_ref, blank_ref,
    fields, stiff, crack, owner, source, offset, blend, count,
    strips, halo_v, halo_h, halo_c, coef, krylov,
    part_a, part_b, got_a, got_b, note, notes, sums,
    load_sem, own_sem, halo_send, halo_recv, send_a, recv_a, send_b, recv_b,
    note_send, note_recv, tile_send, tile_recv,
):
    r = lax.axis_index("row")
    c = lax.axis_index("col")
    y = lax.rem(c, 4)
    z = c // 4
    up, down = lax.rem(r + N_ROW - 1, N_ROW), lax.rem(r + 1, N_ROW)
    left, right = lax.rem(c + N_COL - 1, N_COL), lax.rem(c + 1, N_COL)
    corners = ((up, left), (up, right), (down, left), (down, right))

    barrier = pltpu.get_barrier_semaphore()

    @pl.loop(1, N_ROW)
    def _(d):
        pl.semaphore_signal(barrier, inc=1, device_id=(lax.rem(r + d, N_ROW), c), device_id_type=MESH)

    @pl.loop(1, N_COL)
    def _(d):
        pl.semaphore_signal(barrier, inc=1, device_id=(r, lax.rem(c + d, N_COL)), device_id_type=MESH)

    for corner in corners:
        pl.semaphore_signal(barrier, inc=1, device_id=corner, device_id_type=MESH)

    loads = []
    for n, (near, far) in enumerate((
        (stiff_hbm, stiff), (crack_hbm, crack),
        (load_hbm.at[0], fields.at[pl.ds(0, 2)]), (load_hbm.at[1], fields.at[pl.ds(2, 2)]),
        (anchor_hbm, fields.at[pl.ds(8, 2)]),
        (owner_hbm, owner), (source_hbm, source), (offset_hbm, offset), (blend_hbm, blend), (count_hbm, count),
    )):
        loads.append(pltpu.make_async_copy(near, far, load_sem.at[n]))
    for copy in loads:
        copy.start()
    for copy in loads:
        copy.wait()
    for s in range(S):
        for k in range(2):
            fields[4 + 2 * s + k] = stiff[s, k] * crack[s, k].astype(F32)
    lane = lax.broadcasted_iota(jnp.int32, (VR, VC), 1)
    first = jnp.zeros((VR, VC), F32)
    last = jnp.zeros((VR, VC), F32)
    for f in range(10):
        block = fields[f]
        here = (lane >= 4 * f) & (lane < 4 * f + 4)
        first = jnp.where(here, block if f == 0 else pltpu.roll(block, 4 * f, 1), first)
        last = jnp.where(here, pltpu.roll(block, 4 * f + 4, 1), last)
    strips[0] = first
    strips[1] = last

    pl.semaphore_wait(barrier, N_ROW - 1 + N_COL - 1 + 4)

    halo = []
    for n, (near, far, device) in enumerate((
        (fields.at[:, pl.ds(VR - 8, 8), :], halo_v.at[0], (down, c)),
        (fields.at[:, pl.ds(0, 8), :], halo_v.at[1], (up, c)),
        (strips.at[1], halo_h.at[0], (r, right)),
        (strips.at[0], halo_h.at[1], (r, left)),
        (strips.at[1, pl.ds(VR - 8, 8)], halo_c.at[0], (down, right)),
        (strips.at[0, pl.ds(VR - 8, 8)], halo_c.at[1], (down, left)),
        (strips.at[1, pl.ds(0, 8)], halo_c.at[2], (up, right)),
        (strips.at[0, pl.ds(0, 8)], halo_c.at[3], (up, left)),
    )):
        halo.append(pltpu.make_async_remote_copy(
            src_ref=near, dst_ref=far, send_sem=halo_send.at[n], recv_sem=halo_recv.at[n],
            device_id=device, device_id_type=MESH))
    for copy in halo:
        copy.start()

    half = TILE // 2

    def tile_copy(s, n, slot_from, slot_to, part, peer):
        rows = pl.ds(part * half, half)
        near = images_hbm.at[s, rows] if slot_from == 0 else tiles_ref.at[s, slot_from, rows]
        return pltpu.make_async_remote_copy(
            src_ref=near, dst_ref=tiles_ref.at[s, slot_to, rows],
            send_sem=tile_send.at[s, n], recv_sem=tile_recv.at[s, n],
            device_id=(r, peer_col(y, z, GATHER_MASK[s], peer)), device_id_type=MESH)

    direct = [
        [tile_copy(s, 0, 0, 2, 0, 2), tile_copy(s, 1, 0, 1, 1, 1), tile_copy(s, 2, 0, 1, 0, 1), tile_copy(s, 3, 0, 2, 1, 2)]
        for s in range(S)
    ]
    relayed = [[tile_copy(s, 4, 2, 3, 0, 1), tile_copy(s, 5, 1, 3, 1, 2)] for s in range(S)]
    for n in range(4):
        for s in range(S):
            direct[s][n].start()
    own = pltpu.make_async_copy(images_hbm, tiles_ref.at[:, 0], own_sem)
    own.start()

    entry_lane = lax.broadcasted_iota(jnp.int32, (1, ENT_DEV), 1)
    listed = jnp.zeros((1, ENT_DEV), jnp.int32)
    for t in range(ENT_DEV // K):
        listed = jnp.where(entry_lane // K == t, count[:, t:t + 1], listed)
    note[...] = jnp.zeros((NOTE, VC), F32)
    note[0:1, 0:ENT_DEV] = (owner[...] * TC + source[...]).astype(F32)
    note[1:3, 0:ENT_DEV] = offset[...].astype(F32)
    note[3:4, 0:ENT_DEV] = jnp.where(lax.rem(entry_lane, K) < listed, blend[...], 0.0)

    blank_ref[...] = jnp.zeros(blank_ref.shape, BF16)

    for copy in halo:
        copy.wait_recv()

    wide_row = lax.broadcasted_iota(jnp.int32, (ROWS, VC), 0) + r * VR - 8
    wide_lane = lax.broadcasted_iota(jnp.int32, (ROWS, VC), 1)
    side_col = jnp.where(wide_lane < VC // 2, wide_lane + VC, wide_lane - VC) + c * VC
    row_in = (wide_row >= 0) & (wide_row < VR * N_ROW)
    side_in = row_in & (side_col >= 0) & (side_col < VC * N_COL)
    from_left = jnp.concatenate([halo_c[0], halo_h[0], halo_c[2]], axis=0)
    from_right = jnp.concatenate([halo_c[1], halo_h[1], halo_c[3]], axis=0)

    def widened(f):
        center = jnp.concatenate([halo_v[0, f], fields[f], halo_v[1, f]], axis=0)
        to_left = pltpu.roll(from_left, 124 - 4 * f, 1)
        to_right = from_right if f == 0 else pltpu.roll(from_right, VC - 4 * f, 1)
        side = jnp.where(wide_lane < 4, to_right, jnp.where(wide_lane >= 124, to_left, 0.0))
        return jnp.concatenate(
            [jnp.where(row_in, center, 0.0), jnp.where(side_in, side, 0.0)], axis=1)

    inside = jnp.concatenate([row_in.astype(F32), side_in.astype(F32)], axis=1)
    for s in range(S):
        to_right = widened(4 + 2 * s)
        to_low = widened(5 + 2 * s)
        to_left = pltpu.roll(to_right, 1, 1) * inside
        to_high = pltpu.roll(to_low, 1, 0) * inside
        coef[s, 0] = widened(8 + s) + to_right + to_left + to_low + to_high
        coef[s, 1] = to_right
        coef[s, 2] = to_left
        coef[s, 3] = to_low
        coef[s, 4] = to_high
        for k in range(2):
            krylov[0, 2 * s + k] = widened(2 * s + k)

    for n in range(ITERS):
        for f in range(4):
            s = f // 2
            v = krylov[n, f]
            w = coef[s, 0] * v
            w = w - coef[s, 1] * pltpu.roll(v, COLS - 1, 1)
            w = w - coef[s, 2] * pltpu.roll(v, 1, 1)
            w = w - coef[s, 3] * pltpu.roll(v, ROWS - 1, 0)
            w = w - coef[s, 4] * pltpu.roll(v, 1, 0)
            krylov[n + 1, f] = w * (1.0 / SCALE)

    middle = 8 + VR // 2
    point = lax.rem(lax.broadcasted_iota(jnp.int32, (1, VC), 1), VT) - VT // 2
    for f in range(4):
        row = jnp.zeros((1, VC), F32)
        for n in range(ITERS):
            line = krylov[n, f, pl.ds(middle, 1), pl.ds(0, VC)]
            row = jnp.where(point == n, line if n == 0 else pltpu.roll(line, n, 1), row)
        note[4 + f:5 + f, :] = row
    told = []
    for s in range(S):
        for i in (1, 2, 3):
            told.append(pltpu.make_async_remote_copy(
                src_ref=note, dst_ref=notes.at[s, i - 1],
                send_sem=note_send.at[s, i - 1], recv_sem=note_recv.at[s, i - 1],
                device_id=(r, peer_col(y, z, SCATTER_MASK[s], i)), device_id_type=MESH))

    moments = [[None] * S for _ in range(MOMENTS)]
    for s in range(S):
        totals = [None] * MOMENTS
        for f in (2 * s, 2 * s + 1):
            for g in range(VR // 8):
                vectors = [krylov[n, f, pl.ds(8 + 8 * g, 8), pl.ds(0, VC)] for n in range(ITERS + 1)]
                parts = [split(v) for v in vectors]
                for m in range(MOMENTS):
                    a, b = m // 2, m - m // 2
                    product, rest = two_product(vectors[a], vectors[b], parts[a], parts[b])
                    if totals[m] is None:
                        totals[m] = (product, rest)
                    else:
                        total, slip = two_sum(totals[m][0], product)
                        totals[m] = (total, totals[m][1] + (rest + slip))
        for m in range(MOMENTS):
            moments[m][s] = totals[m]

    level = [moments[m][s] for m in range(MOMENTS) for s in range(S)]
    sublane = lax.broadcasted_iota(jnp.int32, (8, VC), 0)
    packed = []
    for base in range(0, len(level), 8):
        group = level[base:base + 8]
        shift = 4
        while shift:
            low = lax.rem(sublane // shift, 2) == 0
            merged = []
            for n in range(shift):
                a, b = group[n], group[n + shift]
                first = tuple(jnp.where(low, u, pltpu.roll(v, shift, 0)) for u, v in zip(a, b))
                second = tuple(jnp.where(low, pltpu.roll(u, 8 - shift, 0), v) for u, v in zip(a, b))
                merged.append(added(first, second))
            group = merged
            shift //= 2
        packed.append(group[0])
    for step in (VC // 2, VC // 4):
        packed = [added(pair, tuple(pltpu.roll(part, step, 1) for part in pair)) for pair in packed]
    sum_lane = lax.broadcasted_iota(jnp.int32, (8, VC), 1)
    quarter = VC // 4

    def joined(one, two):
        return jnp.where(sum_lane < VC // 2, one, two)

    part_a[...] = joined(
        *[jnp.where(lax.rem(sum_lane, VC // 2) < quarter, one, two) for one, two in zip(*packed)])

    @pl.loop(1, N_ROW)
    def _(d):
        pltpu.make_async_remote_copy(
            src_ref=part_a, dst_ref=got_a.at[d - 1], send_sem=send_a,
            recv_sem=recv_a, device_id=(lax.rem(r + d, N_ROW), c), device_id_type=MESH).start()

    def sum_copy(phase):
        got, send, recv = ((got_a, send_a, recv_a), (got_b, send_b, recv_b))[phase]
        return pltpu.make_async_remote_copy(
            src_ref=got, dst_ref=got, send_sem=send, recv_sem=recv,
            device_id=((down, c), (r, right))[phase], device_id_type=MESH)

    def gathered(own_part, got):
        terms = [own_part[...]] + [got[n] for n in range(got.shape[0])]
        terms = [(term, pltpu.roll(term, VC // 2, 1)) for term in terms]
        while len(terms) > 1:
            terms = [added(terms[n], terms[n + 1]) if n + 1 < len(terms) else terms[n]
                     for n in range(0, len(terms), 2)]
        return terms[0]

    sum_copy(0).wait_recv()
    high, low = gathered(part_a, got_a)
    part_b[...] = joined(high, pltpu.roll(low, VC // 2, 1))

    @pl.loop(1, N_COL)
    def _(d):
        pltpu.make_async_remote_copy(
            src_ref=part_b, dst_ref=got_b.at[d - 1], send_sem=send_b,
            recv_sem=recv_b, device_id=(r, lax.rem(c + d, N_COL)), device_id_type=MESH).start()

    for copy in told:
        copy.start()

    for s in range(S):
        direct[s][0].wait_recv()
        relayed[s][0].start()
        direct[s][1].wait_recv()
        relayed[s][1].start()

    sum_copy(1).wait_recv()
    total = gathered(part_b, got_b)
    shift = quarter // 2
    while shift:
        inner = lax.rem(sum_lane, quarter) < quarter - shift
        total = added(total, tuple(
            jnp.where(inner, pltpu.roll(part, VC - shift, 1), pltpu.roll(part, quarter - shift, 1)) for part in total))
        shift //= 2
    odd = lax.rem(sum_lane // quarter, 2) == 1
    spread = []
    for part in total:
        one = jnp.where(odd, pltpu.roll(part, quarter, 1), part)
        two = jnp.where(odd, part, pltpu.roll(part, VC - quarter, 1))
        spread.append(jnp.concatenate([joined(u, pltpu.roll(u, VC // 2, 1)) for u in (one, two)], axis=0))
    total = spread
    sums[0:16] = total[0]
    sums[16:32] = total[1]
    rho = residual_polynomial([
        (sums[2 * m:2 * m + 2, :], sums[16 + 2 * m:18 + 2 * m, :]) for m in range(MOMENTS)])
    rho = [weight[0] for weight in rho]

    for f in range(4):
        s, k = f // 2, f % 2
        vectors = [krylov[n, f, pl.ds(8, VR), pl.ds(0, VC)] for n in range(ITERS + 1)]
        moved = rho[1][s:s + 1] * vectors[0]
        rest = vectors[0]
        for n in range(1, ITERS + 1):
            rest = rest + rho[n][s:s + 1] * vectors[n]
            if n < ITERS:
                moved = moved + rho[n + 1][s:s + 1] * vectors[n]
        disp_ref[s, k] = moved * (-1.0 / SCALE)
        resid_ref[s, k] = rest

    for copy in told:
        copy.wait_recv()
    texts = [(s, note if i == 0 else notes.at[s, i - 1]) for s in range(S) for i in range(4)]
    note_lane = lax.broadcasted_iota(jnp.int32, (8, VC), 1)
    note_row = lax.broadcasted_iota(jnp.int32, (8, VC), 0)

    def stacked(n):
        rows = jnp.concatenate([text[n:n + 1, :] for _, text in texts], axis=0)
        return jnp.where(note_row < 4, rows, pltpu.roll(rows, VC - TC * K, 1))

    note_point = lax.rem(note_lane, VT) - VT // 2
    scales = jnp.zeros((8, VC), F32)
    for n in range(ITERS):
        scale = jnp.where(note_row < 4, rho[n + 1][0:1], rho[n + 1][1:2])
        scales = jnp.where(note_point == n, scale, scales)

    def shifted(k):
        rows = scales * jnp.concatenate([text[4 + 2 * s + k:5 + 2 * s + k, :] for s, text in texts], axis=0)
        rows = rows + pltpu.roll(rows, VC - 1, 1)
        rows = (rows + pltpu.roll(rows, VC - 2, 1)) * (-SPACING / SCALE)
        shift = stacked(1 + k)
        for j in range(TC):
            at = VT * j + VT // 2
            shift = shift + jnp.where(note_lane // K == j, rows[:, at:at + 1], 0.0)
        return shift

    named = stacked(0).astype(jnp.int32)
    owner_col = named // TC
    weight = stacked(3)
    at_y, at_z = lax.rem(owner_col, 4), owner_col // 4
    near = [((at_y == y) | (at_y == flipped(y, m))) & ((at_z == z) | (at_z == flipped(z, m))) for m in GATHER_MASK]
    mine = jnp.where(note_row < 4, near[0].astype(F32), near[1].astype(F32))
    mine = jnp.where((weight > 0.0) & (note_lane < TC * K), mine, 0.0)
    slot = jnp.where(at_y == y, 0, 1) + jnp.where(at_z == z, 0, 2)
    key = slot * TC + lax.rem(named, TC)
    code = ((note_row * TC + note_lane // K) * 16 + key).astype(F32)
    sent = jnp.where(lax.rem(note_row, 4) == 0, 0.0, mine)
    rank = sent
    for step in (1, 2, 4, 8, 16):
        rank = rank + jnp.where(note_lane >= step, pltpu.roll(rank, step, 1), 0.0)
    above = jnp.sum(sent, axis=1, keepdims=True) + jnp.zeros((8, VC), F32)
    base = above
    for step in (1, 2, 4):
        base = base + jnp.where(note_row >= step, pltpu.roll(base, step, 0), 0.0)
    total = base[7:8, :]
    rank = jnp.where(sent > 0.0, rank + (base - above) - 1.0, -1.0)
    shift_y, shift_x = shifted(0), shifted(1)
    columns = [jnp.transpose(part)[0:TC * K] for part in (rank, code, shift_y, shift_x, weight)]
    own_ref[...] = jnp.concatenate(
        [part[4 * s:4 * s + 1] for s in range(S) for part in (weight, shift_y, shift_x, mine * weight)], axis=0)
    place_ref[...] = jnp.concatenate(
        [part[4 * s:4 * s + 1] for s in range(S) for part in (slot, lax.rem(named, TC), slot, slot)], axis=0)
    place = lax.broadcasted_iota(jnp.int32, (TC * K, LIST), 1).astype(F32)
    listed = [jnp.zeros((1, LIST), F32)] * 4
    for n in range(8):
        chosen = columns[0][:, n:n + 1] == place
        listed = [old + jnp.sum(jnp.where(chosen, column[:, n:n + 1], 0.0), axis=0, keepdims=True)
                  for old, column in zip(listed, columns[1:])]
    list_ref[...] = jnp.concatenate(
        listed + [jnp.concatenate([total] * (LIST // VC), axis=1), jnp.zeros((3, LIST), F32)], axis=0)

    for copy in told:
        copy.wait_send()
    for copy in halo:
        copy.wait_send()
    for phase in range(2):
        sum_copy(phase).wait_send()
    own.wait()
    for s in range(S):
        direct[s][2].wait_recv()
        direct[s][3].wait_recv()
        for copy in relayed[s]:
            copy.wait()
        for copy in direct[s]:
            copy.wait_send()


def relax(*operands):
    vmem = pl.BlockSpec(memory_space=pltpu.VMEM)
    hbm = pl.BlockSpec(memory_space=pltpu.HBM)
    dma = pltpu.SemaphoreType.DMA
    block = (S, 2, VR, VC)
    operands = [pltpu.with_memory_space_constraint(a, pltpu.HBM) for a in operands]
    return pl.pallas_call(
        relax_kernel,
        out_shape=(
            jax.ShapeDtypeStruct(block, F32),
            jax.ShapeDtypeStruct(block, F32),
            jax.ShapeDtypeStruct((8, LIST), F32),
            jax.ShapeDtypeStruct((8, VC), F32),
            jax.ShapeDtypeStruct((8, VC), jnp.int32),
            jax.ShapeDtypeStruct((S, 4, TILE, WIDE), BF16),
            jax.ShapeDtypeStruct((S, 3, TILE, WIDE), BF16),
        ),
        in_specs=[hbm] * 10,
        out_specs=(vmem,) * 7,
        scratch_shapes=[
            pltpu.VMEM((10, VR, VC), F32),
            pltpu.VMEM(block, F32),
            pltpu.VMEM(block, jnp.int32),
            pltpu.VMEM((1, ENT_DEV), jnp.int32),
            pltpu.VMEM((1, ENT_DEV), jnp.int32),
            pltpu.VMEM((2, ENT_DEV), jnp.int32),
            pltpu.VMEM((1, ENT_DEV), F32),
            pltpu.VMEM((1, ENT_DEV // K), jnp.int32),
            pltpu.VMEM((2, VR, VC), F32),
            pltpu.VMEM((2, 10, 8, VC), F32),
            pltpu.VMEM((2, VR, VC), F32),
            pltpu.VMEM((4, 8, VC), F32),
            pltpu.VMEM((S, 5, ROWS, COLS), F32),
            pltpu.VMEM((ITERS + 1, 4, ROWS, COLS), F32),
            pltpu.VMEM((8, VC), F32),
            pltpu.VMEM((8, VC), F32),
            pltpu.VMEM((N_ROW - 1, 8, VC), F32),
            pltpu.VMEM((N_COL - 1, 8, VC), F32),
            pltpu.VMEM((NOTE, VC), F32),
            pltpu.VMEM((S, 3, NOTE, VC), F32),
            pltpu.VMEM((32, VC), F32),
            dma((10,)), dma, dma((8,)), dma((8,)),
            dma, dma, dma, dma,
            dma((S, 3)), dma((S, 3)), dma((S, 6)), dma((S, 6)),
        ],
        compiler_params=pltpu.CompilerParams(
            collective_id=0, has_side_effects=True, vmem_limit_bytes=32 * 1024 * 1024),
        name="relax_and_gather",
    )(*operands)


BATCH = 6


def sampled(apart, shift, side):
    shift = jnp.full((1, TILE), shift, F32)
    low = jnp.floor(shift)
    at_low = jnp.maximum(0.0, 1.0 - jnp.abs(low - shift)).astype(BF16)
    at_high = jnp.maximum(0.0, 1.0 - jnp.abs(low + 1.0 - shift)).astype(BF16)
    low_place = (side * low).astype(BF16)
    high_place = (side * (low + 1.0)).astype(BF16)
    matrix = apart[...]
    return jnp.where(matrix == low_place, at_low, jnp.where(matrix == high_place, at_high, jnp.zeros((), BF16)))


def warped_by(source, apart, shift_y, shift_x):
    across = jnp.dot(source, sampled(apart, shift_x, -1.0), preferred_element_type=F32)
    return jnp.dot(sampled(apart, shift_y, 1.0), across.astype(BF16), preferred_element_type=F32)


def columns_apart():
    row = lax.broadcasted_iota(jnp.int32, (TILE, TILE), 0)
    lane = lax.broadcasted_iota(jnp.int32, (TILE, TILE), 1)
    return (lane - row).astype(F32).astype(BF16)


def warp_kernel(list_ref, tiles_ref, blank_ref, part_ref, apart):
    count = list_ref[4, 0].astype(jnp.int32)
    apart[...] = columns_apart()

    def entry(n):
        code = list_ref[0, n].astype(jnp.int32)
        key = code & 15
        j = (code >> 4) & 3
        place = code >> 6
        s = place >> 2
        source = tiles_ref[s, key >> 2, :, pl.ds(pl.multiple_of((key & 3) * TILE, TILE), TILE)]
        value = list_ref[3, n] * warped_by(source, apart, list_ref[1, n], list_ref[2, n])
        return value, (s, jnp.maximum(place & 3, 1) - 1, slice(None), pl.ds(pl.multiple_of(j * TILE, TILE), TILE))

    def batch(b, carry):
        found = [entry(b * BATCH + n) for n in range(BATCH)]
        for value, place in found:
            part_ref[place] = (part_ref[place].astype(F32) + value).astype(BF16)
        return carry

    lax.fori_loop(0, (count + BATCH - 1) // BATCH, batch, 0)


def warp(entries, tiles, blank):
    vmem = pl.BlockSpec(memory_space=pltpu.VMEM)
    smem = pl.BlockSpec(memory_space=pltpu.SMEM)
    return pl.pallas_call(
        warp_kernel,
        out_shape=jax.ShapeDtypeStruct((S, 3, TILE, WIDE), BF16),
        in_specs=[smem, vmem, vmem],
        out_specs=vmem,
        scratch_shapes=[pltpu.VMEM((TILE, TILE), BF16)],
        input_output_aliases={2: 0},
        compiler_params=pltpu.CompilerParams(vmem_limit_bytes=32 * 1024 * 1024),
        name="warp_partials",
    )(entries, tiles, blank)


HALVES = 2
SUBS = ((0, 64), (64, 64))
DEEP = 64


def scatter_kernel(
    listed_ref, placed_ref, tiles_ref, part_ref, zero_ref, one_ref, two_ref,
    own_ref, place_ref, total, apart, relay, onward, got, pool, half, quarter, twos, list_sem,
    relay_send, relay_recv, direct_send, direct_recv, onward_send, onward_recv,
):
    r = lax.axis_index("row")
    c = lax.axis_index("col")
    y = lax.rem(c, 4)
    z = c // 4
    barrier = pltpu.get_barrier_semaphore()
    for s in range(S):
        for i in (1, 2):
            pl.semaphore_signal(
                barrier, inc=1, device_id=(r, peer_col(y, z, SCATTER_MASK[s], i)), device_id_type=MESH)
    listing = [pltpu.make_async_copy(listed_ref, own_ref, list_sem.at[0]),
               pltpu.make_async_copy(placed_ref, place_ref, list_sem.at[1])]
    for copy in listing:
        copy.start()
    row = lax.broadcasted_iota(jnp.int32, (TILE, VC), 0)
    lane = lax.broadcasted_iota(jnp.int32, (TILE, VC), 1)
    pool[...] = jnp.where(row // 2 == lane, 0.25, 0.0).astype(BF16)
    apart[...] = columns_apart()
    pl.semaphore_wait(barrier, 2 * S)

    def rows_of(h, u):
        return pl.ds(h * (TILE // HALVES) + SUBS[u][0], SUBS[u][1])

    def sub_of(u):
        return pl.ds(*SUBS[u])

    def copy_to(s, peer, near, far, send, recv):
        return pltpu.make_async_remote_copy(
            src_ref=near, dst_ref=far, send_sem=send, recv_sem=recv,
            device_id=(r, peer_col(y, z, SCATTER_MASK[s], peer)), device_id_type=MESH)

    def to_relay(s, h, u):
        return copy_to(s, h + 1, part_ref.at[s, 2, rows_of(h, u)], relay.at[s, h, sub_of(u)],
                       relay_send.at[s, h, u], relay_recv.at[s, h, u])

    def to_end(s, h, u):
        return copy_to(s, h + 1, part_ref.at[s, h, rows_of(h, u)], got.at[s, h, rows_of(h, u)],
                       direct_send.at[s, h, u], direct_recv.at[s, h, u])

    def to_end_summed(s, h, u):
        other = 1 - h
        return copy_to(s, other + 1, onward.at[s, h, sub_of(u)], got.at[s, other, rows_of(h, u)],
                       onward_send.at[s, h, u], onward_recv.at[s, h, u])

    steps = [(u, h, s) for u in range(len(SUBS)) for h in range(HALVES) for s in range(S)]
    for u, h, s in steps:
        to_relay(s, h, u).start()
    for u, h, s in steps:
        to_end(s, h, u).start()

    def own_share(s):
        @pl.loop(0, TC)
        def _(j):
            value = None
            for k in range(K):
                e = j * K + k
                tile = place_ref[4 * s + 1, e]
                wide = tiles_ref[s, place_ref[4 * s, e]]
                source = wide[:, 0:TILE]
                for t in range(1, TC):
                    source = jnp.where(tile == t, wide[:, t * TILE:(t + 1) * TILE], source)
                term = own_ref[4 * s + 3, e] * warped_by(source, apart, own_ref[4 * s + 1, e], own_ref[4 * s + 2, e])
                value = term if value is None else value + term
            total[s, :, pl.ds(pl.multiple_of(j * TILE, TILE), TILE)] = value

    for copy in listing:
        copy.wait()
    for u, h, s in steps:
        to_relay(s, h, u).wait_recv()
        added = relay[s, h, sub_of(u)].astype(F32) + part_ref[s, 1 - h, rows_of(h, u)].astype(F32)
        onward[s, h, sub_of(u)] = added.astype(BF16)
        to_end_summed(s, h, u).start()
    own_share(0)
    own_share(1)

    def pooled(block):
        high = block.astype(BF16)
        low = (block - high.astype(F32)).astype(BF16)
        matrix = pool[...]
        return (jnp.dot(high, matrix, preferred_element_type=F32)
                + jnp.dot(low, matrix, preferred_element_type=F32))

    for u, h, s in steps:
        to_end(s, h, u).wait_recv()
        to_end_summed(s, h, u).wait_recv()
        rows = rows_of(h, u)
        start, deep = rows.start, rows.size
        for j in range(TC):
            cols = pl.ds(j * TILE, TILE)
            block = total[s, rows, cols]
            for i in range(2):
                block = block + got[s, i, rows, cols].astype(F32)
            zero_ref[s, rows, cols] = block.astype(BF16)
            half[j, pl.ds(0, deep)] = pooled(block)
        ones = []
        for j in range(TC):
            piece = half[j, pl.ds(0, deep // 2, stride=2), :] + half[j, pl.ds(1, deep // 2, stride=2), :]
            one_ref[s, pl.ds(start // 2, deep // 2), pl.ds(j * VC, VC)] = piece.astype(BF16)
            ones.append(piece)
        for j in range(2):
            quarter[j, pl.ds(0, deep // 2)] = pooled(jnp.concatenate(ones[2 * j:2 * j + 2], axis=1))
            piece = quarter[j, pl.ds(0, deep // 4, stride=2), :] + quarter[j, pl.ds(1, deep // 4, stride=2), :]
            twos[s, pl.ds(start // 4, deep // 4), pl.ds(j * VC, VC)] = piece
    two_ref[...] = twos[...].astype(BF16)

    for u, h, s in steps:
        to_relay(s, h, u).wait_send()
        to_end(s, h, u).wait_send()
        to_end_summed(s, h, u).wait_send()


def scatter(own_list, places, tiles, part):
    vmem = pl.BlockSpec(memory_space=pltpu.VMEM)
    dma = pltpu.SemaphoreType.DMA((S, HALVES, len(SUBS)))
    halved = pltpu.VMEM((S, HALVES, TILE // HALVES, WIDE), BF16)
    return pl.pallas_call(
        scatter_kernel,
        out_shape=(
            jax.ShapeDtypeStruct((S, TILE, WIDE), BF16),
            jax.ShapeDtypeStruct((S, TILE // 2, WIDE // 2), BF16),
            jax.ShapeDtypeStruct((S, TILE // 4, WIDE // 4), BF16),
        ),
        in_specs=[vmem, vmem, vmem, vmem],
        out_specs=(vmem, vmem, vmem),
        scratch_shapes=[
            pltpu.SMEM((8, VC), F32),
            pltpu.SMEM((8, VC), jnp.int32),
            pltpu.VMEM((S, TILE, WIDE), F32),
            pltpu.VMEM((TILE, TILE), BF16),
            halved,
            halved,
            pltpu.VMEM((S, 2, TILE, WIDE), BF16),
            pltpu.VMEM((TILE, VC), BF16),
            pltpu.VMEM((TC, DEEP, VC), F32),
            pltpu.VMEM((2, DEEP // 2, VC), F32),
            pltpu.VMEM((S, TILE // 4, WIDE // 4), F32),
            pltpu.SemaphoreType.DMA((2,)), dma, dma, dma, dma, dma, dma,
        ],
        compiler_params=pltpu.CompilerParams(
            collective_id=1, has_side_effects=True, vmem_limit_bytes=32 * 1024 * 1024),
        name="scatter_and_pool",
    )(own_list, places, tiles, part)


def store_kernel(*refs):
    count = (len(refs) - 1) // 2
    sems = refs[-1]
    copies = [pltpu.make_async_copy(refs[n], refs[count + n], sems.at[n]) for n in range(count)]
    for copy in copies:
        copy.start()
    for copy in copies:
        copy.wait()


def store(*arrays):
    count = len(arrays)
    return pl.pallas_call(
        store_kernel,
        out_shape=tuple(jax.ShapeDtypeStruct(a.shape, a.dtype) for a in arrays),
        in_specs=[pl.BlockSpec(memory_space=pltpu.VMEM)] * count,
        out_specs=(pl.BlockSpec(memory_space=pltpu.HBM),) * count,
        scratch_shapes=[pltpu.SemaphoreType.DMA((count,))],
        compiler_params=pltpu.CompilerParams(vmem_limit_bytes=32 * 1024 * 1024),
        name="store_results",
    )(*arrays)


def shards(load_force, stiffness, cracks, anchor, images, owners, source_tile, offsets, blend_weight, counts):
    flat = [a.reshape(1, -1) for a in (owners, source_tile)]
    displacement, residual, entries, own_list, places, tiles, blank = relax(
        load_force, stiffness, cracks, anchor, *flat, offsets, blend_weight.reshape(1, -1), counts.reshape(1, -1), images)
    part = warp(entries, tiles, blank)
    level_zero, level_one, level_two = scatter(own_list, places, tiles, part)
    return store(displacement, residual, level_zero, level_one, level_two)


def solution(mesh):
    flat = P(("row", "col"))
    in_specs = (
        P(None, None, "row", "col"),
        P(None, None, "row", "col"),
        P(None, None, "row", "col"),
        P(None, "row", "col"),
        P(None, "row", "col"),
        P(("row", "col"), None),
        flat,
        P(None, ("row", "col")),
        flat,
        flat,
    )
    out_specs = (
        P(None, None, "row", "col"),
        P(None, None, "row", "col"),
        P(None, "row", "col"),
        P(None, "row", "col"),
        P(None, "row", "col"),
    )
    return jax.shard_map(shards, mesh=mesh, in_specs=in_specs, out_specs=out_specs, check_vma=False)
```

```python
import functools

import jax
import jax.numpy as jnp
from jax import lax
from jax.experimental import pallas as pl
from jax.experimental.pallas import tpu as pltpu
from jax.sharding import PartitionSpec as P

S = 2
TILE = 256
SPACING = 8
K = 6
ITERS = 4
TC = 4
ENT_DEV = 48
VR = 32
VC = 128
VT = 32
N_ROW = 8
N_COL = 16
WIDE = TC * TILE
ROWS = VR + 16
COLS = 2 * VC
MESH = pl.DeviceIdType.MESH
F32 = jnp.float32
BF16 = jnp.bfloat16


def flipped(v, mask):
    if mask == 1:
        return v + 1 - 2 * lax.rem(v, 2)
    return 3 - v


def peer_col(y, z, mask, i):
    py = flipped(y, mask) if i % 2 == 1 else y
    pz = flipped(z, mask) if i // 2 == 1 else z
    return pz * 4 + py


GATHER_MASK = (1, 3)
SCATTER_MASK = (3, 1)


NOTE = 8
LIST = 256
MOMENTS = 2 * ITERS
SCALE = 8.0


def two_sum(a, b):
    total = a + b
    part = total - a
    return total, (a - (total - part)) + (b - part)


def renormed(high, low):
    total = high + low
    return total, low - (total - high)


def split(a):
    wide = a * 4097.0
    high = wide - (wide - a)
    return high, a - high


def two_product(a, b, a_parts, b_parts):
    (ah, al), (bh, bl) = a_parts, b_parts
    product = a * b
    return product, ((ah * bh - product) + ah * bl + al * bh) + al * bl


def added(x, y):
    total, rest = two_sum(x[0], y[0])
    return renormed(total, rest + (x[1] + y[1]))


def times(x, y):
    product, rest = two_product(x[0], y[0], split(x[0]), split(y[0]))
    return renormed(product, rest + (x[0] * y[1] + x[1] * y[0]))


def minus(x):
    return -x[0], -x[1]


def over(x, y):
    first = x[0] / y[0]
    nothing = jnp.zeros_like(first)
    rest = added(x, minus(times((first, nothing), y)))
    return renormed(first, rest[0] / y[0])


def residual_polynomial(moment):
    one = (jnp.ones_like(moment[0][0]), jnp.zeros_like(moment[0][0]))
    rho, pi = [one], [one]
    upper = moment[0]
    for k in range(ITERS):
        lower = None
        for j, weight in enumerate(pi):
            term = moment[j + k + 1] if k == 0 else times(weight, moment[j + k + 1])
            lower = term if lower is None else added(lower, term)
        step = over(upper, lower)
        moved = [minus(times(step, weight)) if k else minus(step) for weight in pi]
        rho = [rho[0]] + [added(rho[j], moved[j - 1]) for j in range(1, k + 1)] + [moved[k]]
        if k == ITERS - 1:
            return rho
        upper = moment[k + 1]
        for j in range(1, k + 2):
            upper = added(upper, times(rho[j], moment[j + k + 1]))
        grow = minus(over(upper, lower))
        pi = [added(rho[j], times(grow, pi[j]) if k else grow) for j in range(k + 1)] + [rho[k + 1]]


def relax_kernel(
    load_hbm, stiff_hbm, crack_hbm, anchor_hbm, owner_hbm, source_hbm, offset_hbm, blend_hbm, count_hbm, images_hbm,
    disp_ref, resid_ref, list_ref, own_ref, place_ref, tiles_ref, blank_ref,
    fields, stiff, crack, owner, source, offset, blend, count,
    strips, halo_v, halo_h, halo_c, coef, krylov,
    part_a, part_b, got_a, got_b, note, notes, sums,
    load_sem, own_sem, halo_send, halo_recv, send_a, recv_a, send_b, recv_b,
    note_send, note_recv, tile_send, tile_recv,
):
    r = lax.axis_index("row")
    c = lax.axis_index("col")
    y = lax.rem(c, 4)
    z = c // 4
    up, down = lax.rem(r + N_ROW - 1, N_ROW), lax.rem(r + 1, N_ROW)
    left, right = lax.rem(c + N_COL - 1, N_COL), lax.rem(c + 1, N_COL)
    corners = ((up, left), (up, right), (down, left), (down, right))

    barrier = pltpu.get_barrier_semaphore()

    loads = []
    for n, (near, far) in enumerate((
        (stiff_hbm, stiff), (crack_hbm, crack),
        (load_hbm.at[0], fields.at[pl.ds(0, 2)]), (load_hbm.at[1], fields.at[pl.ds(2, 2)]),
        (anchor_hbm, fields.at[pl.ds(8, 2)]),
        (owner_hbm, owner), (source_hbm, source), (offset_hbm, offset), (blend_hbm, blend), (count_hbm, count),
    )):
        loads.append(pltpu.make_async_copy(near, far, load_sem.at[n]))
    for copy in loads:
        copy.start()
    @pl.loop(1, N_ROW)
    def _(d):
        pl.semaphore_signal(barrier, inc=1, device_id=(lax.rem(r + d, N_ROW), c), device_id_type=MESH)

    @pl.loop(1, N_COL)
    def _(d):
        pl.semaphore_signal(barrier, inc=1, device_id=(r, lax.rem(c + d, N_COL)), device_id_type=MESH)

    for corner in corners:
        pl.semaphore_signal(barrier, inc=1, device_id=corner, device_id_type=MESH)

    for copy in loads:
        copy.wait()
    for s in range(S):
        for k in range(2):
            fields[4 + 2 * s + k] = stiff[s, k] * crack[s, k].astype(F32)
    lane = lax.broadcasted_iota(jnp.int32, (VR, VC), 1)
    first = jnp.zeros((VR, VC), F32)
    last = jnp.zeros((VR, VC), F32)
    for f in range(10):
        block = fields[f]
        here = (lane >= 4 * f) & (lane < 4 * f + 4)
        first = jnp.where(here, block if f == 0 else pltpu.roll(block, 4 * f, 1), first)
        last = jnp.where(here, pltpu.roll(block, 4 * f + 4, 1), last)
    strips[0] = first
    strips[1] = last

    pl.semaphore_wait(barrier, N_ROW - 1 + N_COL - 1 + 4)

    halo = []
    for n, (near, far, device) in enumerate((
        (fields.at[:, pl.ds(VR - 8, 8), :], halo_v.at[0], (down, c)),
        (fields.at[:, pl.ds(0, 8), :], halo_v.at[1], (up, c)),
        (strips.at[1], halo_h.at[0], (r, right)),
        (strips.at[0], halo_h.at[1], (r, left)),
        (strips.at[1, pl.ds(VR - 8, 8)], halo_c.at[0], (down, right)),
        (strips.at[0, pl.ds(VR - 8, 8)], halo_c.at[1], (down, left)),
        (strips.at[1, pl.ds(0, 8)], halo_c.at[2], (up, right)),
        (strips.at[0, pl.ds(0, 8)], halo_c.at[3], (up, left)),
    )):
        halo.append(pltpu.make_async_remote_copy(
            src_ref=near, dst_ref=far, send_sem=halo_send.at[n], recv_sem=halo_recv.at[n],
            device_id=device, device_id_type=MESH))
    for copy in halo:
        copy.start()

    half = TILE // 2

    def tile_copy(s, n, slot_from, slot_to, part, peer):
        rows = pl.ds(part * half, half)
        near = images_hbm.at[s, rows] if slot_from == 0 else tiles_ref.at[s, slot_from, rows]
        return pltpu.make_async_remote_copy(
            src_ref=near, dst_ref=tiles_ref.at[s, slot_to, rows],
            send_sem=tile_send.at[s, n], recv_sem=tile_recv.at[s, n],
            device_id=(r, peer_col(y, z, GATHER_MASK[s], peer)), device_id_type=MESH)

    direct = [
        [tile_copy(s, 0, 0, 2, 0, 2), tile_copy(s, 1, 0, 1, 1, 1), tile_copy(s, 2, 0, 1, 0, 1), tile_copy(s, 3, 0, 2, 1, 2)]
        for s in range(S)
    ]
    relayed = [[tile_copy(s, 4, 2, 3, 0, 1), tile_copy(s, 5, 1, 3, 1, 2)] for s in range(S)]
    for n in range(4):
        for s in range(S):
            direct[s][n].start()
    own = pltpu.make_async_copy(images_hbm, tiles_ref.at[:, 0], own_sem)
    own.start()

    entry_lane = lax.broadcasted_iota(jnp.int32, (1, ENT_DEV), 1)
    listed = jnp.zeros((1, ENT_DEV), jnp.int32)
    for t in range(ENT_DEV // K):
        listed = jnp.where(entry_lane // K == t, count[:, t:t + 1], listed)
    note[...] = jnp.zeros((NOTE, VC), F32)
    note[0:1, 0:ENT_DEV] = (owner[...] * TC + source[...]).astype(F32)
    note[1:3, 0:ENT_DEV] = offset[...].astype(F32)
    note[3:4, 0:ENT_DEV] = jnp.where(lax.rem(entry_lane, K) < listed, blend[...], 0.0)

    blank_ref[...] = jnp.zeros(blank_ref.shape, BF16)

    for copy in halo:
        copy.wait_recv()

    wide_row = lax.broadcasted_iota(jnp.int32, (ROWS, VC), 0) + r * VR - 8
    wide_lane = lax.broadcasted_iota(jnp.int32, (ROWS, VC), 1)
    side_col = jnp.where(wide_lane < VC // 2, wide_lane + VC, wide_lane - VC) + c * VC
    row_in = (wide_row >= 0) & (wide_row < VR * N_ROW)
    side_in = row_in & (side_col >= 0) & (side_col < VC * N_COL)
    from_left = jnp.concatenate([halo_c[0], halo_h[0], halo_c[2]], axis=0)
    from_right = jnp.concatenate([halo_c[1], halo_h[1], halo_c[3]], axis=0)

    def widened(f):
        center = jnp.concatenate([halo_v[0, f], fields[f], halo_v[1, f]], axis=0)
        to_left = pltpu.roll(from_left, 124 - 4 * f, 1)
        to_right = from_right if f == 0 else pltpu.roll(from_right, VC - 4 * f, 1)
        side = jnp.where(wide_lane < 4, to_right, jnp.where(wide_lane >= 124, to_left, 0.0))
        return jnp.concatenate(
            [jnp.where(row_in, center, 0.0), jnp.where(side_in, side, 0.0)], axis=1)

    inside = jnp.concatenate([row_in.astype(F32), side_in.astype(F32)], axis=1)
    for s in range(S):
        to_right = widened(4 + 2 * s)
        to_low = widened(5 + 2 * s)
        to_left = pltpu.roll(to_right, 1, 1) * inside
        to_high = pltpu.roll(to_low, 1, 0) * inside
        coef[s, 0] = widened(8 + s) + to_right + to_left + to_low + to_high
        coef[s, 1] = to_right
        coef[s, 2] = to_left
        coef[s, 3] = to_low
        coef[s, 4] = to_high
        for k in range(2):
            krylov[0, 2 * s + k] = widened(2 * s + k)

    for n in range(ITERS):
        for f in range(4):
            s = f // 2
            v = krylov[n, f]
            w = coef[s, 0] * v
            w = w - coef[s, 1] * pltpu.roll(v, COLS - 1, 1)
            w = w - coef[s, 2] * pltpu.roll(v, 1, 1)
            w = w - coef[s, 3] * pltpu.roll(v, ROWS - 1, 0)
            w = w - coef[s, 4] * pltpu.roll(v, 1, 0)
            krylov[n + 1, f] = w * (1.0 / SCALE)

    middle = 8 + VR // 2
    point = lax.rem(lax.broadcasted_iota(jnp.int32, (1, VC), 1), VT) - VT // 2
    for f in range(4):
        row = jnp.zeros((1, VC), F32)
        for n in range(ITERS):
            line = krylov[n, f, pl.ds(middle, 1), pl.ds(0, VC)]
            row = jnp.where(point == n, line if n == 0 else pltpu.roll(line, n, 1), row)
        note[4 + f:5 + f, :] = row
    told = []
    for s in range(S):
        for i in (1, 2, 3):
            told.append(pltpu.make_async_remote_copy(
                src_ref=note, dst_ref=notes.at[s, i - 1],
                send_sem=note_send.at[s, i - 1], recv_sem=note_recv.at[s, i - 1],
                device_id=(r, peer_col(y, z, SCATTER_MASK[s], i)), device_id_type=MESH))

    moments = [[None] * S for _ in range(MOMENTS)]
    for s in range(S):
        totals = [None] * MOMENTS
        for f in (2 * s, 2 * s + 1):
            for g in range(VR // 8):
                vectors = [krylov[n, f, pl.ds(8 + 8 * g, 8), pl.ds(0, VC)] for n in range(ITERS + 1)]
                parts = [split(v) for v in vectors]
                for m in range(MOMENTS):
                    a, b = m // 2, m - m // 2
                    product, rest = two_product(vectors[a], vectors[b], parts[a], parts[b])
                    if totals[m] is None:
                        totals[m] = (product, rest)
                    else:
                        total, slip = two_sum(totals[m][0], product)
                        totals[m] = (total, totals[m][1] + (rest + slip))
        for m in range(MOMENTS):
            moments[m][s] = totals[m]

    level = [moments[m][s] for m in range(MOMENTS) for s in range(S)]
    sublane = lax.broadcasted_iota(jnp.int32, (8, VC), 0)
    packed = []
    for base in range(0, len(level), 8):
        group = level[base:base + 8]
        shift = 4
        while shift:
            low = lax.rem(sublane // shift, 2) == 0
            merged = []
            for n in range(shift):
                a, b = group[n], group[n + shift]
                first = tuple(jnp.where(low, u, pltpu.roll(v, shift, 0)) for u, v in zip(a, b))
                second = tuple(jnp.where(low, pltpu.roll(u, 8 - shift, 0), v) for u, v in zip(a, b))
                merged.append(added(first, second))
            group = merged
            shift //= 2
        packed.append(group[0])
    for step in (VC // 2, VC // 4):
        packed = [added(pair, tuple(pltpu.roll(part, step, 1) for part in pair)) for pair in packed]
    sum_lane = lax.broadcasted_iota(jnp.int32, (8, VC), 1)
    quarter = VC // 4

    def joined(one, two):
        return jnp.where(sum_lane < VC // 2, one, two)

    part_a[...] = joined(
        *[jnp.where(lax.rem(sum_lane, VC // 2) < quarter, one, two) for one, two in zip(*packed)])

    for d in range(1, N_ROW):
        pltpu.make_async_remote_copy(
            src_ref=part_a, dst_ref=got_a.at[d - 1], send_sem=send_a,
            recv_sem=recv_a, device_id=(lax.rem(r + d, N_ROW), c), device_id_type=MESH).start()

    def sum_copy(phase):
        got, send, recv = ((got_a, send_a, recv_a), (got_b, send_b, recv_b))[phase]
        return pltpu.make_async_remote_copy(
            src_ref=got, dst_ref=got, send_sem=send, recv_sem=recv,
            device_id=((down, c), (r, right))[phase], device_id_type=MESH)

    def gathered(own_part, got):
        terms = [own_part[...]] + [got[n] for n in range(got.shape[0])]
        terms = [(term, pltpu.roll(term, VC // 2, 1)) for term in terms]
        while len(terms) > 1:
            terms = [added(terms[n], terms[n + 1]) if n + 1 < len(terms) else terms[n]
                     for n in range(0, len(terms), 2)]
        return terms[0]

    sum_copy(0).wait_recv()
    high, low = gathered(part_a, got_a)
    part_b[...] = joined(high, pltpu.roll(low, VC // 2, 1))

    for d in range(1, N_COL):
        pltpu.make_async_remote_copy(
            src_ref=part_b, dst_ref=got_b.at[d - 1], send_sem=send_b,
            recv_sem=recv_b, device_id=(r, lax.rem(c + d, N_COL)), device_id_type=MESH).start()

    for copy in told:
        copy.start()

    for s in range(S):
        direct[s][0].wait_recv()
        relayed[s][0].start()
        direct[s][1].wait_recv()
        relayed[s][1].start()

    sum_copy(1).wait_recv()
    total = gathered(part_b, got_b)
    shift = quarter // 2
    while shift:
        inner = lax.rem(sum_lane, quarter) < quarter - shift
        total = added(total, tuple(
            jnp.where(inner, pltpu.roll(part, VC - shift, 1), pltpu.roll(part, quarter - shift, 1)) for part in total))
        shift //= 2
    odd = lax.rem(sum_lane // quarter, 2) == 1
    spread = []
    for part in total:
        one = jnp.where(odd, pltpu.roll(part, quarter, 1), part)
        two = jnp.where(odd, part, pltpu.roll(part, VC - quarter, 1))
        spread.append(jnp.concatenate([joined(u, pltpu.roll(u, VC // 2, 1)) for u in (one, two)], axis=0))
    total = spread
    sums[0:16] = total[0]
    sums[16:32] = total[1]
    rho = residual_polynomial([
        (sums[2 * m:2 * m + 2, :], sums[16 + 2 * m:18 + 2 * m, :]) for m in range(MOMENTS)])
    rho = [weight[0] for weight in rho]

    for f in range(4):
        s, k = f // 2, f % 2
        vectors = [krylov[n, f, pl.ds(8, VR), pl.ds(0, VC)] for n in range(ITERS + 1)]
        moved = rho[1][s:s + 1] * vectors[0]
        rest = vectors[0]
        for n in range(1, ITERS + 1):
            rest = rest + rho[n][s:s + 1] * vectors[n]
            if n < ITERS:
                moved = moved + rho[n + 1][s:s + 1] * vectors[n]
        disp_ref[s, k] = moved * (-1.0 / SCALE)
        resid_ref[s, k] = rest

    for copy in told:
        copy.wait_recv()
    texts = [(s, note if i == 0 else notes.at[s, i - 1]) for s in range(S) for i in range(4)]
    note_lane = lax.broadcasted_iota(jnp.int32, (8, VC), 1)
    note_row = lax.broadcasted_iota(jnp.int32, (8, VC), 0)

    def stacked(n):
        rows = jnp.concatenate([text[n:n + 1, :] for _, text in texts], axis=0)
        return jnp.where(note_row < 4, rows, pltpu.roll(rows, VC - TC * K, 1))

    note_point = lax.rem(note_lane, VT) - VT // 2
    scales = jnp.zeros((8, VC), F32)
    for n in range(ITERS):
        scale = jnp.where(note_row < 4, rho[n + 1][0:1], rho[n + 1][1:2])
        scales = jnp.where(note_point == n, scale, scales)

    def shifted(k):
        rows = scales * jnp.concatenate([text[4 + 2 * s + k:5 + 2 * s + k, :] for s, text in texts], axis=0)
        rows = rows + pltpu.roll(rows, VC - 1, 1)
        rows = (rows + pltpu.roll(rows, VC - 2, 1)) * (-SPACING / SCALE)
        shift = stacked(1 + k)
        for j in range(TC):
            at = VT * j + VT // 2
            shift = shift + jnp.where(note_lane // K == j, rows[:, at:at + 1], 0.0)
        return shift

    named = stacked(0).astype(jnp.int32)
    owner_col = named // TC
    weight = stacked(3)
    at_y, at_z = lax.rem(owner_col, 4), owner_col // 4
    near = [((at_y == y) | (at_y == flipped(y, m))) & ((at_z == z) | (at_z == flipped(z, m))) for m in GATHER_MASK]
    mine = jnp.where(note_row < 4, near[0].astype(F32), near[1].astype(F32))
    mine = jnp.where((weight > 0.0) & (note_lane < TC * K), mine, 0.0)
    slot = jnp.where(at_y == y, 0, 1) + jnp.where(at_z == z, 0, 2)
    key = slot * TC + lax.rem(named, TC)
    code = ((note_row * TC + note_lane // K) * 16 + key).astype(F32)
    sent = jnp.where(lax.rem(note_row, 4) < 2, 0.0, mine)
    rank = sent
    for step in (1, 2, 4, 8, 16):
        rank = rank + jnp.where(note_lane >= step, pltpu.roll(rank, step, 1), 0.0)
    above = jnp.sum(sent, axis=1, keepdims=True) + jnp.zeros((8, VC), F32)
    base = above
    for step in (1, 2, 4):
        base = base + jnp.where(note_row >= step, pltpu.roll(base, step, 0), 0.0)
    total = base[7:8, :]
    rank = jnp.where(sent > 0.0, rank + (base - above) - 1.0, -1.0)
    shift_y, shift_x = shifted(0), shifted(1)
    columns = [jnp.transpose(part)[0:TC * K] for part in (rank, code, shift_y, shift_x, weight)]
    own_ref[...] = jnp.concatenate(
        [part[4 * s + i:4 * s + i + 1] for s in range(S) for i in range(2)
         for part in (weight, shift_y, shift_x, mine * weight)], axis=0)
    place_ref[...] = jnp.concatenate(
        [part[4 * s + i:4 * s + i + 1] for s in range(S) for i in range(2)
         for part in (slot, lax.rem(named, TC), slot, slot)], axis=0)
    place = lax.broadcasted_iota(jnp.int32, (TC * K, LIST), 1).astype(F32)
    listed = [jnp.zeros((1, LIST), F32)] * 4
    for n in range(8):
        chosen = columns[0][:, n:n + 1] == place
        listed = [old + jnp.sum(jnp.where(chosen, column[:, n:n + 1], 0.0), axis=0, keepdims=True)
                  for old, column in zip(listed, columns[1:])]
    list_ref[...] = jnp.concatenate(
        listed + [jnp.concatenate([total] * (LIST // VC), axis=1), jnp.zeros((3, LIST), F32)], axis=0)

    for copy in told:
        copy.wait_send()
    for copy in halo:
        copy.wait_send()
    for phase in range(2):
        sum_copy(phase).wait_send()
    own.wait()
    for s in range(S):
        direct[s][2].wait_recv()
        direct[s][3].wait_recv()
        for copy in relayed[s]:
            copy.wait()
        for copy in direct[s]:
            copy.wait_send()


def relax(*operands):
    vmem = pl.BlockSpec(memory_space=pltpu.VMEM)
    hbm = pl.BlockSpec(memory_space=pltpu.HBM)
    dma = pltpu.SemaphoreType.DMA
    block = (S, 2, VR, VC)
    operands = [pltpu.with_memory_space_constraint(a, pltpu.HBM) for a in operands]
    return pl.pallas_call(
        relax_kernel,
        out_shape=(
            jax.ShapeDtypeStruct(block, F32),
            jax.ShapeDtypeStruct(block, F32),
            jax.ShapeDtypeStruct((8, LIST), F32),
            jax.ShapeDtypeStruct((16, VC), F32),
            jax.ShapeDtypeStruct((16, VC), jnp.int32),
            jax.ShapeDtypeStruct((S, 4, TILE, WIDE), BF16),
            jax.ShapeDtypeStruct((S, 2, TILE, WIDE), BF16),
        ),
        in_specs=[hbm] * 10,
        out_specs=(vmem,) * 7,
        scratch_shapes=[
            pltpu.VMEM((10, VR, VC), F32),
            pltpu.VMEM(block, F32),
            pltpu.VMEM(block, jnp.int32),
            pltpu.VMEM((1, ENT_DEV), jnp.int32),
            pltpu.VMEM((1, ENT_DEV), jnp.int32),
            pltpu.VMEM((2, ENT_DEV), jnp.int32),
            pltpu.VMEM((1, ENT_DEV), F32),
            pltpu.VMEM((1, ENT_DEV // K), jnp.int32),
            pltpu.VMEM((2, VR, VC), F32),
            pltpu.VMEM((2, 10, 8, VC), F32),
            pltpu.VMEM((2, VR, VC), F32),
            pltpu.VMEM((4, 8, VC), F32),
            pltpu.VMEM((S, 5, ROWS, COLS), F32),
            pltpu.VMEM((ITERS + 1, 4, ROWS, COLS), F32),
            pltpu.VMEM((8, VC), F32),
            pltpu.VMEM((8, VC), F32),
            pltpu.VMEM((N_ROW - 1, 8, VC), F32),
            pltpu.VMEM((N_COL - 1, 8, VC), F32),
            pltpu.VMEM((NOTE, VC), F32),
            pltpu.VMEM((S, 3, NOTE, VC), F32),
            pltpu.VMEM((32, VC), F32),
            dma((10,)), dma, dma((8,)), dma((8,)),
            dma, dma, dma, dma,
            dma((S, 3)), dma((S, 3)), dma((S, 6)), dma((S, 6)),
        ],
        compiler_params=pltpu.CompilerParams(
            collective_id=0, has_side_effects=True, vmem_limit_bytes=32 * 1024 * 1024),
        name="relax_and_gather",
    )(*operands)


BATCH = 8


def sampled(apart, shift, side):
    shift = jnp.full((1, TILE), shift, F32)
    low = jnp.floor(shift)
    at_low = jnp.maximum(0.0, 1.0 - jnp.abs(low - shift)).astype(BF16)
    at_high = jnp.maximum(0.0, 1.0 - jnp.abs(low + 1.0 - shift)).astype(BF16)
    low_place = (side * low).astype(BF16)
    high_place = (side * (low + 1.0)).astype(BF16)
    matrix = apart[...]
    return jnp.where(matrix == low_place, at_low, jnp.where(matrix == high_place, at_high, jnp.zeros((), BF16)))


def warped_by(source, apart, shift_y, shift_x):
    across = jnp.dot(source, sampled(apart, shift_x, -1.0), preferred_element_type=F32)
    return jnp.dot(sampled(apart, shift_y, 1.0), across.astype(BF16), preferred_element_type=F32)


def columns_apart():
    row = lax.broadcasted_iota(jnp.int32, (TILE, TILE), 0)
    lane = lax.broadcasted_iota(jnp.int32, (TILE, TILE), 1)
    return (lane - row).astype(F32).astype(BF16)


def warp_kernel(list_ref, tiles_ref, blank_ref, part_ref, apart):
    count = list_ref[4, 0].astype(jnp.int32)
    apart[...] = columns_apart()

    def entry(n):
        code = list_ref[0, n].astype(jnp.int32)
        key = code & 15
        j = (code >> 4) & 3
        place = code >> 6
        s = place >> 2
        source = tiles_ref[s, key >> 2, :, pl.ds(pl.multiple_of((key & 3) * TILE, TILE), TILE)]
        value = list_ref[3, n] * warped_by(source, apart, list_ref[1, n], list_ref[2, n])
        return value, (s, jnp.maximum(place & 3, 2) - 2, slice(None), pl.ds(pl.multiple_of(j * TILE, TILE), TILE))

    def batch(b, carry):
        found = [entry(b * BATCH + n) for n in range(BATCH)]
        for value, place in found:
            part_ref[place] = (part_ref[place].astype(F32) + value).astype(BF16)
        return carry

    lax.fori_loop(0, (count + BATCH - 1) // BATCH, batch, 0)


def warp(entries, tiles, blank):
    vmem = pl.BlockSpec(memory_space=pltpu.VMEM)
    smem = pl.BlockSpec(memory_space=pltpu.SMEM)
    return pl.pallas_call(
        warp_kernel,
        out_shape=jax.ShapeDtypeStruct((S, 2, TILE, WIDE), BF16),
        in_specs=[smem, vmem, vmem],
        out_specs=vmem,
        scratch_shapes=[pltpu.VMEM((TILE, TILE), BF16)],
        input_output_aliases={2: 0},
        compiler_params=pltpu.CompilerParams(vmem_limit_bytes=32 * 1024 * 1024),
        name="warp_partials",
    )(entries, tiles, blank)


HALVES = 2
SUBS = ((0, 64), (64, 64))
DEEP = 64


def scatter_kernel(
    listed_ref, placed_ref, tiles_ref, part_ref, zero_ref, one_ref, two_ref,
    own_ref, place_ref, nearer, total, apart, relay, onward, got, pool, half, quarter, twos, list_sem,
    relay_send, relay_recv, direct_send, direct_recv, onward_send, onward_recv,
):
    r = lax.axis_index("row")
    c = lax.axis_index("col")
    y = lax.rem(c, 4)
    z = c // 4
    barrier = pltpu.get_barrier_semaphore()
    for s in range(S):
        for i in (1, 2):
            pl.semaphore_signal(
                barrier, inc=1, device_id=(r, peer_col(y, z, SCATTER_MASK[s], i)), device_id_type=MESH)
    listing = [pltpu.make_async_copy(listed_ref, own_ref, list_sem.at[0]),
               pltpu.make_async_copy(placed_ref, place_ref, list_sem.at[1])]
    for copy in listing:
        copy.start()
    row = lax.broadcasted_iota(jnp.int32, (TILE, VC), 0)
    lane = lax.broadcasted_iota(jnp.int32, (TILE, VC), 1)
    pool[...] = jnp.where(row // 2 == lane, 0.25, 0.0).astype(BF16)
    apart[...] = columns_apart()
    pl.semaphore_wait(barrier, 2 * S)

    def rows_of(h, u):
        return pl.ds(h * (TILE // HALVES) + SUBS[u][0], SUBS[u][1])

    def sub_of(u):
        return pl.ds(*SUBS[u])

    def copy_to(s, peer, near, far, send, recv):
        return pltpu.make_async_remote_copy(
            src_ref=near, dst_ref=far, send_sem=send, recv_sem=recv,
            device_id=(r, peer_col(y, z, SCATTER_MASK[s], peer)), device_id_type=MESH)

    def to_relay(s, h, u):
        return copy_to(s, h + 1, part_ref.at[s, 1, rows_of(h, u)], relay.at[s, h, sub_of(u)],
                       relay_send.at[s, h, u], relay_recv.at[s, h, u])

    def to_end(s, h, u):
        near = nearer.at[s] if h == 0 else part_ref.at[s, 0]
        return copy_to(s, h + 1, near.at[rows_of(h, u)], got.at[s, h, rows_of(h, u)],
                       direct_send.at[s, h, u], direct_recv.at[s, h, u])

    def to_end_summed(s, h, u):
        other = 1 - h
        return copy_to(s, other + 1, onward.at[s, h, sub_of(u)], got.at[s, other, rows_of(h, u)],
                       onward_send.at[s, h, u], onward_recv.at[s, h, u])

    steps = [(u, h, s) for u in range(len(SUBS)) for h in range(HALVES) for s in range(S)]
    for u, h, s in steps:
        to_relay(s, h, u).start()
    for u, h, s in steps:
        if h == 1:
            to_end(s, h, u).start()

    def share(s, i, put):
        @pl.loop(0, TC)
        def _(j):
            value = None
            base = 4 * (2 * s + i)
            for k in range(K):
                e = j * K + k
                tile = place_ref[base + 1, e]
                wide = tiles_ref[s, place_ref[base, e]]
                source = wide[:, 0:TILE]
                for t in range(1, TC):
                    source = jnp.where(tile == t, wide[:, t * TILE:(t + 1) * TILE], source)
                term = own_ref[base + 3, e] * warped_by(source, apart, own_ref[base + 1, e], own_ref[base + 2, e])
                value = term if value is None else value + term
            put(value, pl.ds(pl.multiple_of(j * TILE, TILE), TILE))

    def put_near(s, value, cols):
        nearer[s, :, cols] = value.astype(BF16)

    def put_own(s, value, cols):
        total[s, :, cols] = value

    for copy in listing:
        copy.wait()
    for s in range(S):
        share(s, 1, functools.partial(put_near, s))
        for u in range(len(SUBS)):
            to_end(s, 0, u).start()
    for u, h, s in steps:
        to_relay(s, h, u).wait_recv()
        ours = part_ref[s, 0, rows_of(h, u)] if h == 0 else nearer[s, rows_of(h, u)]
        summed = relay[s, h, sub_of(u)].astype(F32) + ours.astype(F32)
        onward[s, h, sub_of(u)] = summed.astype(BF16)
        to_end_summed(s, h, u).start()
    for s in range(S):
        share(s, 0, functools.partial(put_own, s))

    def pooled(block):
        high = block.astype(BF16)
        low = (block - high.astype(F32)).astype(BF16)
        matrix = pool[...]
        return (jnp.dot(high, matrix, preferred_element_type=F32)
                + jnp.dot(low, matrix, preferred_element_type=F32))

    for u, h, s in steps:
        to_end(s, h, u).wait_recv()
        rows = rows_of(h, u)
        total[s, rows] = total[s, rows] + got[s, h, rows].astype(F32)

    for u, h, s in steps:
        to_end_summed(s, h, u).wait_recv()
        rows = rows_of(h, u)
        start, deep = rows.start, rows.size
        for j in range(TC):
            cols = pl.ds(j * TILE, TILE)
            block = total[s, rows, cols] + got[s, 1 - h, rows, cols].astype(F32)
            zero_ref[s, rows, cols] = block.astype(BF16)
            half[j, pl.ds(0, deep)] = pooled(block)
        ones = []
        for j in range(TC):
            piece = half[j, pl.ds(0, deep // 2, stride=2), :] + half[j, pl.ds(1, deep // 2, stride=2), :]
            one_ref[s, pl.ds(start // 2, deep // 2), pl.ds(j * VC, VC)] = piece.astype(BF16)
            ones.append(piece)
        for j in range(2):
            quarter[j, pl.ds(0, deep // 2)] = pooled(jnp.concatenate(ones[2 * j:2 * j + 2], axis=1))
            piece = quarter[j, pl.ds(0, deep // 4, stride=2), :] + quarter[j, pl.ds(1, deep // 4, stride=2), :]
            twos[s, pl.ds(start // 4, deep // 4), pl.ds(j * VC, VC)] = piece
    two_ref[...] = twos[...].astype(BF16)

    for u, h, s in steps:
        to_relay(s, h, u).wait_send()
        to_end(s, h, u).wait_send()
        to_end_summed(s, h, u).wait_send()


def scatter(own_list, places, tiles, part):
    vmem = pl.BlockSpec(memory_space=pltpu.VMEM)
    dma = pltpu.SemaphoreType.DMA((S, HALVES, len(SUBS)))
    halved = pltpu.VMEM((S, HALVES, TILE // HALVES, WIDE), BF16)
    return pl.pallas_call(
        scatter_kernel,
        out_shape=(
            jax.ShapeDtypeStruct((S, TILE, WIDE), BF16),
            jax.ShapeDtypeStruct((S, TILE // 2, WIDE // 2), BF16),
            jax.ShapeDtypeStruct((S, TILE // 4, WIDE // 4), BF16),
        ),
        in_specs=[vmem, vmem, vmem, vmem],
        out_specs=(vmem, vmem, vmem),
        scratch_shapes=[
            pltpu.SMEM((16, VC), F32),
            pltpu.SMEM((16, VC), jnp.int32),
            pltpu.VMEM((S, TILE, WIDE), BF16),
            pltpu.VMEM((S, TILE, WIDE), F32),
            pltpu.VMEM((TILE, TILE), BF16),
            halved,
            halved,
            pltpu.VMEM((S, 2, TILE, WIDE), BF16),
            pltpu.VMEM((TILE, VC), BF16),
            pltpu.VMEM((TC, DEEP, VC), F32),
            pltpu.VMEM((2, DEEP // 2, VC), F32),
            pltpu.VMEM((S, TILE // 4, WIDE // 4), F32),
            pltpu.SemaphoreType.DMA((2,)), dma, dma, dma, dma, dma, dma,
        ],
        compiler_params=pltpu.CompilerParams(
            collective_id=1, has_side_effects=True, vmem_limit_bytes=32 * 1024 * 1024),
        name="scatter_and_pool",
    )(own_list, places, tiles, part)


STORES = 8


def store_kernel(*refs):
    count = (len(refs) - 1) // 2
    sems = refs[-1]
    copies = []
    for n in range(count):
        near, far = refs[n], refs[count + n]
        pieces = STORES if n == 2 else 1
        rows = near.shape[1] // pieces
        for p in range(pieces):
            span = pl.ds(p * rows, rows)
            copies.append(pltpu.make_async_copy(near.at[:, span], far.at[:, span], sems.at[len(copies)]))
    for copy in copies:
        copy.start()
    for copy in copies:
        copy.wait()


def store(*arrays):
    count = len(arrays)
    return pl.pallas_call(
        store_kernel,
        out_shape=tuple(jax.ShapeDtypeStruct(a.shape, a.dtype) for a in arrays),
        in_specs=[pl.BlockSpec(memory_space=pltpu.VMEM)] * count,
        out_specs=(pl.BlockSpec(memory_space=pltpu.HBM),) * count,
        scratch_shapes=[pltpu.SemaphoreType.DMA((count + STORES - 1,))],
        compiler_params=pltpu.CompilerParams(vmem_limit_bytes=32 * 1024 * 1024),
        name="store_results",
    )(*arrays)


def shards(load_force, stiffness, cracks, anchor, images, owners, source_tile, offsets, blend_weight, counts):
    flat = [a.reshape(1, -1) for a in (owners, source_tile)]
    displacement, residual, entries, own_list, places, tiles, blank = relax(
        load_force, stiffness, cracks, anchor, *flat, offsets, blend_weight.reshape(1, -1), counts.reshape(1, -1), images)
    part = warp(entries, tiles, blank)
    level_zero, level_one, level_two = scatter(own_list, places, tiles, part)
    return store(displacement, residual, level_zero, level_one, level_two)


def solution(mesh):
    flat = P(("row", "col"))
    in_specs = (
        P(None, None, "row", "col"),
        P(None, None, "row", "col"),
        P(None, None, "row", "col"),
        P(None, "row", "col"),
        P(None, "row", "col"),
        P(("row", "col"), None),
        flat,
        P(None, ("row", "col")),
        flat,
        flat,
    )
    out_specs = (
        P(None, None, "row", "col"),
        P(None, None, "row", "col"),
        P(None, "row", "col"),
        P(None, "row", "col"),
        P(None, "row", "col"),
    )
    return jax.shard_map(shards, mesh=mesh, in_specs=in_specs, out_specs=out_specs, check_vma=False)
```

```python
import functools

import jax
import jax.numpy as jnp
from jax import lax
from jax.experimental import pallas as pl
from jax.experimental.pallas import tpu as pltpu
from jax.sharding import PartitionSpec as P

S = 2
TILE = 256
SPACING = 8
K = 6
ITERS = 4
TC = 4
ENT_DEV = 48
VR = 32
VC = 128
VT = 32
N_ROW = 8
N_COL = 16
WIDE = TC * TILE
ROWS = VR + 16
COLS = 2 * VC
MESH = pl.DeviceIdType.MESH
F32 = jnp.float32
BF16 = jnp.bfloat16


def flipped(v, mask):
    if mask == 1:
        return v + 1 - 2 * lax.rem(v, 2)
    return 3 - v


def peer_col(y, z, mask, i):
    py = flipped(y, mask) if i % 2 == 1 else y
    pz = flipped(z, mask) if i // 2 == 1 else z
    return pz * 4 + py


GATHER_MASK = (1, 3)
SCATTER_MASK = (3, 1)


NOTE = 8
LIST = 256
MOMENTS = 2 * ITERS
SCALE = 8.0


def two_sum(a, b):
    total = a + b
    part = total - a
    return total, (a - (total - part)) + (b - part)


def renormed(high, low):
    total = high + low
    return total, low - (total - high)


def split(a):
    wide = a * 4097.0
    high = wide - (wide - a)
    return high, a - high


def two_product(a, b, a_parts, b_parts):
    (ah, al), (bh, bl) = a_parts, b_parts
    product = a * b
    return product, ((ah * bh - product) + ah * bl + al * bh) + al * bl


def added(x, y):
    total, rest = two_sum(x[0], y[0])
    return renormed(total, rest + (x[1] + y[1]))


def times(x, y):
    product, rest = two_product(x[0], y[0], split(x[0]), split(y[0]))
    return renormed(product, rest + (x[0] * y[1] + x[1] * y[0]))


def minus(x):
    return -x[0], -x[1]


def over(x, y):
    first = x[0] / y[0]
    nothing = jnp.zeros_like(first)
    rest = added(x, minus(times((first, nothing), y)))
    return renormed(first, rest[0] / y[0])


def residual_polynomial(moment):
    one = (jnp.ones_like(moment[0][0]), jnp.zeros_like(moment[0][0]))
    rho, pi = [one], [one]
    upper = moment[0]
    for k in range(ITERS):
        lower = None
        for j, weight in enumerate(pi):
            term = moment[j + k + 1] if k == 0 else times(weight, moment[j + k + 1])
            lower = term if lower is None else added(lower, term)
        step = over(upper, lower)
        moved = [minus(times(step, weight)) if k else minus(step) for weight in pi]
        rho = [rho[0]] + [added(rho[j], moved[j - 1]) for j in range(1, k + 1)] + [moved[k]]
        if k == ITERS - 1:
            return rho
        upper = moment[k + 1]
        for j in range(1, k + 2):
            upper = added(upper, times(rho[j], moment[j + k + 1]))
        grow = minus(over(upper, lower))
        pi = [added(rho[j], times(grow, pi[j]) if k else grow) for j in range(k + 1)] + [rho[k + 1]]


def relax_kernel(
    load_hbm, stiff_hbm, crack_hbm, anchor_hbm, owner_hbm, source_hbm, offset_hbm, blend_hbm, count_hbm, images_hbm,
    disp_ref, resid_ref, list_ref, own_ref, place_ref, tiles_ref, blank_ref,
    fields, stiff, crack, owner, source, offset, blend, count,
    strips, halo_v, halo_h, halo_c, coef, krylov,
    part_a, part_b, got_a, got_b, note, notes, sums,
    load_sem, own_sem, halo_send, halo_recv, send_a, recv_a, send_b, recv_b,
    note_send, note_recv, tile_send, tile_recv,
):
    r = lax.axis_index("row")
    c = lax.axis_index("col")
    y = lax.rem(c, 4)
    z = c // 4
    up, down = lax.rem(r + N_ROW - 1, N_ROW), lax.rem(r + 1, N_ROW)
    left, right = lax.rem(c + N_COL - 1, N_COL), lax.rem(c + 1, N_COL)
    corners = ((up, left), (up, right), (down, left), (down, right))

    barrier = pltpu.get_barrier_semaphore()

    loads = []
    for n, (near, far) in enumerate((
        (stiff_hbm, stiff), (crack_hbm, crack),
        (load_hbm.at[0], fields.at[pl.ds(0, 2)]), (load_hbm.at[1], fields.at[pl.ds(2, 2)]),
        (anchor_hbm, fields.at[pl.ds(8, 2)]),
        (owner_hbm, owner), (source_hbm, source), (offset_hbm, offset), (blend_hbm, blend), (count_hbm, count),
    )):
        loads.append(pltpu.make_async_copy(near, far, load_sem.at[n]))
    for copy in loads:
        copy.start()
    for corner in corners:
        pl.semaphore_signal(barrier, inc=1, device_id=corner, device_id_type=MESH)
    for d in range(1, N_COL):
        pl.semaphore_signal(barrier, inc=1, device_id=(r, lax.rem(c + d, N_COL)), device_id_type=MESH)
    for d in range(1, N_ROW):
        pl.semaphore_signal(barrier, inc=1, device_id=(lax.rem(r + d, N_ROW), c), device_id_type=MESH)

    for copy in loads:
        copy.wait()
    for s in range(S):
        for k in range(2):
            fields[4 + 2 * s + k] = stiff[s, k] * crack[s, k].astype(F32)
    lane = lax.broadcasted_iota(jnp.int32, (VR, VC), 1)
    first = jnp.zeros((VR, VC), F32)
    last = jnp.zeros((VR, VC), F32)
    for f in range(10):
        block = fields[f]
        here = (lane >= 4 * f) & (lane < 4 * f + 4)
        first = jnp.where(here, block if f == 0 else pltpu.roll(block, 4 * f, 1), first)
        last = jnp.where(here, pltpu.roll(block, 4 * f + 4, 1), last)
    strips[0] = first
    strips[1] = last

    pl.semaphore_wait(barrier, N_ROW - 1 + N_COL - 1 + 4)

    halo = []
    for n, (near, far, device) in enumerate((
        (fields.at[:, pl.ds(VR - 8, 8), :], halo_v.at[0], (down, c)),
        (fields.at[:, pl.ds(0, 8), :], halo_v.at[1], (up, c)),
        (strips.at[1], halo_h.at[0], (r, right)),
        (strips.at[0], halo_h.at[1], (r, left)),
        (strips.at[1, pl.ds(VR - 8, 8)], halo_c.at[0], (down, right)),
        (strips.at[0, pl.ds(VR - 8, 8)], halo_c.at[1], (down, left)),
        (strips.at[1, pl.ds(0, 8)], halo_c.at[2], (up, right)),
        (strips.at[0, pl.ds(0, 8)], halo_c.at[3], (up, left)),
    )):
        halo.append(pltpu.make_async_remote_copy(
            src_ref=near, dst_ref=far, send_sem=halo_send.at[n], recv_sem=halo_recv.at[n],
            device_id=device, device_id_type=MESH))
    for copy in halo:
        copy.start()

    half = TILE // 2

    def tile_copy(s, n, slot_from, slot_to, part, peer):
        rows = pl.ds(part * half, half)
        near = images_hbm.at[s, rows] if slot_from == 0 else tiles_ref.at[s, slot_from, rows]
        return pltpu.make_async_remote_copy(
            src_ref=near, dst_ref=tiles_ref.at[s, slot_to, rows],
            send_sem=tile_send.at[s, n], recv_sem=tile_recv.at[s, n],
            device_id=(r, peer_col(y, z, GATHER_MASK[s], peer)), device_id_type=MESH)

    direct = [
        [tile_copy(s, 0, 0, 2, 0, 2), tile_copy(s, 1, 0, 1, 1, 1), tile_copy(s, 2, 0, 1, 0, 1), tile_copy(s, 3, 0, 2, 1, 2)]
        for s in range(S)
    ]
    relayed = [[tile_copy(s, 4, 2, 3, 0, 1), tile_copy(s, 5, 1, 3, 1, 2)] for s in range(S)]
    for n in range(4):
        for s in range(S):
            direct[s][n].start()
    own = pltpu.make_async_copy(images_hbm, tiles_ref.at[:, 0], own_sem)
    own.start()

    entry_lane = lax.broadcasted_iota(jnp.int32, (1, ENT_DEV), 1)
    listed = jnp.zeros((1, ENT_DEV), jnp.int32)
    for t in range(ENT_DEV // K):
        listed = jnp.where(entry_lane // K == t, count[:, t:t + 1], listed)
    note[...] = jnp.zeros((NOTE, VC), F32)
    note[0:1, 0:ENT_DEV] = (owner[...] * TC + source[...]).astype(F32)
    note[1:3, 0:ENT_DEV] = offset[...].astype(F32)
    note[3:4, 0:ENT_DEV] = jnp.where(lax.rem(entry_lane, K) < listed, blend[...], 0.0)

    blank_ref[...] = jnp.zeros(blank_ref.shape, BF16)

    for copy in halo:
        copy.wait_recv()

    wide_row = lax.broadcasted_iota(jnp.int32, (ROWS, VC), 0) + r * VR - 8
    wide_lane = lax.broadcasted_iota(jnp.int32, (ROWS, VC), 1)
    side_col = jnp.where(wide_lane < VC // 2, wide_lane + VC, wide_lane - VC) + c * VC
    row_in = (wide_row >= 0) & (wide_row < VR * N_ROW)
    side_in = row_in & (side_col >= 0) & (side_col < VC * N_COL)
    from_left = jnp.concatenate([halo_c[0], halo_h[0], halo_c[2]], axis=0)
    from_right = jnp.concatenate([halo_c[1], halo_h[1], halo_c[3]], axis=0)

    def widened(f):
        center = jnp.concatenate([halo_v[0, f], fields[f], halo_v[1, f]], axis=0)
        to_left = pltpu.roll(from_left, 124 - 4 * f, 1)
        to_right = from_right if f == 0 else pltpu.roll(from_right, VC - 4 * f, 1)
        side = jnp.where(wide_lane < 4, to_right, jnp.where(wide_lane >= 124, to_left, 0.0))
        return jnp.concatenate(
            [jnp.where(row_in, center, 0.0), jnp.where(side_in, side, 0.0)], axis=1)

    inside = jnp.concatenate([row_in.astype(F32), side_in.astype(F32)], axis=1)
    for s in range(S):
        to_right = widened(4 + 2 * s)
        to_low = widened(5 + 2 * s)
        to_left = pltpu.roll(to_right, 1, 1) * inside
        to_high = pltpu.roll(to_low, 1, 0) * inside
        coef[s, 0] = widened(8 + s) + to_right + to_left + to_low + to_high
        coef[s, 1] = to_right
        coef[s, 2] = to_left
        coef[s, 3] = to_low
        coef[s, 4] = to_high
        for k in range(2):
            krylov[0, 2 * s + k] = widened(2 * s + k)

    for n in range(ITERS):
        for f in range(4):
            s = f // 2
            v = krylov[n, f]
            w = coef[s, 0] * v
            w = w - coef[s, 1] * pltpu.roll(v, COLS - 1, 1)
            w = w - coef[s, 2] * pltpu.roll(v, 1, 1)
            w = w - coef[s, 3] * pltpu.roll(v, ROWS - 1, 0)
            w = w - coef[s, 4] * pltpu.roll(v, 1, 0)
            krylov[n + 1, f] = w * (1.0 / SCALE)

    middle = 8 + VR // 2
    point = lax.rem(lax.broadcasted_iota(jnp.int32, (1, VC), 1), VT) - VT // 2
    for f in range(4):
        row = jnp.zeros((1, VC), F32)
        for n in range(ITERS):
            line = krylov[n, f, pl.ds(middle, 1), pl.ds(0, VC)]
            row = jnp.where(point == n, line if n == 0 else pltpu.roll(line, n, 1), row)
        note[4 + f:5 + f, :] = row
    told = []
    for s in range(S):
        for i in (1, 2, 3):
            told.append(pltpu.make_async_remote_copy(
                src_ref=note, dst_ref=notes.at[s, i - 1],
                send_sem=note_send.at[s, i - 1], recv_sem=note_recv.at[s, i - 1],
                device_id=(r, peer_col(y, z, SCATTER_MASK[s], i)), device_id_type=MESH))

    moments = [[None] * S for _ in range(MOMENTS)]
    for s in range(S):
        totals = [None] * MOMENTS
        for f in (2 * s, 2 * s + 1):
            for g in range(VR // 8):
                vectors = [krylov[n, f, pl.ds(8 + 8 * g, 8), pl.ds(0, VC)] for n in range(ITERS + 1)]
                parts = [split(v) for v in vectors]
                for m in range(MOMENTS):
                    a, b = m // 2, m - m // 2
                    product, rest = two_product(vectors[a], vectors[b], parts[a], parts[b])
                    if totals[m] is None:
                        totals[m] = (product, rest)
                    else:
                        total, slip = two_sum(totals[m][0], product)
                        totals[m] = (total, totals[m][1] + (rest + slip))
        for m in range(MOMENTS):
            moments[m][s] = totals[m]

    level = [moments[m][s] for m in range(MOMENTS) for s in range(S)]
    sublane = lax.broadcasted_iota(jnp.int32, (8, VC), 0)
    packed = []
    for base in range(0, len(level), 8):
        group = level[base:base + 8]
        shift = 4
        while shift:
            low = lax.rem(sublane // shift, 2) == 0
            merged = []
            for n in range(shift):
                a, b = group[n], group[n + shift]
                first = tuple(jnp.where(low, u, pltpu.roll(v, shift, 0)) for u, v in zip(a, b))
                second = tuple(jnp.where(low, pltpu.roll(u, 8 - shift, 0), v) for u, v in zip(a, b))
                merged.append(added(first, second))
            group = merged
            shift //= 2
        packed.append(group[0])
    for step in (VC // 2, VC // 4):
        packed = [added(pair, tuple(pltpu.roll(part, step, 1) for part in pair)) for pair in packed]
    sum_lane = lax.broadcasted_iota(jnp.int32, (8, VC), 1)
    quarter = VC // 4

    def joined(one, two):
        return jnp.where(sum_lane < VC // 2, one, two)

    part_a[...] = joined(
        *[jnp.where(lax.rem(sum_lane, VC // 2) < quarter, one, two) for one, two in zip(*packed)])

    for d in range(1, N_ROW):
        pltpu.make_async_remote_copy(
            src_ref=part_a, dst_ref=got_a.at[d - 1], send_sem=send_a,
            recv_sem=recv_a, device_id=(lax.rem(r + d, N_ROW), c), device_id_type=MESH).start()

    def sum_copy(phase):
        got, send, recv = ((got_a, send_a, recv_a), (got_b, send_b, recv_b))[phase]
        return pltpu.make_async_remote_copy(
            src_ref=got, dst_ref=got, send_sem=send, recv_sem=recv,
            device_id=((down, c), (r, right))[phase], device_id_type=MESH)

    def gathered(own_part, got):
        terms = [own_part[...]] + [got[n] for n in range(got.shape[0])]
        terms = [(term, pltpu.roll(term, VC // 2, 1)) for term in terms]
        while len(terms) > 1:
            terms = [added(terms[n], terms[n + 1]) if n + 1 < len(terms) else terms[n]
                     for n in range(0, len(terms), 2)]
        return terms[0]

    sum_copy(0).wait_recv()
    high, low = gathered(part_a, got_a)
    part_b[...] = joined(high, pltpu.roll(low, VC // 2, 1))

    for d in range(1, N_COL):
        pltpu.make_async_remote_copy(
            src_ref=part_b, dst_ref=got_b.at[d - 1], send_sem=send_b,
            recv_sem=recv_b, device_id=(r, lax.rem(c + d, N_COL)), device_id_type=MESH).start()

    for copy in told:
        copy.start()

    for s in range(S):
        direct[s][0].wait_recv()
        relayed[s][0].start()
        direct[s][1].wait_recv()
        relayed[s][1].start()

    sum_copy(1).wait_recv()
    total = gathered(part_b, got_b)
    shift = quarter // 2
    while shift:
        inner = lax.rem(sum_lane, quarter) < quarter - shift
        total = added(total, tuple(
            jnp.where(inner, pltpu.roll(part, VC - shift, 1), pltpu.roll(part, quarter - shift, 1)) for part in total))
        shift //= 2
    odd = lax.rem(sum_lane // quarter, 2) == 1
    spread = []
    for part in total:
        one = jnp.where(odd, pltpu.roll(part, quarter, 1), part)
        two = jnp.where(odd, part, pltpu.roll(part, VC - quarter, 1))
        spread.append(jnp.concatenate([joined(u, pltpu.roll(u, VC // 2, 1)) for u in (one, two)], axis=0))
    total = spread
    sums[0:16] = total[0]
    sums[16:32] = total[1]
    rho = residual_polynomial([
        (sums[2 * m:2 * m + 2, :], sums[16 + 2 * m:18 + 2 * m, :]) for m in range(MOMENTS)])
    rho = [weight[0] for weight in rho]

    for f in range(4):
        s, k = f // 2, f % 2
        vectors = [krylov[n, f, pl.ds(8, VR), pl.ds(0, VC)] for n in range(ITERS + 1)]
        moved = rho[1][s:s + 1] * vectors[0]
        rest = vectors[0]
        for n in range(1, ITERS + 1):
            rest = rest + rho[n][s:s + 1] * vectors[n]
            if n < ITERS:
                moved = moved + rho[n + 1][s:s + 1] * vectors[n]
        disp_ref[s, k] = moved * (-1.0 / SCALE)
        resid_ref[s, k] = rest

    for copy in told:
        copy.wait_recv()
    texts = [(s, note if i == 0 else notes.at[s, i - 1]) for s in range(S) for i in range(4)]
    note_lane = lax.broadcasted_iota(jnp.int32, (8, VC), 1)
    note_row = lax.broadcasted_iota(jnp.int32, (8, VC), 0)

    def stacked(n):
        rows = jnp.concatenate([text[n:n + 1, :] for _, text in texts], axis=0)
        return jnp.where(note_row < 4, rows, pltpu.roll(rows, VC - TC * K, 1))

    note_point = lax.rem(note_lane, VT) - VT // 2
    scales = jnp.zeros((8, VC), F32)
    for n in range(ITERS):
        scale = jnp.where(note_row < 4, rho[n + 1][0:1], rho[n + 1][1:2])
        scales = jnp.where(note_point == n, scale, scales)

    def shifted(k):
        rows = scales * jnp.concatenate([text[4 + 2 * s + k:5 + 2 * s + k, :] for s, text in texts], axis=0)
        rows = rows + pltpu.roll(rows, VC - 1, 1)
        rows = (rows + pltpu.roll(rows, VC - 2, 1)) * (-SPACING / SCALE)
        shift = stacked(1 + k)
        for j in range(TC):
            at = VT * j + VT // 2
            shift = shift + jnp.where(note_lane // K == j, rows[:, at:at + 1], 0.0)
        return shift

    named = stacked(0).astype(jnp.int32)
    owner_col = named // TC
    weight = stacked(3)
    at_y, at_z = lax.rem(owner_col, 4), owner_col // 4
    near = [((at_y == y) | (at_y == flipped(y, m))) & ((at_z == z) | (at_z == flipped(z, m))) for m in GATHER_MASK]
    mine = jnp.where(note_row < 4, near[0].astype(F32), near[1].astype(F32))
    mine = jnp.where((weight > 0.0) & (note_lane < TC * K), mine, 0.0)
    slot = jnp.where(at_y == y, 0, 1) + jnp.where(at_z == z, 0, 2)
    key = slot * TC + lax.rem(named, TC)
    code = ((note_row * TC + note_lane // K) * 16 + key).astype(F32)
    sent = jnp.where(lax.rem(note_row, 4) < 2, 0.0, mine)
    rank = sent
    for step in (1, 2, 4, 8, 16):
        rank = rank + jnp.where(note_lane >= step, pltpu.roll(rank, step, 1), 0.0)
    above = jnp.sum(sent, axis=1, keepdims=True) + jnp.zeros((8, VC), F32)
    base = above
    for step in (1, 2, 4):
        base = base + jnp.where(note_row >= step, pltpu.roll(base, step, 0), 0.0)
    total = base[7:8, :]
    rank = jnp.where(sent > 0.0, rank + (base - above) - 1.0, -1.0)
    shift_y, shift_x = shifted(0), shifted(1)
    columns = [jnp.transpose(part)[0:TC * K] for part in (rank, code, shift_y, shift_x, weight)]
    own_ref[...] = jnp.concatenate(
        [part[4 * s + i:4 * s + i + 1] for s in range(S) for i in range(2)
         for part in (weight, shift_y, shift_x, mine * weight)], axis=0)
    place_ref[...] = jnp.concatenate(
        [part[4 * s + i:4 * s + i + 1] for s in range(S) for i in range(2)
         for part in (slot, lax.rem(named, TC), slot, slot)], axis=0)
    place = lax.broadcasted_iota(jnp.int32, (TC * K, LIST), 1).astype(F32)
    listed = [jnp.zeros((1, LIST), F32)] * 4
    for n in range(8):
        chosen = columns[0][:, n:n + 1] == place
        listed = [old + jnp.sum(jnp.where(chosen, column[:, n:n + 1], 0.0), axis=0, keepdims=True)
                  for old, column in zip(listed, columns[1:])]
    list_ref[...] = jnp.concatenate(
        listed + [jnp.concatenate([total] * (LIST // VC), axis=1), jnp.zeros((3, LIST), F32)], axis=0)

    for copy in told:
        copy.wait_send()
    for copy in halo:
        copy.wait_send()
    for phase in range(2):
        sum_copy(phase).wait_send()
    own.wait()
    for s in range(S):
        direct[s][2].wait_recv()
        direct[s][3].wait_recv()
        for copy in relayed[s]:
            copy.wait()
        for copy in direct[s]:
            copy.wait_send()


def relax(*operands):
    vmem = pl.BlockSpec(memory_space=pltpu.VMEM)
    hbm = pl.BlockSpec(memory_space=pltpu.HBM)
    dma = pltpu.SemaphoreType.DMA
    block = (S, 2, VR, VC)
    operands = [pltpu.with_memory_space_constraint(a, pltpu.HBM) for a in operands]
    return pl.pallas_call(
        relax_kernel,
        out_shape=(
            jax.ShapeDtypeStruct(block, F32),
            jax.ShapeDtypeStruct(block, F32),
            jax.ShapeDtypeStruct((8, LIST), F32),
            jax.ShapeDtypeStruct((16, VC), F32),
            jax.ShapeDtypeStruct((16, VC), jnp.int32),
            jax.ShapeDtypeStruct((S, 4, TILE, WIDE), BF16),
            jax.ShapeDtypeStruct((S, 2, TILE, WIDE), BF16),
        ),
        in_specs=[hbm] * 10,
        out_specs=(vmem,) * 7,
        scratch_shapes=[
            pltpu.VMEM((10, VR, VC), F32),
            pltpu.VMEM(block, F32),
            pltpu.VMEM(block, jnp.int32),
            pltpu.VMEM((1, ENT_DEV), jnp.int32),
            pltpu.VMEM((1, ENT_DEV), jnp.int32),
            pltpu.VMEM((2, ENT_DEV), jnp.int32),
            pltpu.VMEM((1, ENT_DEV), F32),
            pltpu.VMEM((1, ENT_DEV // K), jnp.int32),
            pltpu.VMEM((2, VR, VC), F32),
            pltpu.VMEM((2, 10, 8, VC), F32),
            pltpu.VMEM((2, VR, VC), F32),
            pltpu.VMEM((4, 8, VC), F32),
            pltpu.VMEM((S, 5, ROWS, COLS), F32),
            pltpu.VMEM((ITERS + 1, 4, ROWS, COLS), F32),
            pltpu.VMEM((8, VC), F32),
            pltpu.VMEM((8, VC), F32),
            pltpu.VMEM((N_ROW - 1, 8, VC), F32),
            pltpu.VMEM((N_COL - 1, 8, VC), F32),
            pltpu.VMEM((NOTE, VC), F32),
            pltpu.VMEM((S, 3, NOTE, VC), F32),
            pltpu.VMEM((32, VC), F32),
            dma((10,)), dma, dma((8,)), dma((8,)),
            dma, dma, dma, dma,
            dma((S, 3)), dma((S, 3)), dma((S, 6)), dma((S, 6)),
        ],
        compiler_params=pltpu.CompilerParams(
            collective_id=0, has_side_effects=True, vmem_limit_bytes=32 * 1024 * 1024),
        name="relax_and_gather",
    )(*operands)


BATCH = 8


def sampled(apart, shift, side):
    shift = jnp.full((1, TILE), shift, F32)
    low = jnp.floor(shift)
    at_low = jnp.maximum(0.0, 1.0 - jnp.abs(low - shift)).astype(BF16)
    at_high = jnp.maximum(0.0, 1.0 - jnp.abs(low + 1.0 - shift)).astype(BF16)
    low_place = (side * low).astype(BF16)
    high_place = (side * (low + 1.0)).astype(BF16)
    matrix = apart[...]
    return jnp.where(matrix == low_place, at_low, jnp.where(matrix == high_place, at_high, jnp.zeros((), BF16)))


def warped_by(source, apart, shift_y, shift_x):
    across = jnp.dot(source, sampled(apart, shift_x, -1.0), preferred_element_type=F32)
    return jnp.dot(sampled(apart, shift_y, 1.0), across.astype(BF16), preferred_element_type=F32)


def columns_apart():
    row = lax.broadcasted_iota(jnp.int32, (TILE, TILE), 0)
    lane = lax.broadcasted_iota(jnp.int32, (TILE, TILE), 1)
    return (lane - row).astype(F32).astype(BF16)


def warp_kernel(list_ref, tiles_ref, blank_ref, part_ref, apart):
    count = list_ref[4, 0].astype(jnp.int32)
    apart[...] = columns_apart()

    def entry(n):
        code = list_ref[0, n].astype(jnp.int32)
        key = code & 15
        j = (code >> 4) & 3
        place = code >> 6
        s = place >> 2
        source = tiles_ref[s, key >> 2, :, pl.ds(pl.multiple_of((key & 3) * TILE, TILE), TILE)]
        value = list_ref[3, n] * warped_by(source, apart, list_ref[1, n], list_ref[2, n])
        return value, (s, jnp.maximum(place & 3, 2) - 2, slice(None), pl.ds(pl.multiple_of(j * TILE, TILE), TILE))

    def batch(b, carry):
        found = [entry(b * BATCH + n) for n in range(BATCH)]
        for value, place in found:
            part_ref[place] = (part_ref[place].astype(F32) + value).astype(BF16)
        return carry

    lax.fori_loop(0, (count + BATCH - 1) // BATCH, batch, 0)


def warp(entries, tiles, blank):
    vmem = pl.BlockSpec(memory_space=pltpu.VMEM)
    smem = pl.BlockSpec(memory_space=pltpu.SMEM)
    return pl.pallas_call(
        warp_kernel,
        out_shape=jax.ShapeDtypeStruct((S, 2, TILE, WIDE), BF16),
        in_specs=[smem, vmem, vmem],
        out_specs=vmem,
        scratch_shapes=[pltpu.VMEM((TILE, TILE), BF16)],
        input_output_aliases={2: 0},
        compiler_params=pltpu.CompilerParams(vmem_limit_bytes=32 * 1024 * 1024),
        name="warp_partials",
    )(entries, tiles, blank)


HALVES = 2
SUBS = ((0, 64), (64, 64))
DEEP = 64


def scatter_kernel(
    listed_ref, placed_ref, tiles_ref, part_ref, zero_ref, one_ref, two_ref,
    own_ref, place_ref, nearer, total, apart, relay, onward, got, pool, half, quarter, twos, list_sem,
    relay_send, relay_recv, direct_send, direct_recv, onward_send, onward_recv,
):
    r = lax.axis_index("row")
    c = lax.axis_index("col")
    y = lax.rem(c, 4)
    z = c // 4
    barrier = pltpu.get_barrier_semaphore()
    for s in range(S):
        for i in (1, 2):
            pl.semaphore_signal(
                barrier, inc=1, device_id=(r, peer_col(y, z, SCATTER_MASK[s], i)), device_id_type=MESH)
    listing = [pltpu.make_async_copy(listed_ref, own_ref, list_sem.at[0]),
               pltpu.make_async_copy(placed_ref, place_ref, list_sem.at[1])]
    for copy in listing:
        copy.start()
    row = lax.broadcasted_iota(jnp.int32, (TILE, VC), 0)
    lane = lax.broadcasted_iota(jnp.int32, (TILE, VC), 1)
    pool[...] = jnp.where(row // 2 == lane, 0.25, 0.0).astype(BF16)
    apart[...] = columns_apart()
    pl.semaphore_wait(barrier, 2 * S)

    def rows_of(h, u):
        return pl.ds(h * (TILE // HALVES) + SUBS[u][0], SUBS[u][1])

    def sub_of(u):
        return pl.ds(*SUBS[u])

    def copy_to(s, peer, near, far, send, recv):
        return pltpu.make_async_remote_copy(
            src_ref=near, dst_ref=far, send_sem=send, recv_sem=recv,
            device_id=(r, peer_col(y, z, SCATTER_MASK[s], peer)), device_id_type=MESH)

    def half_of(h):
        return pl.ds(h * (TILE // HALVES), TILE // HALVES)

    def to_relay(s, h):
        return copy_to(s, h + 1, part_ref.at[s, 1, half_of(h)], relay.at[s, h],
                       relay_send.at[s, h], relay_recv.at[s, h])

    def to_end(s, h):
        near = nearer.at[s] if h == 0 else part_ref.at[s, 0]
        return copy_to(s, h + 1, near.at[half_of(h)], got.at[s, h, half_of(h)],
                       direct_send.at[s, h], direct_recv.at[s, h])

    def to_end_summed(s, h, u):
        other = 1 - h
        return copy_to(s, other + 1, onward.at[s, h, sub_of(u)], got.at[s, other, rows_of(h, u)],
                       onward_send.at[s, h, u], onward_recv.at[s, h, u])

    steps = [(u, h, s) for u in range(len(SUBS)) for h in range(HALVES) for s in range(S)]
    ways = [(h, s) for h in range(HALVES) for s in range(S)]
    for h, s in ways:
        to_relay(s, h).start()
    for s in range(S):
        to_end(s, 1).start()

    def share(s, i, put):
        @pl.loop(0, TC)
        def _(j):
            value = None
            base = 4 * (2 * s + i)
            for k in range(K):
                e = j * K + k
                tile = place_ref[base + 1, e]
                wide = tiles_ref[s, place_ref[base, e]]
                source = wide[:, 0:TILE]
                for t in range(1, TC):
                    source = jnp.where(tile == t, wide[:, t * TILE:(t + 1) * TILE], source)
                term = own_ref[base + 3, e] * warped_by(source, apart, own_ref[base + 1, e], own_ref[base + 2, e])
                value = term if value is None else value + term
            put(value, pl.ds(pl.multiple_of(j * TILE, TILE), TILE))

    def put_near(s, value, cols):
        nearer[s, :, cols] = value.astype(BF16)

    def put_own(s, value, cols):
        total[s, :, cols] = value

    for copy in listing:
        copy.wait()
    for s in range(S):
        share(s, 1, functools.partial(put_near, s))
        to_end(s, 0).start()
    for h, s in ways:
        to_relay(s, h).wait_recv()
    for u, h, s in steps:
        ours = part_ref[s, 0, rows_of(h, u)] if h == 0 else nearer[s, rows_of(h, u)]
        summed = relay[s, h, sub_of(u)].astype(F32) + ours.astype(F32)
        onward[s, h, sub_of(u)] = summed.astype(BF16)
        to_end_summed(s, h, u).start()
    for s in range(S):
        share(s, 0, functools.partial(put_own, s))

    def pooled(block):
        high = block.astype(BF16)
        low = (block - high.astype(F32)).astype(BF16)
        matrix = pool[...]
        return (jnp.dot(high, matrix, preferred_element_type=F32)
                + jnp.dot(low, matrix, preferred_element_type=F32))

    for h, s in ways:
        to_end(s, h).wait_recv()
        rows = half_of(h)
        total[s, rows] = total[s, rows] + got[s, h, rows].astype(F32)

    for u, h, s in steps:
        to_end_summed(s, h, u).wait_recv()
        rows = rows_of(h, u)
        start, deep = rows.start, rows.size
        for j in range(TC):
            cols = pl.ds(j * TILE, TILE)
            block = total[s, rows, cols] + got[s, 1 - h, rows, cols].astype(F32)
            zero_ref[s, rows, cols] = block.astype(BF16)
            half[j, pl.ds(0, deep)] = pooled(block)
        ones = []
        for j in range(TC):
            piece = half[j, pl.ds(0, deep // 2, stride=2), :] + half[j, pl.ds(1, deep // 2, stride=2), :]
            one_ref[s, pl.ds(start // 2, deep // 2), pl.ds(j * VC, VC)] = piece.astype(BF16)
            ones.append(piece)
        for j in range(2):
            quarter[j, pl.ds(0, deep // 2)] = pooled(jnp.concatenate(ones[2 * j:2 * j + 2], axis=1))
            piece = quarter[j, pl.ds(0, deep // 4, stride=2), :] + quarter[j, pl.ds(1, deep // 4, stride=2), :]
            twos[s, pl.ds(start // 4, deep // 4), pl.ds(j * VC, VC)] = piece
    two_ref[...] = twos[...].astype(BF16)

    for h, s in ways:
        to_relay(s, h).wait_send()
        to_end(s, h).wait_send()
    for u, h, s in steps:
        to_end_summed(s, h, u).wait_send()


def scatter(own_list, places, tiles, part):
    vmem = pl.BlockSpec(memory_space=pltpu.VMEM)
    dma = pltpu.SemaphoreType.DMA((S, HALVES, len(SUBS)))
    way = pltpu.SemaphoreType.DMA((S, HALVES))
    halved = pltpu.VMEM((S, HALVES, TILE // HALVES, WIDE), BF16)
    return pl.pallas_call(
        scatter_kernel,
        out_shape=(
            jax.ShapeDtypeStruct((S, TILE, WIDE), BF16),
            jax.ShapeDtypeStruct((S, TILE // 2, WIDE // 2), BF16),
            jax.ShapeDtypeStruct((S, TILE // 4, WIDE // 4), BF16),
        ),
        in_specs=[vmem, vmem, vmem, vmem],
        out_specs=(vmem, vmem, vmem),
        scratch_shapes=[
            pltpu.SMEM((16, VC), F32),
            pltpu.SMEM((16, VC), jnp.int32),
            pltpu.VMEM((S, TILE, WIDE), BF16),
            pltpu.VMEM((S, TILE, WIDE), F32),
            pltpu.VMEM((TILE, TILE), BF16),
            halved,
            halved,
            pltpu.VMEM((S, 2, TILE, WIDE), BF16),
            pltpu.VMEM((TILE, VC), BF16),
            pltpu.VMEM((TC, DEEP, VC), F32),
            pltpu.VMEM((2, DEEP // 2, VC), F32),
            pltpu.VMEM((S, TILE // 4, WIDE // 4), F32),
            pltpu.SemaphoreType.DMA((2,)), way, way, way, way, dma, dma,
        ],
        compiler_params=pltpu.CompilerParams(
            collective_id=1, has_side_effects=True, vmem_limit_bytes=32 * 1024 * 1024),
        name="scatter_and_pool",
    )(own_list, places, tiles, part)


STORES = 8


def store_kernel(*refs):
    count = (len(refs) - 1) // 2
    sems = refs[-1]
    copies = []
    for n in range(count):
        near, far = refs[n], refs[count + n]
        pieces = STORES if n == 2 else 1
        rows = near.shape[1] // pieces
        for p in range(pieces):
            span = pl.ds(p * rows, rows)
            copies.append(pltpu.make_async_copy(near.at[:, span], far.at[:, span], sems.at[len(copies)]))
    for copy in copies:
        copy.start()
    for copy in copies:
        copy.wait()


def store(*arrays):
    count = len(arrays)
    return pl.pallas_call(
        store_kernel,
        out_shape=tuple(jax.ShapeDtypeStruct(a.shape, a.dtype) for a in arrays),
        in_specs=[pl.BlockSpec(memory_space=pltpu.VMEM)] * count,
        out_specs=(pl.BlockSpec(memory_space=pltpu.HBM),) * count,
        scratch_shapes=[pltpu.SemaphoreType.DMA((count + STORES - 1,))],
        compiler_params=pltpu.CompilerParams(vmem_limit_bytes=32 * 1024 * 1024),
        name="store_results",
    )(*arrays)


def shards(load_force, stiffness, cracks, anchor, images, owners, source_tile, offsets, blend_weight, counts):
    flat = [a.reshape(1, -1) for a in (owners, source_tile)]
    displacement, residual, entries, own_list, places, tiles, blank = relax(
        load_force, stiffness, cracks, anchor, *flat, offsets, blend_weight.reshape(1, -1), counts.reshape(1, -1), images)
    part = warp(entries, tiles, blank)
    level_zero, level_one, level_two = scatter(own_list, places, tiles, part)
    return store(displacement, residual, level_zero, level_one, level_two)


def solution(mesh):
    flat = P(("row", "col"))
    in_specs = (
        P(None, None, "row", "col"),
        P(None, None, "row", "col"),
        P(None, None, "row", "col"),
        P(None, "row", "col"),
        P(None, "row", "col"),
        P(("row", "col"), None),
        flat,
        P(None, ("row", "col")),
        flat,
        flat,
    )
    out_specs = (
        P(None, None, "row", "col"),
        P(None, None, "row", "col"),
        P(None, "row", "col"),
        P(None, "row", "col"),
        P(None, "row", "col"),
    )
    return jax.shard_map(shards, mesh=mesh, in_specs=in_specs, out_specs=out_specs, check_vma=False)
```

```python
import functools

import jax
import jax.numpy as jnp
from jax import lax
from jax.experimental import pallas as pl
from jax.experimental.pallas import tpu as pltpu
from jax.sharding import PartitionSpec as P

S = 2
TILE = 256
SPACING = 8
K = 6
ITERS = 4
TC = 4
ENT_DEV = 48
VR = 32
VC = 128
VT = 32
N_ROW = 8
N_COL = 16
WIDE = TC * TILE
ROWS = VR + 16
COLS = 2 * VC
MESH = pl.DeviceIdType.MESH
F32 = jnp.float32
BF16 = jnp.bfloat16


def flipped(v, mask):
    if mask == 1:
        return v + 1 - 2 * lax.rem(v, 2)
    return 3 - v


def peer_col(y, z, mask, i):
    py = flipped(y, mask) if i % 2 == 1 else y
    pz = flipped(z, mask) if i // 2 == 1 else z
    return pz * 4 + py


GATHER_MASK = (1, 3)
SCATTER_MASK = (3, 1)


NOTE = 8
LIST = 256
MOMENTS = 2 * ITERS
SCALE = 8.0


def two_sum(a, b):
    total = a + b
    part = total - a
    return total, (a - (total - part)) + (b - part)


def renormed(high, low):
    total = high + low
    return total, low - (total - high)


def split(a):
    wide = a * 4097.0
    high = wide - (wide - a)
    return high, a - high


def two_product(a, b, a_parts, b_parts):
    (ah, al), (bh, bl) = a_parts, b_parts
    product = a * b
    return product, ((ah * bh - product) + ah * bl + al * bh) + al * bl


def added(x, y):
    total, rest = two_sum(x[0], y[0])
    return renormed(total, rest + (x[1] + y[1]))


def times(x, y):
    product, rest = two_product(x[0], y[0], split(x[0]), split(y[0]))
    return renormed(product, rest + (x[0] * y[1] + x[1] * y[0]))


def minus(x):
    return -x[0], -x[1]


def over(x, y):
    first = x[0] / y[0]
    nothing = jnp.zeros_like(first)
    rest = added(x, minus(times((first, nothing), y)))
    return renormed(first, rest[0] / y[0])


def residual_polynomial(moment):
    one = (jnp.ones_like(moment[0][0]), jnp.zeros_like(moment[0][0]))
    rho, pi = [one], [one]
    upper = moment[0]
    for k in range(ITERS):
        lower = None
        for j, weight in enumerate(pi):
            term = moment[j + k + 1] if k == 0 else times(weight, moment[j + k + 1])
            lower = term if lower is None else added(lower, term)
        step = over(upper, lower)
        moved = [minus(times(step, weight)) if k else minus(step) for weight in pi]
        rho = [rho[0]] + [added(rho[j], moved[j - 1]) for j in range(1, k + 1)] + [moved[k]]
        if k == ITERS - 1:
            return rho
        upper = moment[k + 1]
        for j in range(1, k + 2):
            upper = added(upper, times(rho[j], moment[j + k + 1]))
        grow = minus(over(upper, lower))
        pi = [added(rho[j], times(grow, pi[j]) if k else grow) for j in range(k + 1)] + [rho[k + 1]]


def relax_kernel(
    load_hbm, stiff_hbm, crack_hbm, anchor_hbm, owner_hbm, source_hbm, offset_hbm, blend_hbm, count_hbm, images_hbm,
    disp_ref, resid_ref, list_ref, own_ref, place_ref, tiles_ref, blank_ref,
    fields, stiff, crack, owner, source, offset, blend, count,
    strips, halo_v, halo_h, halo_c, coef, krylov,
    part_a, part_b, got_a, got_b, note, notes, sums,
    load_sem, own_sem, halo_send, halo_recv, send_a, recv_a, send_b, recv_b,
    note_send, note_recv, tile_send, tile_recv,
):
    r = lax.axis_index("row")
    c = lax.axis_index("col")
    y = lax.rem(c, 4)
    z = c // 4
    up, down = lax.rem(r + N_ROW - 1, N_ROW), lax.rem(r + 1, N_ROW)
    left, right = lax.rem(c + N_COL - 1, N_COL), lax.rem(c + 1, N_COL)
    corners = ((up, left), (up, right), (down, left), (down, right))

    barrier = pltpu.get_barrier_semaphore()

    loads = []
    for n, (near, far) in enumerate((
        (stiff_hbm, stiff), (crack_hbm, crack),
        (load_hbm.at[0], fields.at[pl.ds(0, 2)]), (load_hbm.at[1], fields.at[pl.ds(2, 2)]),
        (anchor_hbm, fields.at[pl.ds(8, 2)]),
        (owner_hbm, owner), (source_hbm, source), (offset_hbm, offset), (blend_hbm, blend), (count_hbm, count),
    )):
        loads.append(pltpu.make_async_copy(near, far, load_sem.at[n]))
    for copy in loads:
        copy.start()
    for corner in corners:
        pl.semaphore_signal(barrier, inc=1, device_id=corner, device_id_type=MESH)
    for d in range(1, N_COL):
        pl.semaphore_signal(barrier, inc=1, device_id=(r, lax.rem(c + d, N_COL)), device_id_type=MESH)
    for d in range(1, N_ROW):
        pl.semaphore_signal(barrier, inc=1, device_id=(lax.rem(r + d, N_ROW), c), device_id_type=MESH)

    for copy in loads:
        copy.wait()
    for s in range(S):
        for k in range(2):
            fields[4 + 2 * s + k] = stiff[s, k] * crack[s, k].astype(F32)
    lane = lax.broadcasted_iota(jnp.int32, (VR, VC), 1)
    first = jnp.zeros((VR, VC), F32)
    last = jnp.zeros((VR, VC), F32)
    for f in range(10):
        block = fields[f]
        here = (lane >= 4 * f) & (lane < 4 * f + 4)
        first = jnp.where(here, block if f == 0 else pltpu.roll(block, 4 * f, 1), first)
        last = jnp.where(here, pltpu.roll(block, 4 * f + 4, 1), last)
    strips[0] = first
    strips[1] = last

    pl.semaphore_wait(barrier, N_ROW - 1 + N_COL - 1 + 4)

    halo = []
    for n, (near, far, device) in enumerate((
        (fields.at[:, pl.ds(VR - 8, 8), :], halo_v.at[0], (down, c)),
        (fields.at[:, pl.ds(0, 8), :], halo_v.at[1], (up, c)),
        (strips.at[1], halo_h.at[0], (r, right)),
        (strips.at[0], halo_h.at[1], (r, left)),
        (strips.at[1, pl.ds(VR - 8, 8)], halo_c.at[0], (down, right)),
        (strips.at[0, pl.ds(VR - 8, 8)], halo_c.at[1], (down, left)),
        (strips.at[1, pl.ds(0, 8)], halo_c.at[2], (up, right)),
        (strips.at[0, pl.ds(0, 8)], halo_c.at[3], (up, left)),
    )):
        halo.append(pltpu.make_async_remote_copy(
            src_ref=near, dst_ref=far, send_sem=halo_send.at[n], recv_sem=halo_recv.at[n],
            device_id=device, device_id_type=MESH))
    for copy in halo:
        copy.start()

    half = TILE // 2

    def tile_copy(s, n, slot_from, slot_to, part, peer):
        rows = pl.ds(part * half, half)
        near = images_hbm.at[s, rows] if slot_from == 0 else tiles_ref.at[s, slot_from, rows]
        return pltpu.make_async_remote_copy(
            src_ref=near, dst_ref=tiles_ref.at[s, slot_to, rows],
            send_sem=tile_send.at[s, n], recv_sem=tile_recv.at[s, n],
            device_id=(r, peer_col(y, z, GATHER_MASK[s], peer)), device_id_type=MESH)

    direct = [
        [tile_copy(s, 0, 0, 2, 0, 2), tile_copy(s, 1, 0, 1, 1, 1), tile_copy(s, 2, 0, 1, 0, 1), tile_copy(s, 3, 0, 2, 1, 2)]
        for s in range(S)
    ]
    relayed = [[tile_copy(s, 4, 2, 3, 0, 1), tile_copy(s, 5, 1, 3, 1, 2)] for s in range(S)]
    for n in range(4):
        for s in range(S):
            direct[s][n].start()
    own = pltpu.make_async_copy(images_hbm, tiles_ref.at[:, 0], own_sem)
    own.start()

    entry_lane = lax.broadcasted_iota(jnp.int32, (1, ENT_DEV), 1)
    listed = jnp.zeros((1, ENT_DEV), jnp.int32)
    for t in range(ENT_DEV // K):
        listed = jnp.where(entry_lane // K == t, count[:, t:t + 1], listed)
    note[...] = jnp.zeros((NOTE, VC), F32)
    note[0:1, 0:ENT_DEV] = (owner[...] * TC + source[...]).astype(F32)
    note[1:3, 0:ENT_DEV] = offset[...].astype(F32)
    note[3:4, 0:ENT_DEV] = jnp.where(lax.rem(entry_lane, K) < listed, blend[...], 0.0)

    blank_ref[...] = jnp.zeros(blank_ref.shape, BF16)

    for copy in halo:
        copy.wait_recv()

    wide_row = lax.broadcasted_iota(jnp.int32, (ROWS, VC), 0) + r * VR - 8
    wide_lane = lax.broadcasted_iota(jnp.int32, (ROWS, VC), 1)
    side_col = jnp.where(wide_lane < VC // 2, wide_lane + VC, wide_lane - VC) + c * VC
    row_in = (wide_row >= 0) & (wide_row < VR * N_ROW)
    side_in = row_in & (side_col >= 0) & (side_col < VC * N_COL)
    from_left = jnp.concatenate([halo_c[0], halo_h[0], halo_c[2]], axis=0)
    from_right = jnp.concatenate([halo_c[1], halo_h[1], halo_c[3]], axis=0)

    def widened(f):
        center = jnp.concatenate([halo_v[0, f], fields[f], halo_v[1, f]], axis=0)
        to_left = pltpu.roll(from_left, 124 - 4 * f, 1)
        to_right = from_right if f == 0 else pltpu.roll(from_right, VC - 4 * f, 1)
        side = jnp.where(wide_lane < 4, to_right, jnp.where(wide_lane >= 124, to_left, 0.0))
        return jnp.concatenate(
            [jnp.where(row_in, center, 0.0), jnp.where(side_in, side, 0.0)], axis=1)

    inside = jnp.concatenate([row_in.astype(F32), side_in.astype(F32)], axis=1)
    for s in range(S):
        to_right = widened(4 + 2 * s)
        to_low = widened(5 + 2 * s)
        to_left = pltpu.roll(to_right, 1, 1) * inside
        to_high = pltpu.roll(to_low, 1, 0) * inside
        coef[s, 0] = widened(8 + s) + to_right + to_left + to_low + to_high
        coef[s, 1] = to_right
        coef[s, 2] = to_left
        coef[s, 3] = to_low
        coef[s, 4] = to_high
        for k in range(2):
            krylov[0, 2 * s + k] = widened(2 * s + k)

    for n in range(ITERS):
        for f in range(4):
            s = f // 2
            v = krylov[n, f]
            w = coef[s, 0] * v
            w = w - coef[s, 1] * pltpu.roll(v, COLS - 1, 1)
            w = w - coef[s, 2] * pltpu.roll(v, 1, 1)
            w = w - coef[s, 3] * pltpu.roll(v, ROWS - 1, 0)
            w = w - coef[s, 4] * pltpu.roll(v, 1, 0)
            krylov[n + 1, f] = w * (1.0 / SCALE)

    middle = 8 + VR // 2
    point = lax.rem(lax.broadcasted_iota(jnp.int32, (1, VC), 1), VT) - VT // 2
    for f in range(4):
        row = jnp.zeros((1, VC), F32)
        for n in range(ITERS):
            line = krylov[n, f, pl.ds(middle, 1), pl.ds(0, VC)]
            row = jnp.where(point == n, line if n == 0 else pltpu.roll(line, n, 1), row)
        note[4 + f:5 + f, :] = row
    told = []
    for s in range(S):
        for i in (1, 2, 3):
            told.append(pltpu.make_async_remote_copy(
                src_ref=note, dst_ref=notes.at[s, i - 1],
                send_sem=note_send.at[s, i - 1], recv_sem=note_recv.at[s, i - 1],
                device_id=(r, peer_col(y, z, SCATTER_MASK[s], i)), device_id_type=MESH))

    moments = [[None] * S for _ in range(MOMENTS)]
    for s in range(S):
        totals = [None] * MOMENTS
        for f in (2 * s, 2 * s + 1):
            for g in range(VR // 8):
                vectors = [krylov[n, f, pl.ds(8 + 8 * g, 8), pl.ds(0, VC)] for n in range(ITERS + 1)]
                parts = [split(v) for v in vectors]
                for m in range(MOMENTS):
                    a, b = m // 2, m - m // 2
                    product, rest = two_product(vectors[a], vectors[b], parts[a], parts[b])
                    if totals[m] is None:
                        totals[m] = (product, rest)
                    else:
                        total, slip = two_sum(totals[m][0], product)
                        totals[m] = (total, totals[m][1] + (rest + slip))
        for m in range(MOMENTS):
            moments[m][s] = totals[m]

    level = [moments[m][s] for m in range(MOMENTS) for s in range(S)]
    sublane = lax.broadcasted_iota(jnp.int32, (8, VC), 0)
    packed = []
    for base in range(0, len(level), 8):
        group = level[base:base + 8]
        shift = 4
        while shift:
            low = lax.rem(sublane // shift, 2) == 0
            merged = []
            for n in range(shift):
                a, b = group[n], group[n + shift]
                first = tuple(jnp.where(low, u, pltpu.roll(v, shift, 0)) for u, v in zip(a, b))
                second = tuple(jnp.where(low, pltpu.roll(u, 8 - shift, 0), v) for u, v in zip(a, b))
                merged.append(added(first, second))
            group = merged
            shift //= 2
        packed.append(group[0])
    for step in (VC // 2, VC // 4):
        packed = [added(pair, tuple(pltpu.roll(part, step, 1) for part in pair)) for pair in packed]
    sum_lane = lax.broadcasted_iota(jnp.int32, (8, VC), 1)
    quarter = VC // 4

    def joined(one, two):
        return jnp.where(sum_lane < VC // 2, one, two)

    part_a[...] = joined(
        *[jnp.where(lax.rem(sum_lane, VC // 2) < quarter, one, two) for one, two in zip(*packed)])

    for d in range(1, N_ROW):
        pltpu.make_async_remote_copy(
            src_ref=part_a, dst_ref=got_a.at[d - 1], send_sem=send_a,
            recv_sem=recv_a, device_id=(lax.rem(r + d, N_ROW), c), device_id_type=MESH).start()

    def sum_copy(phase):
        got, send, recv = ((got_a, send_a, recv_a), (got_b, send_b, recv_b))[phase]
        return pltpu.make_async_remote_copy(
            src_ref=got, dst_ref=got, send_sem=send, recv_sem=recv,
            device_id=((down, c), (r, right))[phase], device_id_type=MESH)

    def gathered(own_part, got):
        terms = [own_part[...]] + [got[n] for n in range(got.shape[0])]
        terms = [(term, pltpu.roll(term, VC // 2, 1)) for term in terms]
        while len(terms) > 1:
            terms = [added(terms[n], terms[n + 1]) if n + 1 < len(terms) else terms[n]
                     for n in range(0, len(terms), 2)]
        return terms[0]

    sum_copy(0).wait_recv()
    high, low = gathered(part_a, got_a)
    part_b[...] = joined(high, pltpu.roll(low, VC // 2, 1))

    for d in range(1, N_COL):
        pltpu.make_async_remote_copy(
            src_ref=part_b, dst_ref=got_b.at[d - 1], send_sem=send_b,
            recv_sem=recv_b, device_id=(r, lax.rem(c + d, N_COL)), device_id_type=MESH).start()

    for copy in told:
        copy.start()

    for s in range(S):
        direct[s][0].wait_recv()
        relayed[s][0].start()
        direct[s][1].wait_recv()
        relayed[s][1].start()

    sum_copy(1).wait_recv()
    total = gathered(part_b, got_b)
    shift = quarter // 2
    while shift:
        inner = lax.rem(sum_lane, quarter) < quarter - shift
        total = added(total, tuple(
            jnp.where(inner, pltpu.roll(part, VC - shift, 1), pltpu.roll(part, quarter - shift, 1)) for part in total))
        shift //= 2
    odd = lax.rem(sum_lane // quarter, 2) == 1
    spread = []
    for part in total:
        one = jnp.where(odd, pltpu.roll(part, quarter, 1), part)
        two = jnp.where(odd, part, pltpu.roll(part, VC - quarter, 1))
        spread.append(jnp.concatenate([joined(u, pltpu.roll(u, VC // 2, 1)) for u in (one, two)], axis=0))
    total = spread
    sums[0:16] = total[0]
    sums[16:32] = total[1]
    rho = residual_polynomial([
        (sums[2 * m:2 * m + 2, :], sums[16 + 2 * m:18 + 2 * m, :]) for m in range(MOMENTS)])
    rho = [weight[0] for weight in rho]

    for f in range(4):
        s, k = f // 2, f % 2
        vectors = [krylov[n, f, pl.ds(8, VR), pl.ds(0, VC)] for n in range(ITERS + 1)]
        moved = rho[1][s:s + 1] * vectors[0]
        rest = vectors[0]
        for n in range(1, ITERS + 1):
            rest = rest + rho[n][s:s + 1] * vectors[n]
            if n < ITERS:
                moved = moved + rho[n + 1][s:s + 1] * vectors[n]
        disp_ref[s, k] = moved * (-1.0 / SCALE)
        resid_ref[s, k] = rest

    for copy in told:
        copy.wait_recv()
    texts = [(s, note if i == 0 else notes.at[s, i - 1]) for s in range(S) for i in range(4)]
    note_lane = lax.broadcasted_iota(jnp.int32, (8, VC), 1)
    note_row = lax.broadcasted_iota(jnp.int32, (8, VC), 0)

    def stacked(n):
        rows = jnp.concatenate([text[n:n + 1, :] for _, text in texts], axis=0)
        return jnp.where(note_row < 4, rows, pltpu.roll(rows, VC - TC * K, 1))

    note_point = lax.rem(note_lane, VT) - VT // 2
    scales = jnp.zeros((8, VC), F32)
    for n in range(ITERS):
        scale = jnp.where(note_row < 4, rho[n + 1][0:1], rho[n + 1][1:2])
        scales = jnp.where(note_point == n, scale, scales)

    def shifted(k):
        rows = scales * jnp.concatenate([text[4 + 2 * s + k:5 + 2 * s + k, :] for s, text in texts], axis=0)
        rows = rows + pltpu.roll(rows, VC - 1, 1)
        rows = (rows + pltpu.roll(rows, VC - 2, 1)) * (-SPACING / SCALE)
        shift = stacked(1 + k)
        for j in range(TC):
            at = VT * j + VT // 2
            shift = shift + jnp.where(note_lane // K == j, rows[:, at:at + 1], 0.0)
        return shift

    named = stacked(0).astype(jnp.int32)
    owner_col = named // TC
    weight = stacked(3)
    at_y, at_z = lax.rem(owner_col, 4), owner_col // 4
    near = [((at_y == y) | (at_y == flipped(y, m))) & ((at_z == z) | (at_z == flipped(z, m))) for m in GATHER_MASK]
    mine = jnp.where(note_row < 4, near[0].astype(F32), near[1].astype(F32))
    mine = jnp.where((weight > 0.0) & (note_lane < TC * K), mine, 0.0)
    slot = jnp.where(at_y == y, 0, 1) + jnp.where(at_z == z, 0, 2)
    key = slot * TC + lax.rem(named, TC)
    code = ((note_row * TC + note_lane // K) * 16 + key).astype(F32)
    sent = jnp.where(lax.rem(note_row, 4) < 2, 0.0, mine)
    rank = sent
    for step in (1, 2, 4, 8, 16):
        rank = rank + jnp.where(note_lane >= step, pltpu.roll(rank, step, 1), 0.0)
    above = jnp.sum(sent, axis=1, keepdims=True) + jnp.zeros((8, VC), F32)
    base = above
    for step in (1, 2, 4):
        base = base + jnp.where(note_row >= step, pltpu.roll(base, step, 0), 0.0)
    total = base[7:8, :]
    rank = jnp.where(sent > 0.0, rank + (base - above) - 1.0, -1.0)
    shift_y, shift_x = shifted(0), shifted(1)
    columns = [jnp.transpose(part)[0:TC * K] for part in (rank, code, shift_y, shift_x, weight)]
    own_ref[...] = jnp.concatenate(
        [part[4 * s + i:4 * s + i + 1] for s in range(S) for i in range(2)
         for part in (weight, shift_y, shift_x, mine * weight)], axis=0)
    place_ref[...] = jnp.concatenate(
        [part[4 * s + i:4 * s + i + 1] for s in range(S) for i in range(2)
         for part in (slot, lax.rem(named, TC), slot, slot)], axis=0)
    place = lax.broadcasted_iota(jnp.int32, (TC * K, LIST), 1).astype(F32)
    listed = [jnp.zeros((1, LIST), F32)] * 4
    for n in range(8):
        chosen = columns[0][:, n:n + 1] == place
        listed = [old + jnp.sum(jnp.where(chosen, column[:, n:n + 1], 0.0), axis=0, keepdims=True)
                  for old, column in zip(listed, columns[1:])]
    list_ref[...] = jnp.concatenate(
        listed + [jnp.concatenate([total] * (LIST // VC), axis=1), jnp.zeros((3, LIST), F32)], axis=0)

    for copy in told:
        copy.wait_send()
    for copy in halo:
        copy.wait_send()
    for phase in range(2):
        sum_copy(phase).wait_send()
    own.wait()
    for s in range(S):
        direct[s][2].wait_recv()
        direct[s][3].wait_recv()
        for copy in relayed[s]:
            copy.wait()
        for copy in direct[s]:
            copy.wait_send()


def relax(*operands):
    vmem = pl.BlockSpec(memory_space=pltpu.VMEM)
    hbm = pl.BlockSpec(memory_space=pltpu.HBM)
    dma = pltpu.SemaphoreType.DMA
    block = (S, 2, VR, VC)
    operands = [pltpu.with_memory_space_constraint(a, pltpu.HBM) for a in operands]
    return pl.pallas_call(
        relax_kernel,
        out_shape=(
            jax.ShapeDtypeStruct(block, F32),
            jax.ShapeDtypeStruct(block, F32),
            jax.ShapeDtypeStruct((8, LIST), F32),
            jax.ShapeDtypeStruct((16, VC), F32),
            jax.ShapeDtypeStruct((16, VC), jnp.int32),
            jax.ShapeDtypeStruct((S, 4, TILE, WIDE), BF16),
            jax.ShapeDtypeStruct((S, 2, TILE, WIDE), BF16),
        ),
        in_specs=[hbm] * 10,
        out_specs=(vmem,) * 7,
        scratch_shapes=[
            pltpu.VMEM((10, VR, VC), F32),
            pltpu.VMEM(block, F32),
            pltpu.VMEM(block, jnp.int32),
            pltpu.VMEM((1, ENT_DEV), jnp.int32),
            pltpu.VMEM((1, ENT_DEV), jnp.int32),
            pltpu.VMEM((2, ENT_DEV), jnp.int32),
            pltpu.VMEM((1, ENT_DEV), F32),
            pltpu.VMEM((1, ENT_DEV // K), jnp.int32),
            pltpu.VMEM((2, VR, VC), F32),
            pltpu.VMEM((2, 10, 8, VC), F32),
            pltpu.VMEM((2, VR, VC), F32),
            pltpu.VMEM((4, 8, VC), F32),
            pltpu.VMEM((S, 5, ROWS, COLS), F32),
            pltpu.VMEM((ITERS + 1, 4, ROWS, COLS), F32),
            pltpu.VMEM((8, VC), F32),
            pltpu.VMEM((8, VC), F32),
            pltpu.VMEM((N_ROW - 1, 8, VC), F32),
            pltpu.VMEM((N_COL - 1, 8, VC), F32),
            pltpu.VMEM((NOTE, VC), F32),
            pltpu.VMEM((S, 3, NOTE, VC), F32),
            pltpu.VMEM((32, VC), F32),
            dma((10,)), dma, dma((8,)), dma((8,)),
            dma, dma, dma, dma,
            dma((S, 3)), dma((S, 3)), dma((S, 6)), dma((S, 6)),
        ],
        compiler_params=pltpu.CompilerParams(
            collective_id=0, has_side_effects=True, vmem_limit_bytes=32 * 1024 * 1024),
        name="relax_and_gather",
    )(*operands)


BATCH = 8


def sampled(apart, shift, side):
    shift = jnp.full((1, TILE), shift, F32)
    low = jnp.floor(shift)
    at_low = jnp.maximum(0.0, 1.0 - jnp.abs(low - shift)).astype(BF16)
    at_high = jnp.maximum(0.0, 1.0 - jnp.abs(low + 1.0 - shift)).astype(BF16)
    low_place = (side * low).astype(BF16)
    high_place = (side * (low + 1.0)).astype(BF16)
    matrix = apart[...]
    return jnp.where(matrix == low_place, at_low, jnp.where(matrix == high_place, at_high, jnp.zeros((), BF16)))


def warped_by(source, apart, shift_y, shift_x):
    across = jnp.dot(source, sampled(apart, shift_x, -1.0), preferred_element_type=F32)
    return jnp.dot(sampled(apart, shift_y, 1.0), across.astype(BF16), preferred_element_type=F32)


def columns_apart():
    row = lax.broadcasted_iota(jnp.int32, (TILE, TILE), 0)
    lane = lax.broadcasted_iota(jnp.int32, (TILE, TILE), 1)
    return (lane - row).astype(F32).astype(BF16)


def warp_kernel(listed_ref, tiles_ref, blank_ref, part_ref, apart, list_ref, list_sem):
    listing = pltpu.make_async_copy(listed_ref, list_ref, list_sem)
    listing.start()
    apart[...] = columns_apart()
    listing.wait()
    count = list_ref[4, 0].astype(jnp.int32)

    def entry(n):
        code = list_ref[0, n].astype(jnp.int32)
        key = code & 15
        j = (code >> 4) & 3
        place = code >> 6
        s = place >> 2
        source = tiles_ref[s, key >> 2, :, pl.ds(pl.multiple_of((key & 3) * TILE, TILE), TILE)]
        value = list_ref[3, n] * warped_by(source, apart, list_ref[1, n], list_ref[2, n])
        return value, (s, jnp.maximum(place & 3, 2) - 2, slice(None), pl.ds(pl.multiple_of(j * TILE, TILE), TILE))

    def batch(b, carry):
        found = [entry(b * BATCH + n) for n in range(BATCH)]
        for value, place in found:
            part_ref[place] = (part_ref[place].astype(F32) + value).astype(BF16)
        return carry

    lax.fori_loop(0, (count + BATCH - 1) // BATCH, batch, 0)


def warp(entries, tiles, blank):
    vmem = pl.BlockSpec(memory_space=pltpu.VMEM)
    return pl.pallas_call(
        warp_kernel,
        out_shape=jax.ShapeDtypeStruct((S, 2, TILE, WIDE), BF16),
        in_specs=[vmem, vmem, vmem],
        out_specs=vmem,
        scratch_shapes=[
            pltpu.VMEM((TILE, TILE), BF16), pltpu.SMEM((8, LIST), F32), pltpu.SemaphoreType.DMA],
        input_output_aliases={2: 0},
        compiler_params=pltpu.CompilerParams(vmem_limit_bytes=32 * 1024 * 1024),
        name="warp_partials",
    )(entries, tiles, blank)


HALVES = 2
SUBS = ((0, 64), (64, 64))
DEEP = 64


def scatter_kernel(
    listed_ref, placed_ref, tiles_ref, part_ref, zero_ref, one_ref, two_ref,
    own_ref, place_ref, nearer, total, apart, relay, onward, got, pool, half, quarter, twos, list_sem,
    relay_send, relay_recv, direct_send, direct_recv, onward_send, onward_recv,
):
    r = lax.axis_index("row")
    c = lax.axis_index("col")
    y = lax.rem(c, 4)
    z = c // 4
    barrier = pltpu.get_barrier_semaphore()
    for s in range(S):
        for i in (1, 2):
            pl.semaphore_signal(
                barrier, inc=1, device_id=(r, peer_col(y, z, SCATTER_MASK[s], i)), device_id_type=MESH)
    listing = [pltpu.make_async_copy(listed_ref, own_ref, list_sem.at[0]),
               pltpu.make_async_copy(placed_ref, place_ref, list_sem.at[1])]
    for copy in listing:
        copy.start()
    row = lax.broadcasted_iota(jnp.int32, (TILE, VC), 0)
    lane = lax.broadcasted_iota(jnp.int32, (TILE, VC), 1)
    pool[...] = jnp.where(row // 2 == lane, 0.25, 0.0).astype(BF16)
    apart[...] = columns_apart()
    pl.semaphore_wait(barrier, 2 * S)

    def rows_of(h, u):
        return pl.ds(h * (TILE // HALVES) + SUBS[u][0], SUBS[u][1])

    def sub_of(u):
        return pl.ds(*SUBS[u])

    def copy_to(s, peer, near, far, send, recv):
        return pltpu.make_async_remote_copy(
            src_ref=near, dst_ref=far, send_sem=send, recv_sem=recv,
            device_id=(r, peer_col(y, z, SCATTER_MASK[s], peer)), device_id_type=MESH)

    def half_of(h):
        return pl.ds(h * (TILE // HALVES), TILE // HALVES)

    def to_relay(s, h):
        return copy_to(s, h + 1, part_ref.at[s, 1, half_of(h)], relay.at[s, h],
                       relay_send.at[s, h], relay_recv.at[s, h])

    def to_end(s, h):
        near = nearer.at[s] if h == 0 else part_ref.at[s, 0]
        return copy_to(s, h + 1, near.at[half_of(h)], got.at[s, h, half_of(h)],
                       direct_send.at[s, h], direct_recv.at[s, h])

    def to_end_summed(s, h, u):
        other = 1 - h
        return copy_to(s, other + 1, onward.at[s, h, sub_of(u)], got.at[s, other, rows_of(h, u)],
                       onward_send.at[s, h, u], onward_recv.at[s, h, u])

    steps = [(u, h, s) for u in range(len(SUBS)) for h in range(HALVES) for s in range(S)]
    ways = [(h, s) for h in range(HALVES) for s in range(S)]
    for h, s in ways:
        to_relay(s, h).start()
    for s in range(S):
        to_end(s, 1).start()

    def share(s, i, put):
        @pl.loop(0, TC)
        def _(j):
            value = None
            base = 4 * (2 * s + i)
            for k in range(K):
                e = j * K + k
                tile = place_ref[base + 1, e]
                wide = tiles_ref[s, place_ref[base, e]]
                source = wide[:, 0:TILE]
                for t in range(1, TC):
                    source = jnp.where(tile == t, wide[:, t * TILE:(t + 1) * TILE], source)
                term = own_ref[base + 3, e] * warped_by(source, apart, own_ref[base + 1, e], own_ref[base + 2, e])
                value = term if value is None else value + term
            put(value, pl.ds(pl.multiple_of(j * TILE, TILE), TILE))

    def put_near(s, value, cols):
        nearer[s, :, cols] = value.astype(BF16)

    def put_own(s, value, cols):
        total[s, :, cols] = value

    for copy in listing:
        copy.wait()
    for s in range(S):
        share(s, 1, functools.partial(put_near, s))
        to_end(s, 0).start()
    for h, s in ways:
        to_relay(s, h).wait_recv()
    for u, h, s in steps:
        ours = part_ref[s, 0, rows_of(h, u)] if h == 0 else nearer[s, rows_of(h, u)]
        summed = relay[s, h, sub_of(u)].astype(F32) + ours.astype(F32)
        onward[s, h, sub_of(u)] = summed.astype(BF16)
        to_end_summed(s, h, u).start()
    for s in range(S):
        share(s, 0, functools.partial(put_own, s))

    def pooled(block):
        high = block.astype(BF16)
        low = (block - high.astype(F32)).astype(BF16)
        matrix = pool[...]
        return (jnp.dot(high, matrix, preferred_element_type=F32)
                + jnp.dot(low, matrix, preferred_element_type=F32))

    for h, s in ways:
        to_end(s, h).wait_recv()
        rows = half_of(h)
        total[s, rows] = total[s, rows] + got[s, h, rows].astype(F32)

    for u, h, s in steps:
        to_end_summed(s, h, u).wait_recv()
        rows = rows_of(h, u)
        start, deep = rows.start, rows.size
        for j in range(TC):
            cols = pl.ds(j * TILE, TILE)
            block = total[s, rows, cols] + got[s, 1 - h, rows, cols].astype(F32)
            zero_ref[s, rows, cols] = block.astype(BF16)
            half[j, pl.ds(0, deep)] = pooled(block)
        ones = []
        for j in range(TC):
            piece = half[j, pl.ds(0, deep // 2, stride=2), :] + half[j, pl.ds(1, deep // 2, stride=2), :]
            one_ref[s, pl.ds(start // 2, deep // 2), pl.ds(j * VC, VC)] = piece.astype(BF16)
            ones.append(piece)
        for j in range(2):
            quarter[j, pl.ds(0, deep // 2)] = pooled(jnp.concatenate(ones[2 * j:2 * j + 2], axis=1))
            piece = quarter[j, pl.ds(0, deep // 4, stride=2), :] + quarter[j, pl.ds(1, deep // 4, stride=2), :]
            twos[s, pl.ds(start // 4, deep // 4), pl.ds(j * VC, VC)] = piece
    two_ref[...] = twos[...].astype(BF16)

    for h, s in ways:
        to_relay(s, h).wait_send()
        to_end(s, h).wait_send()
    for u, h, s in steps:
        to_end_summed(s, h, u).wait_send()


def scatter(own_list, places, tiles, part):
    vmem = pl.BlockSpec(memory_space=pltpu.VMEM)
    dma = pltpu.SemaphoreType.DMA((S, HALVES, len(SUBS)))
    way = pltpu.SemaphoreType.DMA((S, HALVES))
    halved = pltpu.VMEM((S, HALVES, TILE // HALVES, WIDE), BF16)
    return pl.pallas_call(
        scatter_kernel,
        out_shape=(
            jax.ShapeDtypeStruct((S, TILE, WIDE), BF16),
            jax.ShapeDtypeStruct((S, TILE // 2, WIDE // 2), BF16),
            jax.ShapeDtypeStruct((S, TILE // 4, WIDE // 4), BF16),
        ),
        in_specs=[vmem, vmem, vmem, vmem],
        out_specs=(vmem, vmem, vmem),
        scratch_shapes=[
            pltpu.SMEM((16, VC), F32),
            pltpu.SMEM((16, VC), jnp.int32),
            pltpu.VMEM((S, TILE, WIDE), BF16),
            pltpu.VMEM((S, TILE, WIDE), F32),
            pltpu.VMEM((TILE, TILE), BF16),
            halved,
            halved,
            pltpu.VMEM((S, 2, TILE, WIDE), BF16),
            pltpu.VMEM((TILE, VC), BF16),
            pltpu.VMEM((TC, DEEP, VC), F32),
            pltpu.VMEM((2, DEEP // 2, VC), F32),
            pltpu.VMEM((S, TILE // 4, WIDE // 4), F32),
            pltpu.SemaphoreType.DMA((2,)), way, way, way, way, dma, dma,
        ],
        compiler_params=pltpu.CompilerParams(
            collective_id=1, has_side_effects=True, vmem_limit_bytes=32 * 1024 * 1024),
        name="scatter_and_pool",
    )(own_list, places, tiles, part)


STORES = 8


def store_kernel(*refs):
    count = (len(refs) - 1) // 2
    sems = refs[-1]
    copies = []
    for n in range(count):
        near, far = refs[n], refs[count + n]
        pieces = STORES if n == 2 else 1
        rows = near.shape[1] // pieces
        for p in range(pieces):
            span = pl.ds(p * rows, rows)
            copies.append(pltpu.make_async_copy(near.at[:, span], far.at[:, span], sems.at[len(copies)]))
    for copy in copies:
        copy.start()
    for copy in copies:
        copy.wait()


def store(*arrays):
    count = len(arrays)
    return pl.pallas_call(
        store_kernel,
        out_shape=tuple(jax.ShapeDtypeStruct(a.shape, a.dtype) for a in arrays),
        in_specs=[pl.BlockSpec(memory_space=pltpu.VMEM)] * count,
        out_specs=(pl.BlockSpec(memory_space=pltpu.HBM),) * count,
        scratch_shapes=[pltpu.SemaphoreType.DMA((count + STORES - 1,))],
        compiler_params=pltpu.CompilerParams(vmem_limit_bytes=32 * 1024 * 1024),
        name="store_results",
    )(*arrays)


def shards(load_force, stiffness, cracks, anchor, images, owners, source_tile, offsets, blend_weight, counts):
    flat = [a.reshape(1, -1) for a in (owners, source_tile)]
    displacement, residual, entries, own_list, places, tiles, blank = relax(
        load_force, stiffness, cracks, anchor, *flat, offsets, blend_weight.reshape(1, -1), counts.reshape(1, -1), images)
    part = warp(entries, tiles, blank)
    level_zero, level_one, level_two = scatter(own_list, places, tiles, part)
    return store(displacement, residual, level_zero, level_one, level_two)


def solution(mesh):
    flat = P(("row", "col"))
    in_specs = (
        P(None, None, "row", "col"),
        P(None, None, "row", "col"),
        P(None, None, "row", "col"),
        P(None, "row", "col"),
        P(None, "row", "col"),
        P(("row", "col"), None),
        flat,
        P(None, ("row", "col")),
        flat,
        flat,
    )
    out_specs = (
        P(None, None, "row", "col"),
        P(None, None, "row", "col"),
        P(None, "row", "col"),
        P(None, "row", "col"),
        P(None, "row", "col"),
    )
    return jax.shard_map(shards, mesh=mesh, in_specs=in_specs, out_specs=out_specs, check_vma=False)
```

```python
import functools

import jax
import jax.numpy as jnp
from jax import lax
from jax.experimental import pallas as pl
from jax.experimental.pallas import tpu as pltpu
from jax.sharding import PartitionSpec as P

S = 2
TILE = 256
SPACING = 8
K = 6
ITERS = 4
TC = 4
ENT_DEV = 48
VR = 32
VC = 128
VT = 32
N_ROW = 8
N_COL = 16
WIDE = TC * TILE
ROWS = VR + 16
COLS = 2 * VC
MESH = pl.DeviceIdType.MESH
F32 = jnp.float32
BF16 = jnp.bfloat16


def flipped(v, mask):
    if mask == 1:
        return v + 1 - 2 * lax.rem(v, 2)
    return 3 - v


def peer_col(y, z, mask, i):
    py = flipped(y, mask) if i % 2 == 1 else y
    pz = flipped(z, mask) if i // 2 == 1 else z
    return pz * 4 + py


GATHER_MASK = (1, 3)
SCATTER_MASK = (3, 1)


NOTE = 8
LIST = 256
MOMENTS = 2 * ITERS
SCALE = 8.0


def two_sum(a, b):
    total = a + b
    part = total - a
    return total, (a - (total - part)) + (b - part)


def renormed(high, low):
    total = high + low
    return total, low - (total - high)


def split(a):
    wide = a * 4097.0
    high = wide - (wide - a)
    return high, a - high


def two_product(a, b, a_parts, b_parts):
    (ah, al), (bh, bl) = a_parts, b_parts
    product = a * b
    return product, ((ah * bh - product) + ah * bl + al * bh) + al * bl


def added(x, y):
    total, rest = two_sum(x[0], y[0])
    return renormed(total, rest + (x[1] + y[1]))


def times(x, y):
    product, rest = two_product(x[0], y[0], split(x[0]), split(y[0]))
    return renormed(product, rest + (x[0] * y[1] + x[1] * y[0]))


def minus(x):
    return -x[0], -x[1]


def over(x, y):
    first = x[0] / y[0]
    nothing = jnp.zeros_like(first)
    rest = added(x, minus(times((first, nothing), y)))
    return renormed(first, rest[0] / y[0])


def residual_polynomial(moment):
    one = (jnp.ones_like(moment[0][0]), jnp.zeros_like(moment[0][0]))
    rho, pi = [one], [one]
    upper = moment[0]
    for k in range(ITERS):
        lower = None
        for j, weight in enumerate(pi):
            term = moment[j + k + 1] if k == 0 else times(weight, moment[j + k + 1])
            lower = term if lower is None else added(lower, term)
        step = over(upper, lower)
        moved = [minus(times(step, weight)) if k else minus(step) for weight in pi]
        rho = [rho[0]] + [added(rho[j], moved[j - 1]) for j in range(1, k + 1)] + [moved[k]]
        if k == ITERS - 1:
            return rho
        upper = moment[k + 1]
        for j in range(1, k + 2):
            upper = added(upper, times(rho[j], moment[j + k + 1]))
        grow = minus(over(upper, lower))
        pi = [added(rho[j], times(grow, pi[j]) if k else grow) for j in range(k + 1)] + [rho[k + 1]]


def relax_kernel(
    load_hbm, stiff_hbm, crack_hbm, anchor_hbm, owner_hbm, source_hbm, offset_hbm, blend_hbm, count_hbm, images_hbm,
    disp_ref, resid_ref, list_ref, own_ref, place_ref, tiles_ref, blank_ref,
    fields, stiff, crack, owner, source, offset, blend, count,
    strips, halo_v, halo_h, halo_c, coef, krylov,
    part_a, part_b, got_a, got_b, note, notes, sums,
    load_sem, own_sem, halo_send, halo_recv, send_a, recv_a, send_b, recv_b,
    note_send, note_recv, tile_send, tile_recv,
):
    r = lax.axis_index("row")
    c = lax.axis_index("col")
    y = lax.rem(c, 4)
    z = c // 4
    up, down = lax.rem(r + N_ROW - 1, N_ROW), lax.rem(r + 1, N_ROW)
    left, right = lax.rem(c + N_COL - 1, N_COL), lax.rem(c + 1, N_COL)
    corners = ((up, left), (up, right), (down, left), (down, right))

    barrier = pltpu.get_barrier_semaphore()

    loads = []
    for n, (near, far) in enumerate((
        (stiff_hbm, stiff), (crack_hbm, crack),
        (load_hbm.at[0], fields.at[pl.ds(0, 2)]), (load_hbm.at[1], fields.at[pl.ds(2, 2)]),
        (anchor_hbm, fields.at[pl.ds(8, 2)]),
        (owner_hbm, owner), (source_hbm, source), (offset_hbm, offset), (blend_hbm, blend), (count_hbm, count),
    )):
        loads.append(pltpu.make_async_copy(near, far, load_sem.at[n]))
    for copy in loads:
        copy.start()
    for corner in corners:
        pl.semaphore_signal(barrier, inc=1, device_id=corner, device_id_type=MESH)
    for d in range(1, N_COL):
        pl.semaphore_signal(barrier, inc=1, device_id=(r, lax.rem(c + d, N_COL)), device_id_type=MESH)
    for d in range(1, N_ROW):
        pl.semaphore_signal(barrier, inc=1, device_id=(lax.rem(r + d, N_ROW), c), device_id_type=MESH)

    for copy in loads:
        copy.wait()
    for s in range(S):
        for k in range(2):
            fields[4 + 2 * s + k] = stiff[s, k] * crack[s, k].astype(F32)
    lane = lax.broadcasted_iota(jnp.int32, (VR, VC), 1)
    first = jnp.zeros((VR, VC), F32)
    last = jnp.zeros((VR, VC), F32)
    for f in range(10):
        block = fields[f]
        here = (lane >= 4 * f) & (lane < 4 * f + 4)
        first = jnp.where(here, block if f == 0 else pltpu.roll(block, 4 * f, 1), first)
        last = jnp.where(here, pltpu.roll(block, 4 * f + 4, 1), last)
    strips[0] = first
    strips[1] = last

    pl.semaphore_wait(barrier, N_ROW - 1 + N_COL - 1 + 4)

    halo = []
    for n, (near, far, device) in enumerate((
        (fields.at[:, pl.ds(VR - 8, 8), :], halo_v.at[0], (down, c)),
        (fields.at[:, pl.ds(0, 8), :], halo_v.at[1], (up, c)),
        (strips.at[1], halo_h.at[0], (r, right)),
        (strips.at[0], halo_h.at[1], (r, left)),
        (strips.at[1, pl.ds(VR - 8, 8)], halo_c.at[0], (down, right)),
        (strips.at[0, pl.ds(VR - 8, 8)], halo_c.at[1], (down, left)),
        (strips.at[1, pl.ds(0, 8)], halo_c.at[2], (up, right)),
        (strips.at[0, pl.ds(0, 8)], halo_c.at[3], (up, left)),
    )):
        halo.append(pltpu.make_async_remote_copy(
            src_ref=near, dst_ref=far, send_sem=halo_send.at[n], recv_sem=halo_recv.at[n],
            device_id=device, device_id_type=MESH))
    for copy in halo:
        copy.start()

    half = TILE // 2

    def tile_copy(s, n, slot_from, slot_to, part, peer):
        rows = pl.ds(part * half, half)
        near = images_hbm.at[s, rows] if slot_from == 0 else tiles_ref.at[s, slot_from, rows]
        return pltpu.make_async_remote_copy(
            src_ref=near, dst_ref=tiles_ref.at[s, slot_to, rows],
            send_sem=tile_send.at[s, n], recv_sem=tile_recv.at[s, n],
            device_id=(r, peer_col(y, z, GATHER_MASK[s], peer)), device_id_type=MESH)

    direct = [
        [tile_copy(s, 0, 0, 2, 0, 2), tile_copy(s, 1, 0, 1, 1, 1), tile_copy(s, 2, 0, 1, 0, 1), tile_copy(s, 3, 0, 2, 1, 2)]
        for s in range(S)
    ]
    relayed = [[tile_copy(s, 4, 2, 3, 0, 1), tile_copy(s, 5, 1, 3, 1, 2)] for s in range(S)]
    for n in range(4):
        for s in range(S):
            direct[s][n].start()
    own = pltpu.make_async_copy(images_hbm, tiles_ref.at[:, 0], own_sem)
    own.start()

    entry_lane = lax.broadcasted_iota(jnp.int32, (1, ENT_DEV), 1)
    listed = jnp.zeros((1, ENT_DEV), jnp.int32)
    for t in range(ENT_DEV // K):
        listed = jnp.where(entry_lane // K == t, count[:, t:t + 1], listed)
    note[...] = jnp.zeros((NOTE, VC), F32)
    note[0:1, 0:ENT_DEV] = (owner[...] * TC + source[...]).astype(F32)
    note[1:3, 0:ENT_DEV] = offset[...].astype(F32)
    note[3:4, 0:ENT_DEV] = jnp.where(lax.rem(entry_lane, K) < listed, blend[...], 0.0)

    blank_ref[...] = jnp.zeros(blank_ref.shape, BF16)

    for copy in halo:
        copy.wait_recv()

    wide_row = lax.broadcasted_iota(jnp.int32, (ROWS, VC), 0) + r * VR - 8
    wide_lane = lax.broadcasted_iota(jnp.int32, (ROWS, VC), 1)
    side_col = jnp.where(wide_lane < VC // 2, wide_lane + VC, wide_lane - VC) + c * VC
    row_in = (wide_row >= 0) & (wide_row < VR * N_ROW)
    side_in = row_in & (side_col >= 0) & (side_col < VC * N_COL)
    from_left = jnp.concatenate([halo_c[0], halo_h[0], halo_c[2]], axis=0)
    from_right = jnp.concatenate([halo_c[1], halo_h[1], halo_c[3]], axis=0)

    def widened(f):
        center = jnp.concatenate([halo_v[0, f], fields[f], halo_v[1, f]], axis=0)
        to_left = pltpu.roll(from_left, 124 - 4 * f, 1)
        to_right = from_right if f == 0 else pltpu.roll(from_right, VC - 4 * f, 1)
        side = jnp.where(wide_lane < 4, to_right, jnp.where(wide_lane >= 124, to_left, 0.0))
        return jnp.concatenate(
            [jnp.where(row_in, center, 0.0), jnp.where(side_in, side, 0.0)], axis=1)

    inside = jnp.concatenate([row_in.astype(F32), side_in.astype(F32)], axis=1)
    for s in range(S):
        to_right = widened(4 + 2 * s)
        to_low = widened(5 + 2 * s)
        to_left = pltpu.roll(to_right, 1, 1) * inside
        to_high = pltpu.roll(to_low, 1, 0) * inside
        coef[s, 0] = widened(8 + s) + to_right + to_left + to_low + to_high
        coef[s, 1] = to_right
        coef[s, 2] = to_left
        coef[s, 3] = to_low
        coef[s, 4] = to_high
        for k in range(2):
            krylov[0, 2 * s + k] = widened(2 * s + k)

    for n in range(ITERS):
        for f in range(4):
            s = f // 2
            v = krylov[n, f]
            w = coef[s, 0] * v
            w = w - coef[s, 1] * pltpu.roll(v, COLS - 1, 1)
            w = w - coef[s, 2] * pltpu.roll(v, 1, 1)
            w = w - coef[s, 3] * pltpu.roll(v, ROWS - 1, 0)
            w = w - coef[s, 4] * pltpu.roll(v, 1, 0)
            krylov[n + 1, f] = w * (1.0 / SCALE)

    middle = 8 + VR // 2
    point = lax.rem(lax.broadcasted_iota(jnp.int32, (1, VC), 1), VT) - VT // 2
    for f in range(4):
        row = jnp.zeros((1, VC), F32)
        for n in range(ITERS):
            line = krylov[n, f, pl.ds(middle, 1), pl.ds(0, VC)]
            row = jnp.where(point == n, line if n == 0 else pltpu.roll(line, n, 1), row)
        note[4 + f:5 + f, :] = row
    told = []
    for s in range(S):
        for i in (1, 2, 3):
            told.append(pltpu.make_async_remote_copy(
                src_ref=note, dst_ref=notes.at[s, i - 1],
                send_sem=note_send.at[s, i - 1], recv_sem=note_recv.at[s, i - 1],
                device_id=(r, peer_col(y, z, SCATTER_MASK[s], i)), device_id_type=MESH))

    moments = [[None] * S for _ in range(MOMENTS)]
    for s in range(S):
        totals = [None] * MOMENTS
        for f in (2 * s, 2 * s + 1):
            for g in range(VR // 8):
                vectors = [krylov[n, f, pl.ds(8 + 8 * g, 8), pl.ds(0, VC)] for n in range(ITERS + 1)]
                parts = [split(v) for v in vectors]
                for m in range(MOMENTS):
                    a, b = m // 2, m - m // 2
                    product, rest = two_product(vectors[a], vectors[b], parts[a], parts[b])
                    if totals[m] is None:
                        totals[m] = (product, rest)
                    else:
                        total, slip = two_sum(totals[m][0], product)
                        totals[m] = (total, totals[m][1] + (rest + slip))
        for m in range(MOMENTS):
            moments[m][s] = totals[m]

    level = [moments[m][s] for m in range(MOMENTS) for s in range(S)]
    sublane = lax.broadcasted_iota(jnp.int32, (8, VC), 0)
    packed = []
    for base in range(0, len(level), 8):
        group = level[base:base + 8]
        shift = 4
        while shift:
            low = lax.rem(sublane // shift, 2) == 0
            merged = []
            for n in range(shift):
                a, b = group[n], group[n + shift]
                first = tuple(jnp.where(low, u, pltpu.roll(v, shift, 0)) for u, v in zip(a, b))
                second = tuple(jnp.where(low, pltpu.roll(u, 8 - shift, 0), v) for u, v in zip(a, b))
                merged.append(added(first, second))
            group = merged
            shift //= 2
        packed.append(group[0])
    for step in (VC // 2, VC // 4):
        packed = [added(pair, tuple(pltpu.roll(part, step, 1) for part in pair)) for pair in packed]
    sum_lane = lax.broadcasted_iota(jnp.int32, (8, VC), 1)
    quarter = VC // 4

    def joined(one, two):
        return jnp.where(sum_lane < VC // 2, one, two)

    part_a[...] = joined(
        *[jnp.where(lax.rem(sum_lane, VC // 2) < quarter, one, two) for one, two in zip(*packed)])

    for d in range(1, N_ROW):
        pltpu.make_async_remote_copy(
            src_ref=part_a, dst_ref=got_a.at[d - 1], send_sem=send_a,
            recv_sem=recv_a, device_id=(lax.rem(r + d, N_ROW), c), device_id_type=MESH).start()

    def sum_copy(phase):
        got, send, recv = ((got_a, send_a, recv_a), (got_b, send_b, recv_b))[phase]
        return pltpu.make_async_remote_copy(
            src_ref=got, dst_ref=got, send_sem=send, recv_sem=recv,
            device_id=((down, c), (r, right))[phase], device_id_type=MESH)

    def gathered(own_part, got):
        terms = [own_part[...]] + [got[n] for n in range(got.shape[0])]
        terms = [(term, pltpu.roll(term, VC // 2, 1)) for term in terms]
        while len(terms) > 1:
            terms = [added(terms[n], terms[n + 1]) if n + 1 < len(terms) else terms[n]
                     for n in range(0, len(terms), 2)]
        return terms[0]

    sum_copy(0).wait_recv()
    high, low = gathered(part_a, got_a)
    part_b[...] = joined(high, pltpu.roll(low, VC // 2, 1))

    for d in range(1, N_COL):
        pltpu.make_async_remote_copy(
            src_ref=part_b, dst_ref=got_b.at[d - 1], send_sem=send_b,
            recv_sem=recv_b, device_id=(r, lax.rem(c + d, N_COL)), device_id_type=MESH).start()

    for copy in told:
        copy.start()

    for s in range(S):
        direct[s][0].wait_recv()
        relayed[s][0].start()
        direct[s][1].wait_recv()
        relayed[s][1].start()

    sum_copy(1).wait_recv()
    total = gathered(part_b, got_b)
    shift = quarter // 2
    while shift:
        inner = lax.rem(sum_lane, quarter) < quarter - shift
        total = added(total, tuple(
            jnp.where(inner, pltpu.roll(part, VC - shift, 1), pltpu.roll(part, quarter - shift, 1)) for part in total))
        shift //= 2
    odd = lax.rem(sum_lane // quarter, 2) == 1
    spread = []
    for part in total:
        one = jnp.where(odd, pltpu.roll(part, quarter, 1), part)
        two = jnp.where(odd, part, pltpu.roll(part, VC - quarter, 1))
        spread.append(jnp.concatenate([joined(u, pltpu.roll(u, VC // 2, 1)) for u in (one, two)], axis=0))
    total = spread
    sums[0:16] = total[0]
    sums[16:32] = total[1]
    rho = residual_polynomial([
        (sums[2 * m:2 * m + 2, :], sums[16 + 2 * m:18 + 2 * m, :]) for m in range(MOMENTS)])
    rho = [weight[0] for weight in rho]

    for f in range(4):
        s, k = f // 2, f % 2
        vectors = [krylov[n, f, pl.ds(8, VR), pl.ds(0, VC)] for n in range(ITERS + 1)]
        moved = rho[1][s:s + 1] * vectors[0]
        rest = vectors[0]
        for n in range(1, ITERS + 1):
            rest = rest + rho[n][s:s + 1] * vectors[n]
            if n < ITERS:
                moved = moved + rho[n + 1][s:s + 1] * vectors[n]
        disp_ref[s, k] = moved * (-1.0 / SCALE)
        resid_ref[s, k] = rest

    for copy in told:
        copy.wait_recv()
    texts = [(s, note if i == 0 else notes.at[s, i - 1]) for s in range(S) for i in range(4)]
    note_lane = lax.broadcasted_iota(jnp.int32, (8, VC), 1)
    note_row = lax.broadcasted_iota(jnp.int32, (8, VC), 0)

    def stacked(n):
        rows = jnp.concatenate([text[n:n + 1, :] for _, text in texts], axis=0)
        return jnp.where(note_row < 4, rows, pltpu.roll(rows, VC - TC * K, 1))

    note_point = lax.rem(note_lane, VT) - VT // 2
    scales = jnp.zeros((8, VC), F32)
    for n in range(ITERS):
        scale = jnp.where(note_row < 4, rho[n + 1][0:1], rho[n + 1][1:2])
        scales = jnp.where(note_point == n, scale, scales)

    def shifted(k):
        rows = scales * jnp.concatenate([text[4 + 2 * s + k:5 + 2 * s + k, :] for s, text in texts], axis=0)
        rows = rows + pltpu.roll(rows, VC - 1, 1)
        rows = (rows + pltpu.roll(rows, VC - 2, 1)) * (-SPACING / SCALE)
        shift = stacked(1 + k)
        for j in range(TC):
            at = VT * j + VT // 2
            shift = shift + jnp.where(note_lane // K == j, rows[:, at:at + 1], 0.0)
        return shift

    named = stacked(0).astype(jnp.int32)
    owner_col = named // TC
    weight = stacked(3)
    at_y, at_z = lax.rem(owner_col, 4), owner_col // 4
    near = [((at_y == y) | (at_y == flipped(y, m))) & ((at_z == z) | (at_z == flipped(z, m))) for m in GATHER_MASK]
    mine = jnp.where(note_row < 4, near[0].astype(F32), near[1].astype(F32))
    mine = jnp.where((weight > 0.0) & (note_lane < TC * K), mine, 0.0)
    slot = jnp.where(at_y == y, 0, 1) + jnp.where(at_z == z, 0, 2)
    key = slot * TC + lax.rem(named, TC)
    code = ((note_row * TC + note_lane // K) * 16 + key).astype(F32)
    sent = jnp.where(lax.rem(note_row, 4) < 2, 0.0, mine)
    rank = sent
    for step in (1, 2, 4, 8, 16):
        rank = rank + jnp.where(note_lane >= step, pltpu.roll(rank, step, 1), 0.0)
    above = jnp.sum(sent, axis=1, keepdims=True) + jnp.zeros((8, VC), F32)
    base = above
    for step in (1, 2, 4):
        base = base + jnp.where(note_row >= step, pltpu.roll(base, step, 0), 0.0)
    total = base[7:8, :]
    rank = jnp.where(sent > 0.0, rank + (base - above) - 1.0, -1.0)
    shift_y, shift_x = shifted(0), shifted(1)
    columns = [jnp.transpose(part)[0:TC * K] for part in (rank, code, shift_y, shift_x, weight)]
    own_ref[...] = jnp.concatenate(
        [part[4 * s + i:4 * s + i + 1] for s in range(S) for i in range(2)
         for part in (weight, shift_y, shift_x, mine * weight)], axis=0)
    place_ref[...] = jnp.concatenate(
        [part[4 * s + i:4 * s + i + 1] for s in range(S) for i in range(2)
         for part in (slot, lax.rem(named, TC), slot, slot)], axis=0)
    place = lax.broadcasted_iota(jnp.int32, (TC * K, LIST), 1).astype(F32)
    listed = [jnp.zeros((1, LIST), F32)] * 4
    for n in range(8):
        chosen = columns[0][:, n:n + 1] == place
        listed = [old + jnp.sum(jnp.where(chosen, column[:, n:n + 1], 0.0), axis=0, keepdims=True)
                  for old, column in zip(listed, columns[1:])]
    list_ref[...] = jnp.concatenate(
        listed + [jnp.concatenate([total] * (LIST // VC), axis=1), jnp.zeros((3, LIST), F32)], axis=0)

    for copy in told:
        copy.wait_send()
    for copy in halo:
        copy.wait_send()
    for phase in range(2):
        sum_copy(phase).wait_send()
    own.wait()
    for s in range(S):
        direct[s][2].wait_recv()
        direct[s][3].wait_recv()
        for copy in relayed[s]:
            copy.wait()
        for copy in direct[s]:
            copy.wait_send()


def relax(*operands):
    vmem = pl.BlockSpec(memory_space=pltpu.VMEM)
    hbm = pl.BlockSpec(memory_space=pltpu.HBM)
    dma = pltpu.SemaphoreType.DMA
    block = (S, 2, VR, VC)
    operands = [pltpu.with_memory_space_constraint(a, pltpu.HBM) for a in operands]
    return pl.pallas_call(
        relax_kernel,
        out_shape=(
            jax.ShapeDtypeStruct(block, F32),
            jax.ShapeDtypeStruct(block, F32),
            jax.ShapeDtypeStruct((8, LIST), F32),
            jax.ShapeDtypeStruct((16, VC), F32),
            jax.ShapeDtypeStruct((16, VC), jnp.int32),
            jax.ShapeDtypeStruct((S, 4, TILE, WIDE), BF16),
            jax.ShapeDtypeStruct((S, 2, TILE, WIDE), BF16),
        ),
        in_specs=[hbm] * 10,
        out_specs=(vmem,) * 7,
        scratch_shapes=[
            pltpu.VMEM((10, VR, VC), F32),
            pltpu.VMEM(block, F32),
            pltpu.VMEM(block, jnp.int32),
            pltpu.VMEM((1, ENT_DEV), jnp.int32),
            pltpu.VMEM((1, ENT_DEV), jnp.int32),
            pltpu.VMEM((2, ENT_DEV), jnp.int32),
            pltpu.VMEM((1, ENT_DEV), F32),
            pltpu.VMEM((1, ENT_DEV // K), jnp.int32),
            pltpu.VMEM((2, VR, VC), F32),
            pltpu.VMEM((2, 10, 8, VC), F32),
            pltpu.VMEM((2, VR, VC), F32),
            pltpu.VMEM((4, 8, VC), F32),
            pltpu.VMEM((S, 5, ROWS, COLS), F32),
            pltpu.VMEM((ITERS + 1, 4, ROWS, COLS), F32),
            pltpu.VMEM((8, VC), F32),
            pltpu.VMEM((8, VC), F32),
            pltpu.VMEM((N_ROW - 1, 8, VC), F32),
            pltpu.VMEM((N_COL - 1, 8, VC), F32),
            pltpu.VMEM((NOTE, VC), F32),
            pltpu.VMEM((S, 3, NOTE, VC), F32),
            pltpu.VMEM((32, VC), F32),
            dma((10,)), dma, dma((8,)), dma((8,)),
            dma, dma, dma, dma,
            dma((S, 3)), dma((S, 3)), dma((S, 6)), dma((S, 6)),
        ],
        compiler_params=pltpu.CompilerParams(
            collective_id=0, has_side_effects=True, vmem_limit_bytes=32 * 1024 * 1024),
        name="relax_and_gather",
    )(*operands)


BATCH = 8


def sampled(apart, shift, side):
    shift = jnp.full((1, TILE), shift, F32)
    low = jnp.floor(shift)
    at_low = jnp.maximum(0.0, 1.0 - jnp.abs(low - shift)).astype(BF16)
    at_high = jnp.maximum(0.0, 1.0 - jnp.abs(low + 1.0 - shift)).astype(BF16)
    low_place = (side * low).astype(BF16)
    high_place = (side * (low + 1.0)).astype(BF16)
    matrix = apart[...]
    return jnp.where(matrix == low_place, at_low, jnp.where(matrix == high_place, at_high, jnp.zeros((), BF16)))


def warped_by(source, apart, shift_y, shift_x):
    across = jnp.dot(source, sampled(apart, shift_x, -1.0), preferred_element_type=F32)
    return jnp.dot(sampled(apart, shift_y, 1.0), across.astype(BF16), preferred_element_type=F32)


def columns_apart():
    row = lax.broadcasted_iota(jnp.int32, (TILE, TILE), 0)
    lane = lax.broadcasted_iota(jnp.int32, (TILE, TILE), 1)
    return (lane - row).astype(F32).astype(BF16)


def warp_kernel(list_ref, tiles_ref, blank_ref, part_ref, apart):
    count = list_ref[4, 0].astype(jnp.int32)
    apart[...] = columns_apart()

    def entry(n):
        code = list_ref[0, n].astype(jnp.int32)
        key = code & 15
        j = (code >> 4) & 3
        place = code >> 6
        s = place >> 2
        source = tiles_ref[s, key >> 2, :, pl.ds(pl.multiple_of((key & 3) * TILE, TILE), TILE)]
        value = list_ref[3, n] * warped_by(source, apart, list_ref[1, n], list_ref[2, n])
        return value, (s, jnp.maximum(place & 3, 2) - 2, slice(None), pl.ds(pl.multiple_of(j * TILE, TILE), TILE))

    def batch(b, carry):
        found = [entry(b * BATCH + n) for n in range(BATCH)]
        for value, place in found:
            part_ref[place] = (part_ref[place].astype(F32) + value).astype(BF16)
        return carry

    lax.fori_loop(0, (count + BATCH - 1) // BATCH, batch, 0)


def warp(entries, tiles, blank):
    vmem = pl.BlockSpec(memory_space=pltpu.VMEM)
    smem = pl.BlockSpec(memory_space=pltpu.SMEM)
    return pl.pallas_call(
        warp_kernel,
        out_shape=jax.ShapeDtypeStruct((S, 2, TILE, WIDE), BF16),
        in_specs=[smem, vmem, vmem],
        out_specs=vmem,
        scratch_shapes=[pltpu.VMEM((TILE, TILE), BF16)],
        input_output_aliases={2: 0},
        compiler_params=pltpu.CompilerParams(vmem_limit_bytes=32 * 1024 * 1024),
        name="warp_partials",
    )(entries, tiles, blank)


HALVES = 2
SUBS = ((0, 64), (64, 64))
DEEP = 64


def scatter_kernel(
    listed_ref, placed_ref, tiles_ref, part_ref, zero_ref, one_ref, two_ref,
    own_ref, place_ref, nearer, total, apart, relay, onward, got, pool, half, quarter, twos, list_sem,
    relay_send, relay_recv, direct_send, direct_recv, onward_send, onward_recv,
):
    r = lax.axis_index("row")
    c = lax.axis_index("col")
    y = lax.rem(c, 4)
    z = c // 4
    barrier = pltpu.get_barrier_semaphore()
    for s in range(S):
        for i in (1, 2):
            pl.semaphore_signal(
                barrier, inc=1, device_id=(r, peer_col(y, z, SCATTER_MASK[s], i)), device_id_type=MESH)
    listing = [pltpu.make_async_copy(listed_ref, own_ref, list_sem.at[0]),
               pltpu.make_async_copy(placed_ref, place_ref, list_sem.at[1])]
    for copy in listing:
        copy.start()
    row = lax.broadcasted_iota(jnp.int32, (TILE, VC), 0)
    lane = lax.broadcasted_iota(jnp.int32, (TILE, VC), 1)
    pool[...] = jnp.where(row // 2 == lane, 0.25, 0.0).astype(BF16)
    apart[...] = columns_apart()
    pl.semaphore_wait(barrier, 2 * S)

    def rows_of(h, u):
        return pl.ds(h * (TILE // HALVES) + SUBS[u][0], SUBS[u][1])

    def sub_of(u):
        return pl.ds(*SUBS[u])

    def copy_to(s, peer, near, far, send, recv):
        return pltpu.make_async_remote_copy(
            src_ref=near, dst_ref=far, send_sem=send, recv_sem=recv,
            device_id=(r, peer_col(y, z, SCATTER_MASK[s], peer)), device_id_type=MESH)

    def half_of(h):
        return pl.ds(h * (TILE // HALVES), TILE // HALVES)

    def to_relay(s, h):
        return copy_to(s, h + 1, part_ref.at[s, 1, half_of(h)], relay.at[s, h],
                       relay_send.at[s, h], relay_recv.at[s, h])

    def to_end(s, h):
        near = nearer.at[s] if h == 0 else part_ref.at[s, 0]
        return copy_to(s, h + 1, near.at[half_of(h)], got.at[s, h, half_of(h)],
                       direct_send.at[s, h], direct_recv.at[s, h])

    def to_end_summed(s, h, u):
        other = 1 - h
        return copy_to(s, other + 1, onward.at[s, h, sub_of(u)], got.at[s, other, rows_of(h, u)],
                       onward_send.at[s, h, u], onward_recv.at[s, h, u])

    steps = [(u, h, s) for u in range(len(SUBS)) for h in range(HALVES) for s in range(S)]
    ways = [(h, s) for h in range(HALVES) for s in range(S)]
    for h, s in ways:
        to_relay(s, h).start()
    for s in range(S):
        to_end(s, 1).start()

    def share(s, i, put):
        @pl.loop(0, TC)
        def _(j):
            value = None
            base = 4 * (2 * s + i)
            for k in range(K):
                e = j * K + k
                tile = place_ref[base + 1, e]
                wide = tiles_ref[s, place_ref[base, e]]
                source = wide[:, 0:TILE]
                for t in range(1, TC):
                    source = jnp.where(tile == t, wide[:, t * TILE:(t + 1) * TILE], source)
                term = own_ref[base + 3, e] * warped_by(source, apart, own_ref[base + 1, e], own_ref[base + 2, e])
                value = term if value is None else value + term
            put(value, pl.ds(pl.multiple_of(j * TILE, TILE), TILE))

    def put_near(s, value, cols):
        nearer[s, :, cols] = value.astype(BF16)

    def put_own(s, value, cols):
        total[s, :, cols] = value

    for copy in listing:
        copy.wait()
    for s in range(S):
        share(s, 1, functools.partial(put_near, s))
        to_end(s, 0).start()
    for h, s in ways:
        to_relay(s, h).wait_recv()
    for u, h, s in steps:
        ours = part_ref[s, 0, rows_of(h, u)] if h == 0 else nearer[s, rows_of(h, u)]
        summed = relay[s, h, sub_of(u)].astype(F32) + ours.astype(F32)
        onward[s, h, sub_of(u)] = summed.astype(BF16)
        to_end_summed(s, h, u).start()
    for s in range(S):
        share(s, 0, functools.partial(put_own, s))

    def pooled(block):
        return jnp.dot(block.astype(BF16), pool[...], preferred_element_type=F32)

    for h, s in ways:
        to_end(s, h).wait_recv()
        rows = half_of(h)
        total[s, rows] = total[s, rows] + got[s, h, rows].astype(F32)

    for u, h, s in steps:
        to_end_summed(s, h, u).wait_recv()
        rows = rows_of(h, u)
        start, deep = rows.start, rows.size
        for j in range(TC):
            cols = pl.ds(j * TILE, TILE)
            block = total[s, rows, cols] + got[s, 1 - h, rows, cols].astype(F32)
            zero_ref[s, rows, cols] = block.astype(BF16)
            half[j, pl.ds(0, deep)] = pooled(block)
        ones = []
        for j in range(TC):
            piece = half[j, pl.ds(0, deep // 2, stride=2), :] + half[j, pl.ds(1, deep // 2, stride=2), :]
            one_ref[s, pl.ds(start // 2, deep // 2), pl.ds(j * VC, VC)] = piece.astype(BF16)
            ones.append(piece)
        for j in range(2):
            quarter[j, pl.ds(0, deep // 2)] = pooled(jnp.concatenate(ones[2 * j:2 * j + 2], axis=1))
            piece = quarter[j, pl.ds(0, deep // 4, stride=2), :] + quarter[j, pl.ds(1, deep // 4, stride=2), :]
            twos[s, pl.ds(start // 4, deep // 4), pl.ds(j * VC, VC)] = piece
    two_ref[...] = twos[...].astype(BF16)

    for h, s in ways:
        to_relay(s, h).wait_send()
        to_end(s, h).wait_send()
    for u, h, s in steps:
        to_end_summed(s, h, u).wait_send()


def scatter(own_list, places, tiles, part):
    vmem = pl.BlockSpec(memory_space=pltpu.VMEM)
    dma = pltpu.SemaphoreType.DMA((S, HALVES, len(SUBS)))
    way = pltpu.SemaphoreType.DMA((S, HALVES))
    halved = pltpu.VMEM((S, HALVES, TILE // HALVES, WIDE), BF16)
    return pl.pallas_call(
        scatter_kernel,
        out_shape=(
            jax.ShapeDtypeStruct((S, TILE, WIDE), BF16),
            jax.ShapeDtypeStruct((S, TILE // 2, WIDE // 2), BF16),
            jax.ShapeDtypeStruct((S, TILE // 4, WIDE // 4), BF16),
        ),
        in_specs=[vmem, vmem, vmem, vmem],
        out_specs=(vmem, vmem, vmem),
        scratch_shapes=[
            pltpu.SMEM((16, VC), F32),
            pltpu.SMEM((16, VC), jnp.int32),
            pltpu.VMEM((S, TILE, WIDE), BF16),
            pltpu.VMEM((S, TILE, WIDE), F32),
            pltpu.VMEM((TILE, TILE), BF16),
            halved,
            halved,
            pltpu.VMEM((S, 2, TILE, WIDE), BF16),
            pltpu.VMEM((TILE, VC), BF16),
            pltpu.VMEM((TC, DEEP, VC), F32),
            pltpu.VMEM((2, DEEP // 2, VC), F32),
            pltpu.VMEM((S, TILE // 4, WIDE // 4), F32),
            pltpu.SemaphoreType.DMA((2,)), way, way, way, way, dma, dma,
        ],
        compiler_params=pltpu.CompilerParams(
            collective_id=1, has_side_effects=True, vmem_limit_bytes=32 * 1024 * 1024),
        name="scatter_and_pool",
    )(own_list, places, tiles, part)


STORES = 8


def store_kernel(*refs):
    count = (len(refs) - 1) // 2
    sems = refs[-1]
    copies = []
    for n in range(count):
        near, far = refs[n], refs[count + n]
        pieces = STORES if n == 2 else 1
        rows = near.shape[1] // pieces
        for p in range(pieces):
            span = pl.ds(p * rows, rows)
            copies.append(pltpu.make_async_copy(near.at[:, span], far.at[:, span], sems.at[len(copies)]))
    for copy in copies:
        copy.start()
    for copy in copies:
        copy.wait()


def store(*arrays):
    count = len(arrays)
    return pl.pallas_call(
        store_kernel,
        out_shape=tuple(jax.ShapeDtypeStruct(a.shape, a.dtype) for a in arrays),
        in_specs=[pl.BlockSpec(memory_space=pltpu.VMEM)] * count,
        out_specs=(pl.BlockSpec(memory_space=pltpu.HBM),) * count,
        scratch_shapes=[pltpu.SemaphoreType.DMA((count + STORES - 1,))],
        compiler_params=pltpu.CompilerParams(vmem_limit_bytes=32 * 1024 * 1024),
        name="store_results",
    )(*arrays)


def shards(load_force, stiffness, cracks, anchor, images, owners, source_tile, offsets, blend_weight, counts):
    flat = [a.reshape(1, -1) for a in (owners, source_tile)]
    displacement, residual, entries, own_list, places, tiles, blank = relax(
        load_force, stiffness, cracks, anchor, *flat, offsets, blend_weight.reshape(1, -1), counts.reshape(1, -1), images)
    part = warp(entries, tiles, blank)
    level_zero, level_one, level_two = scatter(own_list, places, tiles, part)
    return store(displacement, residual, level_zero, level_one, level_two)


def solution(mesh):
    flat = P(("row", "col"))
    in_specs = (
        P(None, None, "row", "col"),
        P(None, None, "row", "col"),
        P(None, None, "row", "col"),
        P(None, "row", "col"),
        P(None, "row", "col"),
        P(("row", "col"), None),
        flat,
        P(None, ("row", "col")),
        flat,
        flat,
    )
    out_specs = (
        P(None, None, "row", "col"),
        P(None, None, "row", "col"),
        P(None, "row", "col"),
        P(None, "row", "col"),
        P(None, "row", "col"),
    )
    return jax.shard_map(shards, mesh=mesh, in_specs=in_specs, out_specs=out_specs, check_vma=False)
```
